128 devices in a mesh: dp: 8 (over z, core), ctx: 16 (over y, x).
Axes of the slice: x: 4, y: 4, z: 4, core: 2. Of those that a mesh axis runs over, the one named last changes fastest.
Arguments:
- hidden_in: bfloat16 [2, 8, 1024, 896], P(None, 'dp', 'ctx'), may hold values from -6 to 6
- positions: int32 [2, 8, 1024], P(None, 'dp', 'ctx'), may hold values from 0 to 1023, as said below
- norm_attn: bfloat16 [896], P(('dp', 'ctx')), may hold values from 0.099609375 to 1.8984375
- w_query: bfloat16 [896, 896], P(('dp', 'ctx')), may hold values from -0.1875 to 0.1875
- b_query: bfloat16 [896], P(('dp', 'ctx')), may hold values from -3 to 3
- w_key: bfloat16 [896, 128], P(('dp', 'ctx')), may hold values from -0.1875 to 0.1875
- b_key: bfloat16 [128], P(('dp', 'ctx')), may hold values from -3 to 3
- value_weight: bfloat16 [896, 128], P(('dp', 'ctx')), may hold values from -0.1875 to 0.1875
- value_bias: bfloat16 [128], P(('dp', 'ctx')), may hold values from -3 to 3
- w_output: bfloat16 [896, 896], P(('dp', 'ctx')), may hold values from -0.375 to 0.375
- norm_mlp: bfloat16 [896], P(('dp', 'ctx')), may hold values from 0.099609375 to 1.8984375
- w_gate: bfloat16 [896, 4864], P(('dp', 'ctx')), may hold values from -0.1875 to 0.1875
- w_up: bfloat16 [896, 4864], P(('dp', 'ctx')), may hold values from -0.1875 to 0.1875
- w_down: bfloat16 [4864, 896], P(('dp', 'ctx')), may hold values from -0.078125 to 0.078125
- cotangent: bfloat16 [2, 8, 1024, 896], P(None, 'dp', 'ctx'), may hold values from -6 to 6
Outputs:
- layer_out: bfloat16 [2, 8, 1024, 896], P(None, 'dp', 'ctx')
- grad_in: float32 [2, 8, 1024, 896], P(None, 'dp', 'ctx')
- grad_norm_attn: float32 [896], P(('dp', 'ctx'))
- grad_w_query: float32 [896, 896], P(('dp', 'ctx'))
- grad_b_query: float32 [896], P(('dp', 'ctx'))
- grad_w_key: float32 [896, 128], P(('dp', 'ctx'))
- grad_b_key: float32 [128], replicated
- grad_w_value: float32 [896, 128], P(('dp', 'ctx'))
- grad_b_value: float32 [128], P(('dp', 'ctx'))
- grad_w_output: float32 [896, 896], P(('dp', 'ctx'))
- grad_norm_mlp: float32 [896], P(('dp', 'ctx'))
- grad_w_gate: float32 [896, 4864], P(('dp', 'ctx'))
- grad_w_up: float32 [896, 4864], P(('dp', 'ctx'))
- grad_w_down: float32 [4864, 896], P(('dp', 'ctx'))
The draws below stay inside these ranges and needn't reach their ends.
Inputs may be any that keep to these rules, and one draw needn't show every extreme that they name: Each sequence's stored rows hold every position 0 to 1023 once. The 64 rows of a sequence on one index of ctx are two runs of 32 consecutive positions: first one starting at p * 32, then one starting at (31 - p) * 32, with p differing between the indices of ctx.
All inputs are finite; a program needn't handle non-finite values.
Results may differ from the reference program's by a relative error of at most 0.024.
Values may be sent and summed in bfloat16 or wider, within the bound.
A program may use at most 192 MiB of HBM per device.

```python
import jax
import jax.numpy as jnp
from jax import lax

D = 896
QUERY_HEADS = 14
KEY_VALUE_HEADS = 2
HEAD_SIZE = 64
FF = 4864
MB = 2
LENGTH = 1024
QD = 896
KD = 128
SEQ_DEV = 64
SEQS = 16
N_DP = 8


def draw_positions(key, part):
    half_len = SEQ_DEV // 2
    pair_count = LENGTH // SEQ_DEV
    seq_keys = jax.random.split(key, SEQS)

    def arrange(seq_key):
        pair_order = jax.random.permutation(seq_key, pair_count).astype(jnp.int32)
        offsets = jnp.arange(half_len, dtype=jnp.int32)
        front_rows = pair_order[:, None] * half_len + offsets[None, :]
        back_rows = (2 * pair_count - 1 - pair_order)[:, None] * half_len + offsets[None, :]
        return jnp.concatenate([front_rows, back_rows], axis=1).reshape(LENGTH)
    return jax.vmap(arrange)(seq_keys).reshape(MB, SEQS // MB, LENGTH).astype(jnp.int32)


def levels(stream_key, shape, cuts, least, largest):
    level = 1.0
    for position, shards_of in cuts:
        draws = jax.random.uniform(jax.random.fold_in(jax.random.fold_in(stream_key, 6), position), (shards_of,), jnp.float32, least / len(cuts), largest / len(cuts))
        level = level * jnp.repeat(jnp.exp(draws), shape[position] // shards_of).reshape((-1,) + (1,) * (len(shape) - 1 - position))
    return level


def gaussian(rng, dims, spread, reach, cuts=(), kind=jnp.bfloat16):
    array = spread * jax.random.normal(rng, dims, jnp.float32)
    if cuts:
        array = array * levels(rng, dims, cuts, -0.22, 0.18)
    return jnp.clip(array, -reach, reach).astype(kind)


def setup_inputs(seed: int = 0) -> dict:
    key_list = jax.random.split(jax.random.key(seed), 16)
    return {
        "hidden_in": gaussian(key_list[0], (MB, N_DP, LENGTH, D), 1.0, 6.0, ((1, 8), (2, 16))),
        "positions": draw_positions(jax.random.fold_in(key_list[15], 71), 0),
        "norm_attn": jnp.clip(1.0 + 0.18 * jax.random.normal(key_list[2], (D,), jnp.float32), 0.099609375, 1.8984375).astype(jnp.bfloat16),
        "w_query": gaussian(key_list[3], (D, QD), D ** -0.5, 0.1875, ((0, 128),)),
        "b_query": gaussian(key_list[4], (QD,), 0.5, 3.0, ((0, 128),)),
        "w_key": gaussian(key_list[5], (D, KD), D ** -0.5, 0.1875, ((0, 128),)),
        "b_key": gaussian(key_list[6], (KD,), 0.5, 3.0, ((0, 128),)),
        "value_weight": gaussian(key_list[7], (D, KD), D ** -0.5, 0.1875, ((0, 128),)),
        "value_bias": gaussian(key_list[8], (KD,), 0.5, 3.0, ((0, 128),)),
        "w_output": gaussian(key_list[9], (QD, D), (max(QD // 4, 1)) ** -0.5, 0.375, ((0, 128),)),
        "norm_mlp": jnp.clip(1.0 + 0.18 * jax.random.normal(key_list[10], (D,), jnp.float32), 0.099609375, 1.8984375).astype(jnp.bfloat16),
        "w_gate": gaussian(key_list[11], (D, FF), D ** -0.5, 0.1875, ((0, 128),)),
        "w_up": gaussian(key_list[12], (D, FF), D ** -0.5, 0.1875, ((0, 128),)),
        "w_down": gaussian(key_list[13], (FF, D), FF ** -0.5, 0.078125, ((0, 128),)),
        "cotangent": gaussian(key_list[14], (MB, N_DP, LENGTH, D), 1.0, 6.0, ((1, 8), (2, 16))),
    }


@jax.custom_vjp
def low(v):
    return lax.optimization_barrier(v.astype(jnp.bfloat16)).astype(jnp.float32)

@jax.custom_vjp
def low_back(v):
    return v

def low_keep(v):
    return (low(v), None)

def low_pass(kept, grad):
    return (grad,)

def back_keep(v):
    return (v, None)

def back_low(kept, grad):
    return (low(grad),)
low.defvjp(low_keep, low_pass)
low_back.defvjp(back_keep, back_low)
EPSILON = 1e-06
THETA_BASE = 1000000.0

def matrix_product(left, right):
    return jnp.dot(left, right, precision=lax.Precision.HIGHEST)

def rms_scale(values):
    return lax.rsqrt(lax.optimization_barrier(jnp.mean(values * values, axis=-1, keepdims=True)) + EPSILON)

def rope_tables(places):
    freqs = THETA_BASE ** (-jnp.arange(0, HEAD_SIZE, 2).astype(jnp.float32) / HEAD_SIZE)
    angles = places.astype(jnp.float32)[:, None] * freqs[None, :]
    angles = jnp.concatenate([angles, angles], axis=-1)
    return (jnp.cos(angles), jnp.sin(angles))

def apply_rotary(values, cosine_table, sine_table):
    first_half = values[..., :HEAD_SIZE // 2]
    second_half = values[..., HEAD_SIZE // 2:]
    turned = jnp.concatenate([-second_half, first_half], axis=-1)
    return values * cosine_table[:, None, :] + turned * sine_table[:, None, :]

def layer(params, residual, places):
    norm_attn, w_query, b_query, w_key, b_key, value_weight, value_bias, w_output, norm_mlp, w_gate, w_up, w_down = params
    count_of_rows = residual.shape[0]
    normalized_input = low(residual * rms_scale(residual) * norm_attn)
    cosine_table, sine_table = rope_tables(places)
    query_lin = low_back(matrix_product(normalized_input, w_query) + b_query)
    key_linear = low_back(matrix_product(normalized_input, w_key) + b_key)
    narrow_values = low(low_back(matrix_product(normalized_input, value_weight) + value_bias)).reshape(count_of_rows, KEY_VALUE_HEADS, HEAD_SIZE)
    rotated_queries = low(apply_rotary(query_lin.reshape(count_of_rows, QUERY_HEADS, HEAD_SIZE), cosine_table, sine_table))
    rotated_queries = rotated_queries.reshape(count_of_rows, KEY_VALUE_HEADS, QUERY_HEADS // KEY_VALUE_HEADS, HEAD_SIZE)
    rotated_keys = low(apply_rotary(key_linear.reshape(count_of_rows, KEY_VALUE_HEADS, HEAD_SIZE), cosine_table, sine_table))
    scores = jnp.einsum('qghd,kgd->ghqk', rotated_queries, rotated_keys, precision=lax.Precision.HIGHEST) * HEAD_SIZE ** (-0.5)
    scores = low_back(scores)
    allowed = places[None, :] <= places[:, None]
    scores = jnp.where(allowed[None, None], scores, -1e+30)
    attn_probs = low(jax.nn.softmax(scores, axis=-1))
    attended = jnp.einsum('ghqk,kgd->qghd', attn_probs, narrow_values, precision=lax.Precision.HIGHEST)
    attended = low_back(low(attended.reshape(count_of_rows, QUERY_HEADS * HEAD_SIZE)))
    mixed = residual + low_back(matrix_product(attended, w_output))
    normed_mid = low(mixed * rms_scale(mixed) * norm_mlp)
    gate_lin = low_back(matrix_product(normed_mid, w_gate))
    up_lin = low_back(matrix_product(normed_mid, w_up))
    hidden = low_back(low(jax.nn.silu(gate_lin) * up_lin))
    return mixed + low_back(matrix_product(hidden, w_down))

def reference(hidden_in, positions, norm_attn, w_query, b_query, w_key, b_key, value_weight, value_bias, w_output, norm_mlp, w_gate, w_up, w_down, cotangent):
    params = tuple((tensor.astype(jnp.float32) for tensor in (norm_attn, w_query, b_query, w_key, b_key, value_weight, value_bias, w_output, norm_mlp, w_gate, w_up, w_down)))
    inputs = hidden_in.astype(jnp.float32).reshape(SEQS, LENGTH, D)
    places = positions.reshape(SEQS, LENGTH).astype(jnp.int32)

    def forward(weights, activations):
        per_sequence = jax.checkpoint(lambda item_pair: layer(weights, item_pair[0], item_pair[1]))
        return lax.map(per_sequence, (activations, places))
    outputs, pullback = jax.vjp(forward, params, inputs)
    grads, grad_inputs = pullback(cotangent.astype(jnp.float32).reshape(SEQS, LENGTH, D))
    full_shape = hidden_in.shape
    return (outputs.reshape(full_shape).astype(jnp.bfloat16), grad_inputs.reshape(full_shape), grads[0], grads[1], grads[2], grads[3], grads[4], grads[5], grads[6], grads[7], grads[8], grads[9], grads[10], grads[11])
```

```python
import functools

import jax
import jax.numpy as jnp
import numpy as np
from jax import lax
from jax.experimental import pallas as pl
from jax.experimental.pallas import tpu as pltpu
from jax.sharding import PartitionSpec as P

QUERY_HEADS = 14
KEY_VALUE_HEADS = 2
HEAD_SIZE = 64
GROUP = QUERY_HEADS // KEY_VALUE_HEADS
MB = 2
D = 896
DPAD = 1024
EPSILON = 1e-06
THETA_BASE = 1000000.0
F32 = jnp.float32
BF16 = jnp.bfloat16
MESH = pl.DeviceIdType.MESH
DMA = pltpu.SemaphoreType.DMA
VM = pltpu.VMEM


def remote(src, dst, ss, rs, peer):
    return pltpu.make_async_remote_copy(
        src_ref=src, dst_ref=dst, send_sem=ss, recv_sem=rs, device_id=peer, device_id_type=MESH
    )


def barrier(peers):
    sem = pltpu.get_barrier_semaphore()
    for peer in peers:
        pl.semaphore_signal(sem, inc=1, device_id=peer, device_id_type=MESH)
    pl.semaphore_wait(sem, len(peers))


class Place:
    def __init__(self):
        self.dp = lax.axis_index("dp")
        self.ctx = lax.axis_index("ctx")
        self.y, self.x = self.ctx // 4, lax.rem(self.ctx, 4)
        self.z, self.core = self.dp // 2, lax.rem(self.dp, 2)

    def at_x(self, k):
        return lax.rem(self.x + (k + 4), 4)

    def at_y(self, k):
        return lax.rem(self.y + (k + 4), 4)

    def at_z(self, k):
        return lax.rem(self.z + (k + 4), 4)

    def line(self, axis, k):
        return self.y * 4 + self.at_x(k) if axis == 0 else self.at_y(k) * 4 + self.x

    def xpeer(self, k):
        return {"ctx": self.line(0, k)}

    def ypeer(self, k):
        return {"ctx": self.line(1, k)}

    def peer(self, axis, k):
        return {"ctx": self.line(axis, k)}

    def zindex(self, k):
        return self.at_z(k) * 2 + self.core

    def mate(self):
        return self.z * 2 + 1 - self.core

    def dpindex(self, k):
        return lax.rem(self.dp + k, 8)


NEAR = (1, 3, 2)


class GatherCtx:
    SEMS = [DMA((2, 4)), DMA((2, 4)), DMA((2, 4, 4)), DMA((2, 4, 4)), DMA]

    def __init__(self, place, src, dst, sems):
        self.p, self.src, self.dst, self.sems = place, src, dst, sems

    def start(self):
        p, (s1, r1, s2, r2, ls) = self.p, self.sems
        self.local = pltpu.make_async_copy(self.src, self.dst.at[p.ctx], ls)
        self.local.start()
        self.first = {}
        for k in NEAR:
            for h in (0, 1):
                c = remote(self.src.at[h], self.dst.at[p.ctx, h], s1.at[h, k], r1.at[h, k], p.peer(h, k))
                c.start()
                self.first[h, k] = c

    def forward(self):
        p, (s1, r1, s2, r2, ls) = self.p, self.sems
        self.second = []
        for j in (0,) + NEAR:
            for h in (0, 1):
                if j:
                    self.first[h, j].wait_recv()
                block = p.line(h, -j)
                for k in NEAR:
                    src = self.src.at[h] if j == 0 else self.dst.at[block, h]
                    c = remote(src, self.dst.at[block, h], s2.at[h, j, k], r2.at[h, j, k], p.peer(1 - h, k))
                    c.start()
                    self.second.append(c)

    def arrive(self):
        self.local.wait()
        for c in self.second:
            c.wait_recv()

    def finish(self):
        for c in list(self.first.values()) + self.second:
            c.wait_send()


class ReduceCtx:
    SEMS = [DMA((2, 4)), DMA((2, 4)), DMA((2, 4)), DMA((2, 4))]

    @staticmethod
    def scratch(rows, cols):
        return [VM((2, 3, 4, rows, cols), BF16), VM((2, 4, rows, cols), BF16), VM((2, 3, rows, cols), BF16)]

    def __init__(self, place, src, bufs, sems):
        self.p, self.src, self.bufs, self.sems = place, src, bufs, sems

    def start(self):
        p, (s1, r1, s2, r2) = self.p, self.sems
        got = self.bufs[0]
        self.first = {}
        for k in NEAR:
            for h in (0, 1):
                src = self.src.at[p.at_y(k), :, 0] if h == 0 else self.src.at[:, p.at_x(k), 1]
                c = remote(src, got.at[h, k - 1], s1.at[h, k], r1.at[h, k], p.peer(1 - h, k))
                c.start()
                self.first[h, k] = c

    def forward(self):
        p, (s1, r1, s2, r2) = self.p, self.sems
        got, mid, last = self.bufs
        self.second = {}
        for h in (0, 1):
            for k in NEAR:
                self.first[h, k].wait_recv()
            for i in range(4):
                own = self.src[p.y, i, 0] if h == 0 else self.src[i, p.x, 1]
                total = own.astype(F32)
                for k in NEAR:
                    total = total + got[h, k - 1, i].astype(F32)
                mid[h, i] = total.astype(BF16)
            for k in NEAR:
                to = p.at_x(k) if h == 0 else p.at_y(k)
                c = remote(mid.at[h, to], last.at[h, k - 1], s2.at[h, k], r2.at[h, k], p.peer(h, k))
                c.start()
                self.second[h, k] = c

    def result(self, h):
        p = self.p
        got, mid, last = self.bufs
        for k in NEAR:
            self.second[h, k].wait_recv()
        total = mid[h, p.x if h == 0 else p.y].astype(F32)
        for k in NEAR:
            total = total + last[h, k - 1].astype(F32)
        return total

    def finish(self):
        for c in list(self.first.values()) + list(self.second.values()):
            c.wait_send()


class GatherDp:
    SEMS = [DMA((4,)), DMA((4,)), DMA((4,)), DMA((4,)), DMA]

    def __init__(self, place, src, dst, sems):
        self.p, self.src, self.dst, self.sems = place, src, dst, sems

    def start(self):
        p, (s1, r1, s2, r2, ls) = self.p, self.sems
        self.local = pltpu.make_async_copy(self.src, self.dst.at[p.dp], ls)
        self.local.start()
        self.first = {}
        for k in NEAR:
            c = remote(self.src, self.dst.at[p.dp], s1.at[k], r1.at[k], {"dp": p.zindex(k)})
            c.start()
            self.first[k] = c

    def forward(self):
        p, (s1, r1, s2, r2, ls) = self.p, self.sems
        self.second = []
        for j in (0,) + NEAR:
            if j:
                self.first[j].wait_recv()
            block = p.zindex(-j)
            src = self.src if j == 0 else self.dst.at[block]
            c = remote(src, self.dst.at[block], s2.at[j], r2.at[j], {"dp": p.mate()})
            c.start()
            self.second.append(c)

    def arrive(self):
        self.local.wait()
        for c in self.second:
            c.wait_recv()

    def finish(self):
        for c in list(self.first.values()) + self.second:
            c.wait_send()


class ReduceDp:
    SEMS = [DMA((4,)), DMA((4,)), DMA((4,)), DMA((4,))]

    @staticmethod
    def scratch(rows, cols):
        return [VM((4, rows, cols), BF16), VM((4, rows, cols), BF16), VM((3, rows, cols), BF16)]

    def __init__(self, place, src, bufs, sems):
        self.p, self.src, self.bufs, self.sems = place, src, bufs, sems

    def start(self):
        p, (s1, r1, s2, r2) = self.p, self.sems
        self.first = {}
        for k in NEAR + (0,):
            to = p.at_z(k)
            c = remote(self.src.at[to, 1 - p.core], self.bufs[0].at[to], s1.at[k], r1.at[k], {"dp": p.mate()})
            c.start()
            self.first[k] = c

    def forward(self):
        p, (s1, r1, s2, r2) = self.p, self.sems
        got, mid, last = self.bufs
        self.second = {}
        for k in NEAR + (0,):
            to = p.at_z(k)
            self.first[k].wait_recv()
            total = self.src[to, p.core].astype(F32) + got[to].astype(F32)
            mid[to] = total.astype(BF16)
            if k:
                c = remote(mid.at[to], last.at[k - 1], s2.at[k], r2.at[k], {"dp": p.zindex(k)})
                c.start()
                self.second[k] = c

    def result(self):
        got, mid, last = self.bufs
        total = mid[self.p.z].astype(F32)
        for k in NEAR:
            self.second[k].wait_recv()
            total = total + last[k - 1].astype(F32)
        return total

    def finish(self):
        for c in list(self.first.values()) + list(self.second.values()):
            c.wait_send()


def xy_peers(p):
    return [p.peer(axis, k) for axis in (0, 1) for k in NEAR]


def dp_peers(p):
    return [{"dp": p.dpindex(k)} for k in range(1, 8)]


def z_peers(p):
    return [{"dp": p.zindex(k)} for k in NEAR] + [{"dp": p.mate()}]


def comm_call(kernel, args, outs, scratch, cid, name):
    return pl.pallas_call(
        kernel,
        out_shape=outs,
        in_specs=[pl.BlockSpec(memory_space=VM)] * len(args),
        out_specs=jax.tree.map(lambda _: pl.BlockSpec(memory_space=VM), outs),
        scratch_shapes=scratch,
        name=name,
        compiler_params=pltpu.CompilerParams(
            collective_id=cid, has_side_effects=True, vmem_limit_bytes=56 << 20
        ),
    )(*args)


def shape(dims, kind):
    return jax.ShapeDtypeStruct(dims, kind)


def weights_kernel(
    attn, gate_up, down, small, places, cot,
    w_attn, w_gate_up, w_down, small_all, places_all, cot_all,
    attn_in, gu_in, down_in, small_x, small_y, small_dp, places_x, attn_block, gu_block, small_sum,
    s_attn, r_attn, s_gu, r_gu, s_down, r_down, s_down2, r_down2, s_small, r_small, s_place, r_place,
    s_place2, r_place2, s_mate, r_mate, local_sem, local2, *ring_sems,
):
    p = Place()
    barrier(xy_peers(p) + dp_peers(p))
    to_dp = []
    for k in range(1, 8):
        to = p.dpindex(k)
        c = remote(attn, attn_in.at[p.dp], s_attn.at[k], r_attn.at[k], {"dp": to})
        c.start()
        to_dp.append(c)
    for k in range(1, 8):
        to = p.dpindex(k)
        c = remote(gate_up.at[to], gu_in.at[p.dp], s_gu.at[k], r_gu.at[k], {"dp": to})
        c.start()
        to_dp.append(c)
    small_copies = []
    for k in NEAR:
        c = remote(small, small_x.at[k - 1], s_small.at[0, k], r_small.at[0, k], p.xpeer(k))
        c.start()
        small_copies.append(c)
    place_copies = []
    for k in NEAR:
        c = remote(places, places_x.at[p.x], s_place.at[k], r_place.at[k], p.xpeer(k))
        c.start()
        place_copies.append(c)
    down_copies = []
    for k in NEAR:
        c = remote(down, down_in.at[p.x], s_down.at[k], r_down.at[k], p.xpeer(k))
        c.start()
        down_copies.append(c)
    cots = GatherDp(p, cot, cot_all, ring_sems[10:15])
    cots.start()
    attn_in[p.dp] = attn[...]
    gu_in[p.dp] = gate_up[p.dp]
    down_in[p.x] = down[...]
    places_x[p.x] = places[...]
    for c in to_dp[:7]:
        c.wait_recv()
    for half in (0, 1):
        for i in range(2):
            attn_block[half, i] = jnp.concatenate(
                [attn_in[4 * i + d, half] for d in range(4)], axis=0
            ).astype(BF16)
    own = attn_block.at[p.core]
    target = w_attn.at[p.core]
    ring_attn = GatherCtx(p, own, target, ring_sems[0:5])
    ring_attn.start()
    for c in to_dp[7:]:
        c.wait_recv()
    for i in range(2):
        gu_block[i] = jnp.concatenate([gu_in[4 * i + d] for d in range(4)], axis=0).astype(BF16)
    ring_gu = GatherCtx(p, gu_block, w_gate_up, ring_sems[5:10])
    ring_gu.start()
    total = small[...]
    for c in small_copies:
        c.wait_recv()
    for k in NEAR:
        total = total + small_x[k - 1]
    small_sum[0] = total
    small_y_copies = []
    for k in NEAR:
        c = remote(small_sum.at[0], small_y.at[k - 1], s_small.at[1, k], r_small.at[1, k], p.ypeer(k))
        c.start()
        small_y_copies.append(c)
    ring_attn.forward()
    for c in place_copies:
        c.wait_recv()
    place_copies2 = []
    for k in NEAR:
        c = remote(places_x, places_all.at[p.y], s_place2.at[k], r_place2.at[k], p.ypeer(k))
        c.start()
        place_copies2.append(c)
    places_all[p.y] = places_x[...]
    for c in down_copies:
        c.wait_recv()
    w_down[p.y] = jnp.concatenate([down_in[i] for i in range(4)], axis=0).astype(BF16)
    down_copies2 = []
    for k in NEAR:
        c = remote(w_down.at[p.y], w_down.at[p.y], s_down2.at[k], r_down2.at[k], p.ypeer(k))
        c.start()
        down_copies2.append(c)
    for c in small_y_copies:
        c.wait_recv()
    total = small_sum[0]
    for k in NEAR:
        total = total + small_y[k - 1]
    small_sum[1] = total
    small_dp_copies = []
    for k in range(1, 8):
        c = remote(small_sum.at[1], small_dp.at[k - 1], s_small.at[2, k], r_small.at[2, k], {"dp": p.dpindex(k)})
        c.start()
        small_dp_copies.append(c)
    cots.forward()
    ring_gu.forward()
    ring_attn.arrive()
    mate = remote(w_attn.at[p.core], w_attn.at[p.core], s_mate, r_mate, {"dp": p.mate()})
    mate.start()
    total = small_sum[1]
    for k in range(1, 8):
        small_dp_copies[k - 1].wait_recv()
        total = total + small_dp[k - 1]
    small_all[...] = total
    cots.arrive()
    for c in down_copies2 + place_copies2:
        c.wait_recv()
    ring_gu.arrive()
    mate.wait()
    for ring in (ring_attn, ring_gu, cots):
        ring.finish()
    for c in to_dp + small_copies + place_copies + down_copies + place_copies2 + down_copies2 + small_y_copies:
        c.wait_send()
    for c in small_dp_copies:
        c.wait_send()


def gather_weights(attn, gate_up, down, small, places, cot):
    outs = (
        shape((2, 16, 2, 32, 1024), BF16),
        shape((16, 2, 32, 1280), BF16),
        shape((4, 160, D), BF16),
        shape((24, 128), F32),
        shape((4, 4, 8, 128), F32),
        shape((8, 128, D), BF16),
    )
    scratch = [
        VM((8, 2, 8, 1024), F32), VM((8, 8, 1280), F32), VM((4, 40, D), F32), VM((3, 24, 128), F32),
        VM((3, 24, 128), F32), VM((7, 24, 128), F32), VM((4, 8, 128), F32), VM((2, 2, 32, 1024), BF16),
        VM((2, 32, 1280), BF16), VM((2, 24, 128), F32),
        DMA((8,)), DMA((8,)), DMA((8,)), DMA((8,)), DMA((4,)), DMA((4,)), DMA((4,)), DMA((4,)),
        DMA((3, 8)), DMA((3, 8)), DMA((4,)), DMA((4,)), DMA((4,)), DMA((4,)), DMA, DMA, DMA, DMA,
    ] + GatherCtx.SEMS * 2 + GatherDp.SEMS
    return comm_call(
        weights_kernel, (attn, gate_up, down, small, places, cot), outs, scratch, 0, "gather_weights"
    )


def grads_kernel(
    g_attn, g_gu, g_down, small,
    o_attn, o_gu, o_down, o_small,
    mate_in, attn_sum, down_y, down_mid, down_x, attn_out, gu_out, attn_dp, small_x, small_y, small_dp, small_sum,
    *rest,
):
    bufs_attn, bufs_gu, rest = rest[:3], rest[3:6], rest[6:]
    (s_mate, r_mate, s_down, r_down, s_down2, r_down2, s_small, r_small, s_attn, r_attn, s_gu, r_gu) = rest[:12]
    sems_attn, sems_gu = rest[12:16], rest[16:20]
    p = Place()
    barrier(xy_peers(p) + dp_peers(p))
    mate_copies = []
    for y in range(4):
        c = remote(g_attn.at[1 - p.core, y], mate_in.at[y], s_mate.at[y], r_mate.at[y], {"dp": p.mate()})
        c.start()
        mate_copies.append(c)
    small_copies = []
    for k in NEAR:
        c = remote(small, small_x.at[k - 1], s_small.at[0, k], r_small.at[0, k], p.xpeer(k))
        c.start()
        small_copies.append(c)
    ring_gu = ReduceCtx(p, g_gu, bufs_gu, sems_gu)
    ring_gu.start()
    down_copies = []
    for k in NEAR:
        c = remote(g_down.at[p.at_y(k)], down_y.at[k - 1], s_down.at[k], r_down.at[k], p.ypeer(k))
        c.start()
        down_copies.append(c)
    for y in range(4):
        mate_copies[y].wait_recv()
        attn_sum[y] = (g_attn[p.core, y].astype(F32) + mate_in[y].astype(F32)).astype(BF16)
    ring_attn = ReduceCtx(p, attn_sum, bufs_attn, sems_attn)
    ring_attn.start()
    for c in small_copies:
        c.wait_recv()
    small_sum[0] = small[...] + small_x[0] + small_x[1] + small_x[2]
    small_y_copies = []
    for k in NEAR:
        c = remote(small_sum.at[0], small_y.at[k - 1], s_small.at[1, k], r_small.at[1, k], p.ypeer(k))
        c.start()
        small_y_copies.append(c)
    ring_gu.forward()
    for c in down_copies:
        c.wait_recv()
    total = g_down[p.y].astype(F32)
    for k in NEAR:
        total = total + down_y[k - 1].astype(F32)
    for i in range(4):
        down_mid[i] = total[40 * i : 40 * i + 40]
    down_copies2 = []
    for k in NEAR:
        c = remote(down_mid.at[p.at_x(k)], down_x.at[k - 1], s_down2.at[k], r_down2.at[k], p.xpeer(k))
        c.start()
        down_copies2.append(c)
    for c in small_y_copies:
        c.wait_recv()
    small_sum[1] = small_sum[0] + small_y[0] + small_y[1] + small_y[2]
    small_dp_copies = []
    for k in range(1, 8):
        c = remote(small_sum.at[1], small_dp.at[k - 1], s_small.at[2, k], r_small.at[2, k], {"dp": p.dpindex(k)})
        c.start()
        small_dp_copies.append(c)
    ring_attn.forward()
    for h in (0, 1):
        part = ring_gu.result(h)
        for d in range(4):
            gu_out[4 * h + d] = part[8 * d : 8 * d + 8]
    out_copies = []
    for k in range(1, 8):
        to = p.dpindex(k)
        c = remote(gu_out.at[to], o_gu.at[p.dp], s_gu.at[k], r_gu.at[k], {"dp": to})
        c.start()
        out_copies.append(c)
    o_gu[p.dp] = gu_out[p.dp]
    for c in down_copies2:
        c.wait_recv()
    o_down[...] = down_mid[p.x] + down_x[0] + down_x[1] + down_x[2]
    for h in (0, 1):
        part = ring_attn.result(h)
        for d in range(4):
            attn_out[4 * h + d] = part[8 * d : 8 * d + 8]
    for k in range(1, 8):
        to = p.dpindex(k)
        c = remote(attn_out.at[to], attn_dp.at[p.z, p.core], s_attn.at[k], r_attn.at[k], {"dp": to})
        c.start()
        out_copies.append(c)
    attn_dp[p.z, p.core] = attn_out[p.dp]
    total = small_sum[1]
    for k in range(1, 8):
        small_dp_copies[k - 1].wait_recv()
        total = total + small_dp[k - 1]
    o_small[...] = total
    for c in out_copies:
        c.wait_recv()
    for half in (0, 1):
        o_attn[half] = attn_dp[0, half] + attn_dp[1, half] + attn_dp[2, half] + attn_dp[3, half]
    ring_gu.finish()
    ring_attn.finish()
    for c in mate_copies + small_copies + small_y_copies + small_dp_copies + down_copies + down_copies2 + out_copies:
        c.wait_send()


def reduce_grads(g_attn, g_gu, g_down, small):
    outs = (
        shape((2, 8, 1024), F32),
        shape((8, 8, 1280), F32),
        shape((40, D), F32),
        shape((24, 128), F32),
    )
    scratch = [
        VM((4, 4, 2, 32, 1024), BF16), VM((4, 4, 2, 32, 1024), BF16), VM((3, 160, D), BF16), VM((4, 40, D), F32),
        VM((3, 40, D), F32), VM((8, 8, 1024), F32), VM((8, 8, 1280), F32), VM((4, 2, 8, 1024), F32),
        VM((3, 24, 128), F32), VM((3, 24, 128), F32), VM((7, 24, 128), F32), VM((2, 24, 128), F32),
    ] + ReduceCtx.scratch(32, 1024) + ReduceCtx.scratch(32, 1280) + [
        DMA((4,)), DMA((4,)), DMA((4,)), DMA((4,)), DMA((4,)), DMA((4,)), DMA((3, 8)), DMA((3, 8)),
        DMA((8,)), DMA((8,)), DMA((8,)), DMA((8,)),
    ] + ReduceCtx.SEMS * 2
    return comm_call(grads_kernel, (g_attn, g_gu, g_down, small), outs, scratch, 1, "reduce_grads")


def gather_ctx_kernel(src, dst, *sems):
    p = Place()
    barrier(xy_peers(p))
    ring = GatherCtx(p, src, dst, sems)
    ring.start()
    ring.forward()
    ring.arrive()
    ring.finish()


def gather_ctx(src, cid, name):
    return comm_call(
        gather_ctx_kernel, (src,), shape((16,) + src.shape, src.dtype), GatherCtx.SEMS, cid, name
    )


def reduce_ctx_kernel(src, out, b0, b1, b2, *sems):
    p = Place()
    barrier(xy_peers(p))
    ring = ReduceCtx(p, src, (b0, b1, b2), sems)
    ring.start()
    ring.forward()
    for h in (0, 1):
        out[h] = ring.result(h)
    ring.finish()


def reduce_ctx(src, cid, name):
    rows, cols = src.shape[-2:]
    return comm_call(
        reduce_ctx_kernel, (src,), shape((2, rows, cols), F32),
        ReduceCtx.scratch(rows, cols) + ReduceCtx.SEMS, cid, name,
    )


def gather_dp_kernel(src, dst, *sems):
    p = Place()
    barrier(z_peers(p))
    ring = GatherDp(p, src, dst, sems)
    ring.start()
    ring.forward()
    ring.arrive()
    ring.finish()


def gather_dp(src, cid, name):
    return comm_call(gather_dp_kernel, (src,), shape((8,) + src.shape, src.dtype), GatherDp.SEMS, cid, name)


def reduce_dp_kernel(src, out, b0, b1, b2, *sems):
    p = Place()
    barrier(z_peers(p))
    ring = ReduceDp(p, src, (b0, b1, b2), sems)
    ring.start()
    ring.forward()
    out[...] = ring.result()
    ring.finish()


def reduce_dp(src, cid, name):
    rows, cols = src.shape[-2:]
    return comm_call(
        reduce_dp_kernel, (src,), shape((rows, cols), F32), ReduceDp.scratch(rows, cols) + ReduceDp.SEMS, cid, name
    )


def matrix_product(left, right):
    return jnp.dot(left, right, preferred_element_type=F32)


def matmul_tn(left, right):
    return lax.dot_general(left, right, (((0,), (0,)), ((), ())), preferred_element_type=F32)


def matmul_nt(left, right):
    return lax.dot_general(left, right, (((1,), (1,)), ((), ())), preferred_element_type=F32)


def rms_scale(values):
    return lax.rsqrt(jnp.mean(values * values, axis=-1, keepdims=True) + EPSILON)


def rope_tables(places, head_dim):
    freqs = THETA_BASE ** (-jnp.arange(0, head_dim, 2).astype(F32) / head_dim)
    angles = places.astype(F32)[:, None] * freqs[None, :]
    angles = jnp.concatenate([angles, angles], axis=-1)
    return (jnp.cos(angles), jnp.sin(angles))


def apply_rotary(values, cosine_table, sine_table):
    half_dim = values.shape[-1] // 2
    turned = jnp.concatenate([-values[..., half_dim:], values[..., :half_dim]], axis=-1)
    return values * cosine_table[:, None, :] + turned * sine_table[:, None, :]


def inverse_rotary(grads, cosine_table, sine_table):
    half_dim = grads.shape[-1] // 2
    direct = grads * cosine_table[:, None, :]
    turned = grads * sine_table[:, None, :]
    return direct + jnp.concatenate([turned[..., half_dim:], -turned[..., :half_dim]], axis=-1)


def attend(queries, key_all, value_all, query_places, key_places, factor):
    scores = jnp.einsum("bqghd,bkgd->bghqk", queries, key_all, preferred_element_type=F32) * factor
    allowed = key_places[:, None, :] <= query_places[:, :, None]
    scores = jnp.where(allowed[:, None, None], scores, -1e30)
    top = jnp.max(scores, axis=-1, keepdims=True)
    expo = jnp.exp(scores - top)
    probs = (expo / jnp.sum(expo, axis=-1, keepdims=True)).astype(BF16)
    return probs, jnp.einsum("bghqk,bkgd->bqghd", probs, value_all, preferred_element_type=F32)


def attend_back(queries, key_all, value_all, probs, attended_gradient, factor):
    grad_probs = jnp.einsum("bqghd,bkgd->bghqk", attended_gradient, value_all, preferred_element_type=F32)
    wide = probs.astype(F32)
    inner = jnp.sum(wide * grad_probs, axis=-1, keepdims=True)
    grad_scores = (wide * (grad_probs - inner)).astype(BF16)
    grad_query = jnp.einsum("bghqk,bkgd->bqghd", grad_scores, key_all, preferred_element_type=F32) * factor
    grad_key = jnp.einsum("bghqk,bqghd->bkgd", grad_scores, queries, preferred_element_type=F32) * factor
    grad_value = jnp.einsum("bghqk,bqghd->bkgd", probs, attended_gradient, preferred_element_type=F32)
    return grad_query, grad_key, grad_value


def spread(values, kind):
    rows = values.shape[0]
    parts = values.astype(kind).reshape(rows, 8, 16, 7)
    parts = jnp.pad(parts, ((0, 0), (0, 0), (0, 0), (0, 1)))
    return parts.transpose(0, 2, 1, 3).reshape(rows, DPAD)


def unspread(values):
    rows = values.shape[0]
    return values.reshape(rows, 16, 8, 8)[..., :7].transpose(0, 2, 1, 3).reshape(rows, D)


def body(
    hidden_in, positions, norm_attn, w_query, b_query, w_key, b_key, value_weight, value_bias, w_output,
    norm_mlp, w_gate, w_up, w_down, cotangent,
):
    factor = HEAD_SIZE ** (-0.5)
    rows = MB * 64
    me = lax.axis_index("dp") * 16 + lax.axis_index("ctx")
    places = positions[:, 0]
    attn = jnp.pad(
        jnp.stack(
            [jnp.concatenate([w_query, w_key], axis=1), jnp.concatenate([value_weight, w_output], axis=1)]
        ).astype(F32),
        ((0, 0), (0, 1), (0, 0)),
    )

    def slices(w):
        parts = w.astype(F32).reshape(7, 8, 16, 38)
        return jnp.pad(parts, ((0, 1), (0, 0), (0, 0), (0, 2))).transpose(1, 0, 2, 3).reshape(8, 8, 640)

    gate_up = jnp.concatenate([slices(w_gate), slices(w_up)], axis=-1)
    down = jnp.pad(w_down.astype(F32), ((0, 2), (0, 0)))

    def put(vector, width):
        full = jnp.zeros((128, width), F32)
        return lax.dynamic_update_slice(full, vector.astype(F32)[None], (me, 0)).reshape(-1)

    small = jnp.concatenate(
        [put(norm_attn, 7), put(b_query, 7), put(norm_mlp, 7), put(b_key, 1), put(value_bias, 1), jnp.zeros((128,), F32)]
    ).reshape(24, 128)
    place_rows = jnp.pad(jnp.tile(places.astype(F32), (1, 2)), ((0, 6), (0, 0)))
    cot = cotangent.reshape(rows, D)
    w_attn, w_gu, down_full, small_all, places_all, cot_all = gather_weights(
        attn, gate_up, down, small, place_rows, cot
    )
    w_attn = w_attn.reshape(2, DPAD, 1024)
    qk_full, vo_full = w_attn[0], w_attn[1]
    query_full, key_full = qk_full[:, :896], qk_full[:, 896:]
    value_full, output_full = vo_full[:, :128], vo_full[:, 128:]
    w_gu = w_gu.reshape(DPAD, 1280)
    down_full = down_full.reshape(640, D)
    vectors = small_all.reshape(-1)
    gain_attn, bias_query, gain_mlp = vectors[:896], vectors[896:1792], vectors[1792:2688]
    bias_key, bias_value = vectors[2688:2816], vectors[2816:2944]
    key_places = places_all.reshape(16, 8, 128)[:, :2, :64].transpose(1, 0, 2).reshape(2, 1024)
    query_places = places.astype(F32)

    residual = hidden_in.reshape(rows, D).astype(F32)
    inv_rms = rms_scale(residual)
    unit_in = residual * inv_rms
    normed_in = spread((unit_in * gain_attn).astype(BF16), BF16)
    cosine, sine = rope_tables(places.reshape(rows), HEAD_SIZE)
    query_lin = matrix_product(normed_in, query_full) + bias_query
    key_lin = matrix_product(normed_in, key_full) + bias_key
    value_lin = matrix_product(normed_in, value_full) + bias_value
    queries = apply_rotary(query_lin.reshape(rows, QUERY_HEADS, HEAD_SIZE), cosine, sine).astype(BF16)
    queries = queries.reshape(MB, 64, KEY_VALUE_HEADS, GROUP, HEAD_SIZE)
    keys = apply_rotary(key_lin.reshape(rows, KEY_VALUE_HEADS, HEAD_SIZE), cosine, sine).astype(BF16)
    key_value = jnp.concatenate([keys.reshape(rows, 128), value_lin.astype(BF16)], axis=1).reshape(MB, 64, 256)
    kv_all = gather_ctx(key_value, 2, "gather_kv").transpose(1, 0, 2, 3).reshape(MB, 1024, 256)
    key_all = kv_all[..., :128].reshape(MB, 1024, 2, 64)
    value_all = kv_all[..., 128:].reshape(MB, 1024, 2, 64)
    probs, attended = attend(queries, key_all, value_all, query_places, key_places, factor)
    attended_low = spread(attended.reshape(rows, D).astype(BF16), BF16)
    mixed = residual + matrix_product(attended_low, output_full)
    inv_mid = rms_scale(mixed)
    unit_mid = mixed * inv_mid
    normed_mid = spread((unit_mid * gain_mlp).astype(BF16), BF16)

    normed_all = gather_dp(normed_mid, 3, "gather_rows").reshape(1024, DPAD)
    cot_all = cot_all.reshape(1024, D)
    gu_lin = matrix_product(normed_all, w_gu)
    gate_lin, up_lin = gu_lin[:, :640], gu_lin[:, 640:]
    sigmoid_gate = jax.nn.sigmoid(gate_lin)
    hidden_low = (gate_lin * sigmoid_gate * up_lin).astype(BF16)
    part_out = matrix_product(hidden_low, down_full).astype(BF16)
    branch = reduce_dp(part_out.reshape(4, 2, 128, D), 4, "reduce_out")
    layer_out = (mixed + branch).astype(BF16)

    grad_top = cot.astype(F32)
    grad_down_w = matmul_tn(hidden_low, cot_all)
    hidden_back = matmul_nt(cot_all, down_full).astype(BF16).astype(F32)
    grad_gate = (hidden_back * up_lin * sigmoid_gate * (1.0 + gate_lin * (1.0 - sigmoid_gate))).astype(BF16)
    grad_upward = (hidden_back * gate_lin * sigmoid_gate).astype(BF16)
    grad_gu = jnp.concatenate([grad_gate, grad_upward], axis=1)
    part_normed = matmul_nt(grad_gu, w_gu).astype(BF16)
    grad_normed_mid = unspread(reduce_dp(part_normed.reshape(4, 2, 128, DPAD), 5, "reduce_normed"))
    grad_gu_w = matmul_tn(normed_all, grad_gu)
    grad_gain_mid = jnp.sum(grad_normed_mid * unit_mid, axis=0)
    scaled_mid = grad_normed_mid * gain_mlp
    grad_mixed = grad_top + inv_mid * (
        scaled_mid - unit_mid * jnp.mean(scaled_mid * unit_mid, axis=-1, keepdims=True)
    )
    grad_attn_branch = grad_mixed.astype(BF16)
    grad_output_w = matmul_tn(attended_low, grad_attn_branch)
    attended_gradient = unspread(matmul_nt(grad_attn_branch, output_full).astype(BF16))
    attended_gradient = attended_gradient.reshape(MB, 64, KEY_VALUE_HEADS, GROUP, HEAD_SIZE)
    grad_query_rot, grad_key_part, grad_value_part = attend_back(
        queries, key_all, value_all, probs, attended_gradient, factor
    )
    kv_grad = jnp.concatenate(
        [grad_key_part.reshape(MB, 1024, 128), grad_value_part.reshape(MB, 1024, 128)], axis=-1
    ).astype(BF16)
    kv_grad = kv_grad.reshape(MB, 4, 4, 64, 256).transpose(1, 2, 0, 3, 4)
    kv_sum = reduce_ctx(kv_grad, 6, "reduce_kv").reshape(rows, 256)
    grad_query_low = inverse_rotary(grad_query_rot.reshape(rows, QUERY_HEADS, HEAD_SIZE), cosine, sine)
    grad_query_low = grad_query_low.reshape(rows, D).astype(BF16)
    grad_key_low = inverse_rotary(kv_sum[:, :128].reshape(rows, KEY_VALUE_HEADS, HEAD_SIZE), cosine, sine)
    grad_key_low = grad_key_low.reshape(rows, 128).astype(BF16)
    grad_value_low = kv_sum[:, 128:].astype(BF16)
    grad_qk = jnp.concatenate([grad_query_low, grad_key_low], axis=1)
    grad_qk_w = matmul_tn(normed_in, grad_qk)
    grad_vo_w = jnp.concatenate([matmul_tn(normed_in, grad_value_low), grad_output_w], axis=1)
    grad_normed_in = unspread(matmul_nt(grad_qk, qk_full) + matmul_nt(grad_value_low, value_full))
    scaled_in = grad_normed_in * gain_attn
    grad_in = grad_mixed + inv_rms * (
        scaled_in - unit_in * jnp.mean(scaled_in * unit_in, axis=-1, keepdims=True)
    )
    small_grads = jnp.concatenate(
        [
            jnp.sum(grad_normed_in * unit_in, axis=0),
            jnp.sum(grad_query_low.astype(F32), axis=0),
            grad_gain_mid,
            jnp.sum(grad_key_low.astype(F32), axis=0),
            jnp.sum(grad_value_low.astype(F32), axis=0),
            jnp.zeros((128,), F32),
        ]
    ).reshape(24, 128)
    o_attn, o_gu, o_down, o_small = reduce_grads(
        jnp.stack([grad_qk_w, grad_vo_w]).astype(BF16).reshape(2, 4, 4, 2, 32, 1024),
        grad_gu_w.astype(BF16).reshape(4, 4, 2, 32, 1280),
        grad_down_w.astype(BF16).reshape(4, 160, D),
        small_grads,
    )

    def joined(parts):
        return parts[:, :7].reshape(8, 7, 16, 40)[..., :38].transpose(1, 0, 2, 3).reshape(7, 4864)

    sums = o_small.reshape(-1)

    def take(start, width):
        return lax.dynamic_slice(sums, (start + me * width,), (width,))

    return (
        layer_out.reshape(MB, 1, 64, D),
        grad_in.reshape(MB, 1, 64, D),
        take(0, 7),
        o_attn[0, :7, :896],
        take(896, 7),
        o_attn[0, :7, 896:],
        sums[2688:2816],
        o_attn[1, :7, :128],
        take(2816, 1),
        o_attn[1, :7, 128:],
        take(1792, 7),
        joined(o_gu[..., :640]),
        joined(o_gu[..., 640:]),
        o_down[:38],
    )


def solution(mesh):
    rows = P(("dp", "ctx"), None)
    vector = P(("dp", "ctx"))
    tokens = P(None, "dp", "ctx", None)
    in_specs = (
        tokens, P(None, "dp", "ctx"), vector, rows, vector, rows, vector, rows, vector, rows, vector,
        rows, rows, rows, tokens,
    )
    out_specs = (
        tokens, tokens, vector, rows, vector, rows, P(), rows, vector, rows, vector, rows, rows, rows,
    )
    return jax.shard_map(body, mesh=mesh, in_specs=in_specs, out_specs=out_specs, check_vma=False)
```

```python
import types

import jax
import jax.numpy as jnp
from jax import lax
from jax.experimental import pallas as pl
from jax.experimental.pallas import tpu as pltpu
from jax.sharding import PartitionSpec as P

QUERY_HEADS = 14
KEY_VALUE_HEADS = 2
HEAD_SIZE = 64
GROUP = QUERY_HEADS // KEY_VALUE_HEADS
MB = 2
D = 896
DPAD = 1024
EPSILON = 1e-06
THETA_BASE = 1000000.0
F32 = jnp.float32
BF16 = jnp.bfloat16
MESH = pl.DeviceIdType.MESH
DMA = pltpu.SemaphoreType.DMA
VM = pltpu.VMEM


def remote(src, dst, ss, rs, peer):
    return pltpu.make_async_remote_copy(
        src_ref=src, dst_ref=dst, send_sem=ss, recv_sem=rs, device_id=peer, device_id_type=MESH
    )


def barrier(peers):
    sem = pltpu.get_barrier_semaphore()
    for peer in peers:
        pl.semaphore_signal(sem, inc=1, device_id=peer, device_id_type=MESH)
    pl.semaphore_wait(sem, len(peers))


class Place:
    def __init__(self):
        self.dp = lax.axis_index("dp")
        self.ctx = lax.axis_index("ctx")
        self.y, self.x = self.ctx // 4, lax.rem(self.ctx, 4)
        self.z, self.core = self.dp // 2, lax.rem(self.dp, 2)

    def at_x(self, k):
        return lax.rem(self.x + (k + 4), 4)

    def at_y(self, k):
        return lax.rem(self.y + (k + 4), 4)

    def at_z(self, k):
        return lax.rem(self.z + (k + 4), 4)

    def line(self, axis, k):
        return self.y * 4 + self.at_x(k) if axis == 0 else self.at_y(k) * 4 + self.x

    def xpeer(self, k):
        return {"ctx": self.line(0, k)}

    def ypeer(self, k):
        return {"ctx": self.line(1, k)}

    def peer(self, axis, k):
        return {"ctx": self.line(axis, k)}

    def zindex(self, k):
        return self.at_z(k) * 2 + self.core

    def mate(self):
        return self.z * 2 + 1 - self.core

    def dpindex(self, k):
        return lax.rem(self.dp + k, 8)


NEAR = (1, 3, 2)


class GatherCtx:
    SEMS = [DMA((2, 4)), DMA((2, 4)), DMA((2, 4, 4)), DMA((2, 4, 4)), DMA]
    MATE = [DMA((2, 4, 4)), DMA((2, 4, 4))]

    def __init__(self, place, src, dst, sems, mate=None):
        self.p, self.src, self.dst, self.sems, self.mate = place, src, dst, sems, mate
        self.mated = []

    def block(self, h, j, k):
        p = self.p
        return p.at_y(-k) * 4 + p.at_x(-j) if h == 0 else p.at_y(-j) * 4 + p.at_x(-k)

    def share(self, h, j, k):
        if self.mate is None:
            return
        src = self.src.at[h] if j == 0 and k == 0 else self.dst.at[self.block(h, j, k), h]
        dst = self.dst.at[self.block(h, j, k), h]
        c = remote(src, dst, self.mate[0].at[h, j, k], self.mate[1].at[h, j, k], {"dp": self.p.mate()})
        c.start()
        self.mated.append(c)

    def start(self):
        p, (s1, r1, s2, r2, ls) = self.p, self.sems
        self.local = pltpu.make_async_copy(self.src, self.dst.at[p.ctx], ls)
        self.local.start()
        self.first = {}
        for k in NEAR:
            for h in (0, 1):
                c = remote(self.src.at[h], self.dst.at[p.ctx, h], s1.at[h, k], r1.at[h, k], p.peer(h, k))
                c.start()
                self.first[h, k] = c
        for h in (0, 1):
            self.share(h, 0, 0)

    def forward(self):
        p, (s1, r1, s2, r2, ls) = self.p, self.sems
        self.second = {}
        for j in (0,) + NEAR:
            for h in (0, 1):
                if j:
                    self.first[h, j].wait_recv()
                block = p.line(h, -j)
                for k in NEAR:
                    src = self.src.at[h] if j == 0 else self.dst.at[block, h]
                    c = remote(src, self.dst.at[block, h], s2.at[h, j, k], r2.at[h, j, k], p.peer(1 - h, k))
                    c.start()
                    self.second[h, j, k] = c
                if j:
                    self.share(h, j, 0)

    def arrive(self):
        self.local.wait()
        for (h, j, k), c in self.second.items():
            c.wait_recv()
            self.share(h, j, k)
        for c in self.mated:
            c.wait_recv()

    def finish(self):
        for c in list(self.first.values()) + list(self.second.values()) + self.mated:
            c.wait_send()


class ReduceCtx:
    SEMS = [DMA((2, 4)), DMA((2, 4)), DMA((2, 4)), DMA((2, 4))]

    @staticmethod
    def scratch(rows, cols):
        return [VM((2, 3, 4, rows, cols), BF16), VM((2, 4, rows, cols), BF16), VM((2, 3, rows, cols), BF16)]

    def __init__(self, place, src, bufs, sems):
        self.p, self.src, self.bufs, self.sems = place, src, bufs, sems

    def start(self):
        p, (s1, r1, s2, r2) = self.p, self.sems
        got = self.bufs[0]
        self.first = {}
        for k in NEAR:
            for h in (0, 1):
                src = self.src.at[p.at_y(k), :, 0] if h == 0 else self.src.at[:, p.at_x(k), 1]
                c = remote(src, got.at[h, k - 1], s1.at[h, k], r1.at[h, k], p.peer(1 - h, k))
                c.start()
                self.first[h, k] = c

    def forward(self):
        p, (s1, r1, s2, r2) = self.p, self.sems
        got, mid, last = self.bufs
        self.second = {}
        for h in (0, 1):
            for k in NEAR:
                self.first[h, k].wait_recv()
            for i in range(4):
                own = self.src[p.y, i, 0] if h == 0 else self.src[i, p.x, 1]
                total = own.astype(F32)
                for k in NEAR:
                    total = total + got[h, k - 1, i].astype(F32)
                mid[h, i] = total.astype(BF16)
            for k in NEAR:
                to = p.at_x(k) if h == 0 else p.at_y(k)
                c = remote(mid.at[h, to], last.at[h, k - 1], s2.at[h, k], r2.at[h, k], p.peer(h, k))
                c.start()
                self.second[h, k] = c

    def result(self, h):
        p = self.p
        got, mid, last = self.bufs
        for k in NEAR:
            self.second[h, k].wait_recv()
        total = mid[h, p.x if h == 0 else p.y].astype(F32)
        for k in NEAR:
            total = total + last[h, k - 1].astype(F32)
        return total

    def finish(self):
        for c in list(self.first.values()) + list(self.second.values()):
            c.wait_send()


class GatherDp:
    SEMS = [DMA((4,)), DMA((4,)), DMA((4,)), DMA((4,)), DMA]

    def __init__(self, place, src, dst, sems):
        self.p, self.src, self.dst, self.sems = place, src, dst, sems

    def start(self):
        p, (s1, r1, s2, r2, ls) = self.p, self.sems
        self.local = pltpu.make_async_copy(self.src, self.dst.at[p.dp], ls)
        self.local.start()
        self.first = {}
        for k in NEAR:
            c = remote(self.src, self.dst.at[p.dp], s1.at[k], r1.at[k], {"dp": p.zindex(k)})
            c.start()
            self.first[k] = c

    def forward(self):
        p, (s1, r1, s2, r2, ls) = self.p, self.sems
        self.second = []
        for j in (0,) + NEAR:
            if j:
                self.first[j].wait_recv()
            block = p.zindex(-j)
            src = self.src if j == 0 else self.dst.at[block]
            c = remote(src, self.dst.at[block], s2.at[j], r2.at[j], {"dp": p.mate()})
            c.start()
            self.second.append(c)

    def arrive(self):
        self.local.wait()
        for c in self.second:
            c.wait_recv()

    def finish(self):
        for c in list(self.first.values()) + self.second:
            c.wait_send()


class ReduceDp:
    SEMS = [DMA((4,)), DMA((4,)), DMA((4,)), DMA((4,))]

    @staticmethod
    def scratch(rows, cols):
        return [VM((4, rows, cols), BF16), VM((4, rows, cols), BF16), VM((3, rows, cols), BF16)]

    def __init__(self, place, src, bufs, sems):
        self.p, self.src, self.bufs, self.sems = place, src, bufs, sems

    def copy(self, to, k):
        p, (s1, r1, s2, r2) = self.p, self.sems
        return remote(self.src.at[to, 1 - p.core], self.bufs[0].at[to], s1.at[k], r1.at[k], {"dp": p.mate()})

    def send(self, i):
        to = lax.rem(self.p.z + 1 + i, 4)
        self.copy(to, lax.rem(1 + i, 4)).start()

    def forward(self):
        p, (s1, r1, s2, r2) = self.p, self.sems
        got, mid, last = self.bufs
        self.second = {}
        for k in (1, 2, 3, 0):
            to = p.at_z(k)
            self.copy(to, k).wait_recv()
            total = self.src[to, p.core].astype(F32) + got[to].astype(F32)
            mid[to] = total.astype(BF16)
            if k:
                c = remote(mid.at[to], last.at[k - 1], s2.at[k], r2.at[k], {"dp": p.zindex(k)})
                c.start()
                self.second[k] = c

    def result(self):
        got, mid, last = self.bufs
        total = mid[self.p.z].astype(F32)
        for k in NEAR:
            self.second[k].wait_recv()
            total = total + last[k - 1].astype(F32)
        return total

    def sent(self):
        for k in range(4):
            self.copy(self.p.at_z(k), k).wait_send()

    def finish(self):
        for c in self.second.values():
            c.wait_send()


def xy_peers(p):
    return [p.peer(axis, k) for axis in (0, 1) for k in NEAR]


def dp_peers(p):
    return [{"dp": p.dpindex(k)} for k in range(1, 8)]


def shape(dims, kind):
    return jax.ShapeDtypeStruct(dims, kind)


def call(phase, inputs, outs, scratch, cid, name):
    flat, where = [], {}
    for key, entry in scratch.items():
        entries = entry if isinstance(entry, list) else [entry]
        where[key] = (len(flat), len(entries), isinstance(entry, list))
        flat += entries

    def kernel(*refs):
        named = dict(zip(list(inputs) + list(outs), refs))
        tail = refs[len(inputs) + len(outs) :]
        for key, (start, count, many) in where.items():
            named[key] = list(tail[start : start + count]) if many else tail[start]
        phase(types.SimpleNamespace(**named))

    results = pl.pallas_call(
        kernel,
        out_shape=tuple(outs.values()),
        in_specs=[pl.BlockSpec(memory_space=VM)] * len(inputs),
        out_specs=tuple(pl.BlockSpec(memory_space=VM) for _ in outs),
        scratch_shapes=flat,
        name=name,
        compiler_params=pltpu.CompilerParams(
            collective_id=cid, has_side_effects=True, vmem_limit_bytes=60 << 20
        ),
    )(*inputs.values())
    return dict(zip(outs, results))


def dot(left, right):
    return jnp.dot(left, right, preferred_element_type=F32)


def dot_tn(left, right):
    return lax.dot_general(left, right, (((0,), (0,)), ((), ())), preferred_element_type=F32)


def dot_nt(left, right):
    return lax.dot_general(left, right, (((1,), (1,)), ((), ())), preferred_element_type=F32)


def rms_scale(values):
    return lax.rsqrt(jnp.mean(values * values, axis=-1, keepdims=True) + EPSILON)


def row_vector(ref, start):
    return jnp.concatenate([ref[start + i : start + i + 1, :] for i in range(7)], axis=1)


def store_rows(ref, start, vector):
    for i in range(vector.shape[1] // 128):
        ref[start + i : start + i + 1, :] = vector[:, 128 * i : 128 * i + 128]


def build_spread(ref):
    for part in range(7):
        source = lax.broadcasted_iota(jnp.int32, (128, DPAD), 0) + 128 * part
        column = lax.broadcasted_iota(jnp.int32, (128, DPAD), 1)
        inner = column & 7
        wanted = (((column >> 3) & 7) * 16 + (column >> 6)) * 7 + inner
        ref[128 * part : 128 * part + 128, :] = jnp.where(
            (source == wanted) & (inner < 7), 1.0, 0.0
        ).astype(BF16)


def spread(values, matrix):
    return dot(values, matrix).astype(BF16)


def unspread(values, matrix):
    high = values.astype(BF16)
    low = (values - high.astype(F32)).astype(BF16)
    return dot_nt(high, matrix) + dot_nt(low, matrix)


def lanes(rows):
    return lax.broadcasted_iota(jnp.int32, (rows, 128), 1)


def half_turn(tile):
    first = (lanes(tile.shape[0]) & 63) < 32
    return jnp.where(first, pltpu.roll(tile, 96, 1), pltpu.roll(tile, 32, 1))


def rotate(tile, cosine, signed_sine):
    return tile * cosine + half_turn(tile) * signed_sine


def rotate_back(tile, cosine, signed_sine):
    return tile * cosine - half_turn(tile) * signed_sine


def scatter_heads(tile_of, dst):
    for mb in range(MB):
        for head in range(QUERY_HEADS):
            tile = tile_of(mb, head // 2)
            group = head // GROUP
            if head % 2 != group:
                tile = pltpu.roll(tile, 64, 1)
            tile = jnp.where((lanes(64) >= 64) == (group == 1), tile, 0.0)
            at = (head % 2) * 64
            dst[mb * 7 + head // 2, at : at + 64, :] = tile.astype(BF16)


def collect_heads(transposed, t):
    both = jnp.transpose(transposed)
    even, odd = both[:64], both[64:]
    even = jnp.where(t >= 4, pltpu.roll(even, 64, 1), even)
    odd = jnp.where(t <= 2, pltpu.roll(odd, 64, 1), odd)
    return jnp.where(lanes(64) < 64, even, odd)


def start_all(copies):
    for c in copies:
        c.start()
    return copies


def arrive_all(copies):
    for c in copies:
        c.wait_recv()


def sent_all(copies):
    for c in copies:
        c.wait_send()


class SmallSum:
    SCRATCH = [VM((3, 24, 128), F32), VM((3, 24, 128), F32), VM((7, 24, 128), F32), VM((2, 24, 128), F32)]
    SEMS = [DMA((3, 8)), DMA((3, 8))]

    def __init__(self, place, src, bufs, sems):
        self.p, self.src, self.bufs, self.sems = place, src, bufs, sems
        self.copies = []

    def start(self):
        p, (s, r) = self.p, self.sems
        self.x = start_all([remote(self.src, self.bufs[0].at[k - 1], s.at[0, k], r.at[0, k], p.xpeer(k)) for k in NEAR])

    def along_y(self):
        p, (s, r) = self.p, self.sems
        arrive_all(self.x)
        got, sums = self.bufs[0], self.bufs[3]
        sums[0] = self.src[...] + got[0] + got[1] + got[2]
        self.y = start_all(
            [remote(sums.at[0], self.bufs[1].at[k - 1], s.at[1, k], r.at[1, k], p.ypeer(k)) for k in NEAR]
        )

    def along_dp(self):
        p, (s, r) = self.p, self.sems
        arrive_all(self.y)
        got, sums = self.bufs[1], self.bufs[3]
        sums[1] = sums[0] + got[0] + got[1] + got[2]
        self.d = start_all(
            [
                remote(sums.at[1], self.bufs[2].at[k - 1], s.at[2, k], r.at[2, k], {"dp": p.dpindex(k)})
                for k in range(1, 8)
            ]
        )

    def result(self):
        arrive_all(self.d)
        total = self.bufs[3][1]
        for k in range(7):
            total = total + self.bufs[2][k]
        return total

    def finish(self):
        sent_all(self.x + self.y + self.d)


def front(r):
    p = Place()
    barrier(xy_peers(p) + dp_peers(p))
    attn_copies, gu_copies = [], []
    for k in range(1, 8):
        to = p.dpindex(k)
        attn_copies.append(remote(r.attn, r.attn_in.at[p.dp], r.s_attn.at[k], r.r_attn.at[k], {"dp": to}))
    start_all(attn_copies)
    small = SmallSum(p, r.small, r.small_bufs, r.small_sems)
    small.start()
    place_copies = start_all(
        [remote(r.places, r.places_x.at[p.x], r.s_place.at[0, k], r.r_place.at[0, k], p.xpeer(k)) for k in NEAR]
    )
    for k in range(1, 8):
        to = p.dpindex(k)
        gu_copies.append(remote(r.gate_up.at[to], r.gu_in.at[p.dp], r.s_gu.at[k], r.r_gu.at[k], {"dp": to}))
    start_all(gu_copies)
    cots = GatherDp(p, r.cot, r.cot_all, r.cot_sems)
    cots.start()
    r.attn_in[p.dp] = r.attn[...]
    r.gu_in[p.dp] = r.gate_up[p.dp]
    r.places_x[p.x] = r.places[...]
    build_spread(r.spread)
    arrive_all(attn_copies)
    for half in (0, 1):
        for i in range(2):
            r.attn_block[half, i] = jnp.concatenate(
                [r.attn_in[4 * i + d, half] for d in range(4)], axis=0
            ).astype(BF16)
    ring_attn = GatherCtx(p, r.attn_block.at[p.core], r.w_attn.at[p.core], r.attn_sems, r.mate_sems)
    ring_attn.start()
    small.along_y()
    arrive_all(place_copies)
    place_copies2 = start_all(
        [remote(r.places_x, r.places_all.at[p.y], r.s_place.at[1, k], r.r_place.at[1, k], p.ypeer(k)) for k in NEAR]
    )
    r.places_all[p.y] = r.places_x[...]
    ring_attn.forward()
    small.along_dp()
    arrive_all(gu_copies)
    for i in range(2):
        r.gu_block[i] = jnp.concatenate([r.gu_in[4 * i + d] for d in range(4)], axis=0).astype(BF16)
    cots.forward()
    residual = r.hidden[...].astype(F32)
    unit_in = residual * rms_scale(residual)
    arrive_all(place_copies2)
    low_lane = lanes(8) < 64
    for c in range(8):
        a, b = r.places_all[(2 * c) // 4, (2 * c) % 4], r.places_all[(2 * c + 1) // 4, (2 * c + 1) % 4]
        r.key_row[:, 128 * c : 128 * c + 128] = jnp.where(low_lane, a, b)
    for mb in range(MB):
        r.key_places[mb] = jnp.transpose(jnp.broadcast_to(r.key_row[mb : mb + 1, :], (128, 1024)))
    r.small_all[...] = small.result()
    normed = spread((unit_in * row_vector(r.small_all, 0)).astype(BF16), r.spread[...])
    r.normed_in[...] = normed
    bias_query = row_vector(r.small_all, 7)
    ring_attn.arrive()
    cosine, sine = r.cosine[...], r.sine[...]
    lin = dot(normed, r.w_attn[0].reshape(DPAD, 1024))
    query_tiles = []
    for t in range(7):
        tile = lin[:, 128 * t : 128 * t + 128] + bias_query[:, 128 * t : 128 * t + 128]
        query_tiles.append((rotate(tile, cosine, sine).astype(BF16)).astype(F32) * (HEAD_SIZE**-0.5))
    keys = rotate(lin[:, 896:] + r.small_all[21:22, :], cosine, sine).astype(BF16)
    values = dot(normed, r.w_attn[1, :, :, :, :128].reshape(DPAD, 128)) + r.small_all[22:23, :]
    values = values.astype(BF16)
    for mb in range(MB):
        r.kv[mb, :, :128] = keys[64 * mb : 64 * mb + 64]
        r.kv[mb, :, 128:] = values[64 * mb : 64 * mb + 64]
    ring_kv = GatherCtx(p, r.kv, r.kv_all, r.kv_sems)
    ring_kv.start()
    scatter_heads(lambda mb, t: query_tiles[t][64 * mb : 64 * mb + 64], r.heads)
    ring_kv.forward()
    ring_gu = GatherCtx(p, r.gu_block, r.w_gu, r.gu_sems)
    ring_gu.start()
    down_copies = start_all(
        [remote(r.down, r.down_in.at[p.x], r.s_down.at[0, k], r.r_down.at[0, k], p.xpeer(k)) for k in NEAR]
    )
    r.down_in[p.x] = r.down[...]
    ring_kv.arrive()
    for mb in range(MB):
        r.keys[mb] = r.kv_all[:, mb, :, :128].reshape(1024, 128)
        r.values[mb] = r.kv_all[:, mb, :, 128:].reshape(1024, 128)
        r.values_t[mb] = jnp.transpose(r.values[mb].astype(F32)).astype(BF16)

    def attend(mb):
        def step(t, carry):
            i = mb * 7 + t
            scores = dot_nt(r.keys[mb], r.heads[i])
            scores = jnp.where(r.key_places[mb] <= r.places[mb : mb + 1, :], scores, -1e30)
            expo = jnp.exp(scores - jnp.max(scores, axis=0, keepdims=True))
            probs = (expo * (1.0 / jnp.sum(expo, axis=0, keepdims=True))).astype(BF16)
            r.probs[i] = probs
            r.attended[i] = collect_heads(dot(r.values_t[mb], probs), t).astype(BF16)
            return carry

        lax.fori_loop(0, 7, step, 0)

    attend(0)
    ring_gu.forward()
    arrive_all(down_copies)
    r.w_down[pl.ds(pl.multiple_of(160 * p.y, 32), 160), :] = jnp.concatenate(
        [r.down_in[i] for i in range(4)], axis=0
    ).astype(BF16)
    own_down = r.w_down.at[pl.ds(pl.multiple_of(160 * p.y, 32), 160)]
    down_copies2 = start_all(
        [remote(own_down, own_down, r.s_down.at[1, k], r.r_down.at[1, k], p.ypeer(k)) for k in NEAR]
    )
    attend(1)
    attended = jnp.concatenate(
        [jnp.concatenate([r.attended[mb * 7 + t] for t in range(7)], axis=1) for mb in range(MB)], axis=0
    )
    attended_wide = spread(attended, r.spread[...])
    r.attended_wide[...] = attended_wide
    mixed = residual + dot(attended_wide, r.w_attn[1, :, :, :, 128:].reshape(DPAD, D))
    r.mixed[...] = mixed
    unit_mid = mixed * rms_scale(mixed)
    r.normed_mid[...] = spread((unit_mid * row_vector(r.small_all, 14)).astype(BF16), r.spread[...])
    ring_mid = GatherDp(p, r.normed_mid, r.normed_all, r.mid_sems)
    ring_mid.start()
    ring_gu.arrive()
    arrive_all(down_copies2)
    cots.arrive()
    ring_mid.forward()
    for ring in (ring_attn, ring_kv, ring_gu, cots, small):
        ring.finish()
    sent_all(attn_copies + gu_copies + place_copies + place_copies2 + down_copies + down_copies2)
    ring_mid.arrive()
    ring_mid.finish()


FRONT_OUTS = {
    "w_attn": shape((2, 16, 2, 32, 1024), BF16),
    "w_gu": shape((16, 2, 32, 1280), BF16),
    "w_down": shape((640, D), BF16),
    "small_all": shape((24, 128), F32),
    "cot_all": shape((8, 128, D), BF16),
    "normed_all": shape((8, 128, DPAD), BF16),
    "probs": shape((14, 1024, 128), BF16),
    "heads": shape((14, 128, 128), BF16),
    "keys": shape((2, 1024, 128), BF16),
    "values": shape((2, 1024, 128), BF16),
    "attended_wide": shape((128, DPAD), BF16),
    "normed_in": shape((128, DPAD), BF16),
    "mixed": shape((128, D), F32),
    "spread": shape((D, DPAD), BF16),
}
FRONT_SCRATCH = {
    "attn_in": VM((8, 2, 8, 1024), F32),
    "gu_in": VM((8, 8, 1280), F32),
    "down_in": VM((4, 40, D), F32),
    "places_x": VM((4, 8, 128), F32),
    "places_all": VM((4, 4, 8, 128), F32),
    "key_row": VM((8, 1024), F32),
    "key_places": VM((2, 1024, 128), F32),
    "attn_block": VM((2, 2, 32, 1024), BF16),
    "gu_block": VM((2, 32, 1280), BF16),
    "kv": VM((2, 64, 256), BF16),
    "kv_all": VM((16, 2, 64, 256), BF16),
    "values_t": VM((2, 128, 1024), BF16),
    "attended": VM((14, 64, 128), BF16),
    "normed_mid": VM((128, DPAD), BF16),
    "small_bufs": SmallSum.SCRATCH,
    "small_sems": SmallSum.SEMS,
    "s_attn": DMA((8,)), "r_attn": DMA((8,)), "s_gu": DMA((8,)), "r_gu": DMA((8,)),
    "s_place": DMA((2, 4)), "r_place": DMA((2, 4)), "s_down": DMA((2, 4)), "r_down": DMA((2, 4)),
    "attn_sems": GatherCtx.SEMS, "mate_sems": GatherCtx.MATE, "kv_sems": GatherCtx.SEMS,
    "gu_sems": GatherCtx.SEMS, "cot_sems": GatherDp.SEMS, "mid_sems": GatherDp.SEMS,
}


def back(r):
    p = Place()
    barrier(xy_peers(p) + dp_peers(p))
    red_normed = ReduceDp(p, r.part_normed, r.normed_bufs, r.normed_sems)
    red_out = ReduceDp(p, r.part_normed.at[:, :, :, pl.ds(0, D)], r.out_bufs, r.out_sems)

    def rows_of(ref, to):
        return ref[pl.ds(2 * to, 2)].reshape(256, ref.shape[-1])

    def feed(i, carry):
        to = lax.rem(p.z + 1 + i, 4)
        at = pl.ds(pl.multiple_of(256 * to, 256), 256)
        lin = dot(rows_of(r.normed_all, to), r.w_gu[...].reshape(DPAD, 1280))
        gate, up = lin[:, :640], lin[:, 640:]
        sig = 1.0 / (1.0 + jnp.exp(-gate))
        silu = gate * sig
        hidden = (silu * up).astype(BF16)
        back_hidden = dot_nt(rows_of(r.cot_all, to), r.w_down[...]).astype(BF16).astype(F32)
        grad_gate = (back_hidden * up * sig * (1.0 + gate * (1.0 - sig))).astype(BF16)
        grad_up = (back_hidden * silu).astype(BF16)
        for t in range(5):
            r.big[t, at, :] = grad_gate[:, 128 * t : 128 * t + 128]
            r.big[5 + t, at, :] = grad_up[:, 128 * t : 128 * t + 128]
            r.big[10 + t, at, :] = hidden[:, 128 * t : 128 * t + 128]
        part = dot_nt(jnp.concatenate([grad_gate, grad_up], axis=1), r.w_gu[...].reshape(DPAD, 1280))
        r.part_normed[to] = part.astype(BF16).reshape(2, 128, DPAD)
        red_normed.send(i)
        return carry

    lax.fori_loop(0, 4, feed, 0)
    red_normed.forward()

    def project(i, carry):
        to = lax.rem(p.z + 1 + i, 4)
        at = pl.ds(pl.multiple_of(256 * to, 256), 256)
        hidden = jnp.concatenate([r.big[10 + t, at, :] for t in range(5)], axis=1)
        r.part_normed[to, :, :, :D] = dot(hidden, r.w_down[...]).astype(BF16).reshape(2, 128, D)
        red_out.send(i)
        return carry

    def grad_gate_up(i, carry):
        at = pl.ds(pl.multiple_of(256 * i, 256), 256)
        left = r.normed_all[:, :, at].reshape(1024, 256)
        right = jnp.concatenate([r.big[t] for t in range(10)], axis=1)
        r.g_gu[i] = dot_tn(left, right).astype(BF16).reshape(4, 2, 32, 1280)
        return carry

    lax.fori_loop(0, 4, grad_gate_up, 0)
    ring_gu = ReduceCtx(p, r.g_gu, r.gu_bufs, r.gu_sems)
    ring_gu.start()

    def grad_down(t, carry):
        at = pl.ds(pl.multiple_of(128 * t, 128), 128)
        r.g_down[at, :] = dot_tn(r.big[10 + t], r.cot_all[...].reshape(1024, D)).astype(BF16)
        return carry

    lax.fori_loop(0, 5, grad_down, 0)
    down_copies = start_all(
        [
            remote(
                r.g_down.at[pl.ds(pl.multiple_of(160 * p.at_y(k), 32), 160)],
                r.down_y.at[k - 1], r.s_down.at[0, k], r.r_down.at[0, k], p.ypeer(k),
            )
            for k in NEAR
        ]
    )
    red_normed.sent()
    lax.fori_loop(0, 4, project, 0)
    gain_mlp = row_vector(r.small_all, 14)
    mixed = r.mixed[...]
    inv_mid = rms_scale(mixed)
    unit_mid = mixed * inv_mid
    r.held[...] = unspread(red_normed.result(), r.spread[...])
    grad_normed = r.held[...]
    store_rows(r.small_grads, 14, jnp.sum(grad_normed * unit_mid, axis=0, keepdims=True))
    scaled = grad_normed * gain_mlp
    grad_mixed = r.cot[...].astype(F32) + inv_mid * (
        scaled - unit_mid * jnp.mean(scaled * unit_mid, axis=-1, keepdims=True)
    )
    r.grad_mixed[...] = grad_mixed
    grad_branch = grad_mixed.astype(BF16)
    wide = dot_nt(grad_branch, r.w_attn[1, :, :, :, 128:].reshape(DPAD, D)).astype(BF16)
    grad_attended = dot_nt(wide, r.spread[...])
    scatter_heads(
        lambda mb, t: grad_attended[64 * mb : 64 * mb + 64, 128 * t : 128 * t + 128], r.grad_heads
    )
    for mb in range(MB):
        r.keys_t[mb] = jnp.transpose(r.keys[mb].astype(F32)).astype(BF16)
    red_out.forward()

    def attend_back(mb):
        def step(t, carry):
            i = mb * 7 + t
            grad_probs = dot_nt(r.values[mb], r.grad_heads[i])
            probs = r.probs[i].astype(F32)
            weighted = probs * grad_probs
            inner = jnp.sum(weighted, axis=0, keepdims=True)
            grad_scores = (weighted - probs * inner).astype(BF16)
            r.big[i] = grad_scores
            r.grad_query[i] = collect_heads(dot(r.keys_t[mb], grad_scores), t)
            return carry

        lax.fori_loop(0, 7, step, 0)

    def grad_key_value(i, carry):
        mb, y = i // 4, lax.rem(i, 4)
        at = pl.ds(pl.multiple_of(256 * y, 256), 256)
        scores = jnp.concatenate([r.big[mb * 7 + t, at, :] for t in range(7)], axis=1)
        probs = jnp.concatenate([r.probs[mb * 7 + t, at, :] for t in range(7)], axis=1)
        grad_keys = dot(scores, r.heads[pl.ds(7 * mb, 7)].reshape(896, 128))
        grad_values = dot(probs, r.grad_heads[pl.ds(7 * mb, 7)].reshape(896, 128))
        r.g_kv[y, :, mb, :, :128] = grad_keys.astype(BF16).reshape(4, 64, 128)
        r.g_kv[y, :, mb, :, 128:] = grad_values.astype(BF16).reshape(4, 64, 128)
        return carry

    attend_back(0)
    attend_back(1)
    lax.fori_loop(0, 8, grad_key_value, 0)
    ring_kv = ReduceCtx(p, r.g_kv, r.kv_bufs, r.kv_sems)
    ring_kv.start()
    cosine, sine = r.cosine[...], r.sine[...]
    tiles = []
    for t in range(7):
        tile = jnp.concatenate([r.grad_query[t], r.grad_query[7 + t]], axis=0) * (HEAD_SIZE**-0.5)
        tiles.append(rotate_back(tile, cosine, sine).astype(BF16))
    grad_query = jnp.concatenate(tiles, axis=1)
    store_rows(r.small_grads, 7, jnp.sum(grad_query.astype(F32), axis=0, keepdims=True))
    ring_kv.forward()
    r.low_a[...] = grad_query
    r.low_b[...] = grad_branch

    def grad_query_output(y, carry):
        at = pl.ds(pl.multiple_of(256 * y, 256), 256)
        part = dot_tn(r.normed_in[:, at], r.low_a[...])
        r.g_attn[0, y, :, :, :, :896] = part.astype(BF16).reshape(4, 2, 32, 896)
        part = dot_tn(r.attended_wide[:, at], r.low_b[...])
        r.g_attn[1, y, :, :, :, 128:] = part.astype(BF16).reshape(4, 2, 32, D)
        return carry

    lax.fori_loop(0, 4, grad_query_output, 0)
    kv_sum = jnp.concatenate([ring_kv.result(0), ring_kv.result(1)], axis=0)
    grad_key = rotate_back(kv_sum[:, :128], cosine, sine).astype(BF16)
    grad_value = kv_sum[:, 128:].astype(BF16)
    for y in range(4):
        left = r.normed_in[:, 256 * y : 256 * y + 256]
        part = dot_tn(left, jnp.concatenate([grad_key, grad_value], axis=1)).astype(BF16)
        r.g_attn[0, y, :, :, :, 896:] = part[:, :128].reshape(4, 2, 32, 128)
        r.g_attn[1, y, :, :, :, :128] = part[:, 128:].reshape(4, 2, 32, 128)
    mate_copies = start_all(
        [
            remote(r.g_attn.at[1 - p.core, y], r.mate_in.at[y], r.s_mate.at[y], r.r_mate.at[y], {"dp": p.mate()})
            for y in range(4)
        ]
    )
    store_rows(r.small_grads, 21, jnp.sum(grad_key.astype(F32), axis=0, keepdims=True))
    store_rows(r.small_grads, 22, jnp.sum(grad_value.astype(F32), axis=0, keepdims=True))
    r.small_grads[23:24, :] = jnp.zeros((1, 128), F32)
    grad_normed_wide = dot_nt(
        jnp.concatenate([grad_query, grad_key], axis=1), r.w_attn[0].reshape(DPAD, 1024)
    ) + dot_nt(grad_value, r.w_attn[1, :, :, :, :128].reshape(DPAD, 128))
    grad_normed_in = unspread(grad_normed_wide, r.spread[...])
    residual = r.hidden[...].astype(F32)
    inv_rms = rms_scale(residual)
    unit_in = residual * inv_rms
    store_rows(r.small_grads, 0, jnp.sum(grad_normed_in * unit_in, axis=0, keepdims=True))
    small = SmallSum(p, r.small_grads, r.small_bufs, r.small_sems)
    small.start()
    for y in range(4):
        mate_copies[y].wait_recv()
        r.mate_in[y] = (r.g_attn[p.core, y].astype(F32) + r.mate_in[y].astype(F32)).astype(BF16)
    ring_attn = ReduceCtx(p, r.mate_in, r.attn_bufs, r.attn_sems)
    ring_attn.start()
    scaled = grad_normed_in * row_vector(r.small_all, 0)
    r.grad_in[...] = r.grad_mixed[...] + inv_rms * (
        scaled - unit_in * jnp.mean(scaled * unit_in, axis=-1, keepdims=True)
    )
    r.layer_out[...] = (mixed + red_out.result()).astype(BF16)
    ring_gu.forward()
    arrive_all(down_copies)
    total = r.g_down[pl.ds(pl.multiple_of(160 * p.y, 32), 160), :].astype(F32)
    for k in NEAR:
        total = total + r.down_y[k - 1].astype(F32)
    for i in range(4):
        r.down_mid[i] = total[40 * i : 40 * i + 40]
    down_copies2 = start_all(
        [
            remote(r.down_mid.at[p.at_x(k)], r.down_x.at[k - 1], r.s_down.at[1, k], r.r_down.at[1, k], p.xpeer(k))
            for k in NEAR
        ]
    )
    small.along_y()
    ring_attn.forward()
    small.along_dp()
    for h in (0, 1):
        part = ring_gu.result(h)
        for d in range(4):
            r.gu_out[4 * h + d] = part[8 * d : 8 * d + 8]
    out_copies = []
    for k in range(1, 8):
        to = p.dpindex(k)
        out_copies.append(remote(r.gu_out.at[to], r.o_gu.at[p.dp], r.s_gu.at[k], r.r_gu.at[k], {"dp": to}))
    start_all(out_copies)
    r.o_gu[p.dp] = r.gu_out[p.dp]
    arrive_all(down_copies2)
    r.o_down[...] = r.down_mid[p.x] + r.down_x[0] + r.down_x[1] + r.down_x[2]
    for h in (0, 1):
        part = ring_attn.result(h)
        for d in range(4):
            r.attn_out[4 * h + d] = part[8 * d : 8 * d + 8]
    attn_copies = []
    for k in range(1, 8):
        to = p.dpindex(k)
        attn_copies.append(
            remote(r.attn_out.at[to], r.attn_dp.at[p.z, p.core], r.s_attn.at[k], r.r_attn.at[k], {"dp": to})
        )
    start_all(attn_copies)
    r.attn_dp[p.z, p.core] = r.attn_out[p.dp]
    r.o_small[...] = small.result()
    arrive_all(out_copies + attn_copies)
    for half in (0, 1):
        r.o_attn[half] = r.attn_dp[0, half] + r.attn_dp[1, half] + r.attn_dp[2, half] + r.attn_dp[3, half]
    red_out.sent()
    for ring in (red_normed, red_out, ring_gu, ring_kv, ring_attn, small):
        ring.finish()
    sent_all(mate_copies + down_copies + down_copies2 + out_copies + attn_copies)


BACK_OUTS = {
    "layer_out": shape((128, D), BF16),
    "grad_in": shape((128, D), F32),
    "o_attn": shape((2, 8, 1024), F32),
    "o_gu": shape((8, 8, 1280), F32),
    "o_down": shape((40, D), F32),
    "o_small": shape((24, 128), F32),
}
BACK_SCRATCH = {
    "big": VM((15, 1024, 128), BF16),
    "part_normed": VM((4, 2, 128, DPAD), BF16),
    "normed_bufs": ReduceDp.scratch(128, DPAD), "normed_sems": ReduceDp.SEMS,
    "out_bufs": ReduceDp.scratch(128, D), "out_sems": ReduceDp.SEMS,
    "g_gu": VM((4, 4, 2, 32, 1280), BF16),
    "gu_bufs": ReduceCtx.scratch(32, 1280), "gu_sems": ReduceCtx.SEMS,
    "g_down": VM((640, D), BF16),
    "down_y": VM((3, 160, D), BF16), "down_mid": VM((4, 40, D), F32), "down_x": VM((3, 40, D), F32),
    "grad_mixed": VM((128, D), F32),
    "held": VM((128, D), F32),
    "low_a": VM((128, D), BF16),
    "low_b": VM((128, D), BF16),
    "grad_heads": VM((14, 128, 128), BF16),
    "keys_t": VM((2, 128, 1024), BF16),
    "grad_query": VM((14, 64, 128), F32),
    "g_kv": VM((4, 4, 2, 64, 256), BF16),
    "kv_bufs": ReduceCtx.scratch(64, 256), "kv_sems": ReduceCtx.SEMS,
    "g_attn": VM((2, 4, 4, 2, 32, 1024), BF16),
    "mate_in": VM((4, 4, 2, 32, 1024), BF16),
    "attn_bufs": ReduceCtx.scratch(32, 1024), "attn_sems": ReduceCtx.SEMS,
    "small_grads": VM((24, 128), F32),
    "small_bufs": SmallSum.SCRATCH, "small_sems": SmallSum.SEMS,
    "gu_out": VM((8, 8, 1280), F32), "attn_out": VM((8, 8, 1024), F32), "attn_dp": VM((4, 2, 8, 1024), F32),
    "s_mate": DMA((4,)), "r_mate": DMA((4,)), "s_down": DMA((2, 4)), "r_down": DMA((2, 4)),
    "s_gu": DMA((8,)), "r_gu": DMA((8,)), "s_attn": DMA((8,)), "r_attn": DMA((8,)),
}


def body(
    hidden_in, positions, norm_attn, w_query, b_query, w_key, b_key, value_weight, value_bias, w_output,
    norm_mlp, w_gate, w_up, w_down, cotangent,
):
    rows = MB * 64
    me = lax.axis_index("dp") * 16 + lax.axis_index("ctx")
    places = positions[:, 0]
    attn = jnp.pad(
        jnp.stack(
            [jnp.concatenate([w_query, w_key], axis=1), jnp.concatenate([value_weight, w_output], axis=1)]
        ).astype(F32),
        ((0, 0), (0, 1), (0, 0)),
    )

    def slices(w):
        parts = w.astype(F32).reshape(7, 8, 16, 38)
        return jnp.pad(parts, ((0, 1), (0, 0), (0, 0), (0, 2))).transpose(1, 0, 2, 3).reshape(8, 8, 640)

    def put(vector, width):
        full = jnp.zeros((128, width), F32)
        return lax.dynamic_update_slice(full, vector.astype(F32)[None], (me, 0)).reshape(-1)

    small = jnp.concatenate(
        [put(norm_attn, 7), put(b_query, 7), put(norm_mlp, 7), put(b_key, 1), put(value_bias, 1), jnp.zeros((128,), F32)]
    ).reshape(24, 128)
    freqs = THETA_BASE ** (-jnp.arange(0, HEAD_SIZE, 2).astype(F32) / HEAD_SIZE)
    angles = places.reshape(rows).astype(F32)[:, None] * jnp.tile(freqs, 4)[None, :]
    sign = jnp.tile(jnp.repeat(jnp.array([-1.0, 1.0], F32), HEAD_SIZE // 2), 2)
    own = {
        "hidden": hidden_in.reshape(rows, D),
        "cot": cotangent.reshape(rows, D),
        "cosine": jnp.cos(angles),
        "sine": jnp.sin(angles) * sign,
    }
    sent = {
        "attn": attn,
        "gate_up": jnp.concatenate([slices(w_gate), slices(w_up)], axis=-1),
        "down": jnp.pad(w_down.astype(F32), ((0, 2), (0, 0))),
        "small": small,
        "places": jnp.pad(jnp.tile(places.astype(F32), (1, 2)), ((0, 6), (0, 0))),
    }
    kept = call(front, {**own, **sent}, FRONT_OUTS, FRONT_SCRATCH, 0, "front")
    done = call(back, {**own, **kept}, BACK_OUTS, BACK_SCRATCH, 1, "back")
    o_attn, o_gu = done["o_attn"], done["o_gu"]

    def joined(parts):
        return parts[:, :7].reshape(8, 7, 16, 40)[..., :38].transpose(1, 0, 2, 3).reshape(7, 4864)

    sums = done["o_small"].reshape(-1)

    def take(start, width):
        return lax.dynamic_slice(sums, (start + me * width,), (width,))

    return (
        done["layer_out"].reshape(MB, 1, 64, D),
        done["grad_in"].reshape(MB, 1, 64, D),
        take(0, 7),
        o_attn[0, :7, :896],
        take(896, 7),
        o_attn[0, :7, 896:],
        sums[2688:2816],
        o_attn[1, :7, :128],
        take(2816, 1),
        o_attn[1, :7, 128:],
        take(1792, 7),
        joined(o_gu[..., :640]),
        joined(o_gu[..., 640:]),
        done["o_down"][:38],
    )


def solution(mesh):
    rows = P(("dp", "ctx"), None)
    vector = P(("dp", "ctx"))
    tokens = P(None, "dp", "ctx", None)
    in_specs = (
        tokens, P(None, "dp", "ctx"), vector, rows, vector, rows, vector, rows, vector, rows, vector,
        rows, rows, rows, tokens,
    )
    out_specs = (
        tokens, tokens, vector, rows, vector, rows, P(), rows, vector, rows, vector, rows, rows, rows,
    )
    return jax.shard_map(body, mesh=mesh, in_specs=in_specs, out_specs=out_specs, check_vma=False)
```

```python
import types

import jax
import jax.numpy as jnp
from jax import lax
from jax.experimental import pallas as pl
from jax.experimental.pallas import tpu as pltpu
from jax.sharding import PartitionSpec as P

QUERY_HEADS = 14
KEY_VALUE_HEADS = 2
HEAD_SIZE = 64
GROUP = QUERY_HEADS // KEY_VALUE_HEADS
MB = 2
D = 896
DPAD = 1024
EPSILON = 1e-06
THETA_BASE = 1000000.0
F32 = jnp.float32
BF16 = jnp.bfloat16
MESH = pl.DeviceIdType.MESH
DMA = pltpu.SemaphoreType.DMA
VM = pltpu.VMEM


def remote(src, dst, ss, rs, peer):
    return pltpu.make_async_remote_copy(
        src_ref=src, dst_ref=dst, send_sem=ss, recv_sem=rs, device_id=peer, device_id_type=MESH
    )


def barrier(peers):
    sem = pltpu.get_barrier_semaphore()
    for peer in peers:
        pl.semaphore_signal(sem, inc=1, device_id=peer, device_id_type=MESH)
    pl.semaphore_wait(sem, len(peers))


class Place:
    def __init__(self):
        self.dp = lax.axis_index("dp")
        self.ctx = lax.axis_index("ctx")
        self.y, self.x = self.ctx // 4, lax.rem(self.ctx, 4)
        self.z, self.core = self.dp // 2, lax.rem(self.dp, 2)

    def at_x(self, k):
        return lax.rem(self.x + (k + 4), 4)

    def at_y(self, k):
        return lax.rem(self.y + (k + 4), 4)

    def at_z(self, k):
        return lax.rem(self.z + (k + 4), 4)

    def line(self, axis, k):
        return self.y * 4 + self.at_x(k) if axis == 0 else self.at_y(k) * 4 + self.x

    def xpeer(self, k):
        return {"ctx": self.line(0, k)}

    def ypeer(self, k):
        return {"ctx": self.line(1, k)}

    def peer(self, axis, k):
        return {"ctx": self.line(axis, k)}

    def zindex(self, k):
        return self.at_z(k) * 2 + self.core

    def mate(self):
        return self.z * 2 + 1 - self.core

    def dpindex(self, k):
        return lax.rem(self.dp + k, 8)


NEAR = (1, 3, 2)


class GatherCtx:
    SEMS = [DMA((2, 4)), DMA((2, 4)), DMA((2, 4, 4)), DMA((2, 4, 4)), DMA((2,))]
    MATE = [DMA((2, 4, 4)), DMA((2, 4, 4))]

    def __init__(self, place, src, dst_at, sems, mate=None):
        self.p, self.src, self.dst_at, self.sems, self.mate = place, src, dst_at, sems, mate
        self.mated = []

    def block(self, h, j, k):
        p = self.p
        return p.at_y(-k) * 4 + p.at_x(-j) if h == 0 else p.at_y(-j) * 4 + p.at_x(-k)

    def share(self, h, j, k):
        if self.mate is None:
            return
        dst = self.dst_at(self.block(h, j, k), h)
        src = self.src.at[h] if j == 0 and k == 0 else dst
        c = remote(src, dst, self.mate[0].at[h, j, k], self.mate[1].at[h, j, k], {"dp": self.p.mate()})
        c.start()
        self.mated.append(c)

    def start(self):
        p, (s1, r1, s2, r2, ls) = self.p, self.sems
        self.local = []
        for h in (0, 1):
            c = pltpu.make_async_copy(self.src.at[h], self.dst_at(p.ctx, h), ls.at[h])
            c.start()
            self.local.append(c)
        self.first = {}
        for k in NEAR:
            for h in (0, 1):
                c = remote(self.src.at[h], self.dst_at(p.ctx, h), s1.at[h, k], r1.at[h, k], p.peer(h, k))
                c.start()
                self.first[h, k] = c
        for h in (0, 1):
            self.share(h, 0, 0)

    def forward(self):
        p, (s1, r1, s2, r2, ls) = self.p, self.sems
        self.second = {}
        for j in (0,) + NEAR:
            for h in (0, 1):
                if j:
                    self.first[h, j].wait_recv()
                dst = self.dst_at(p.line(h, -j), h)
                src = self.src.at[h] if j == 0 else dst
                for k in NEAR:
                    c = remote(src, dst, s2.at[h, j, k], r2.at[h, j, k], p.peer(1 - h, k))
                    c.start()
                    self.second[h, j, k] = c
                if j:
                    self.share(h, j, 0)

    def arrive(self):
        for c in self.local:
            c.wait()
        for (h, j, k), c in self.second.items():
            c.wait_recv()
            self.share(h, j, k)
        for c in self.mated:
            c.wait_recv()

    def finish(self):
        for c in list(self.first.values()) + list(self.second.values()) + self.mated:
            c.wait_send()


class ReduceCtx:
    SEMS = [DMA((2, 4)), DMA((2, 4)), DMA((2, 4)), DMA((2, 4))]

    @staticmethod
    def scratch(rows, cols):
        return [VM((2, 3, 4, rows, cols), BF16), VM((2, 3, rows, cols), BF16)]

    def __init__(self, place, src_at, bufs, sems):
        self.p, self.src_at, self.bufs, self.sems = place, src_at, bufs, sems

    def start(self):
        p, (s1, r1, s2, r2) = self.p, self.sems
        got = self.bufs[0]
        every = slice(None)
        self.first = {}
        for k in NEAR:
            for h in (0, 1):
                src = self.src_at(0, p.at_y(k), every) if h == 0 else self.src_at(1, every, p.at_x(k))
                c = remote(src, got.at[h, k - 1], s1.at[h, k], r1.at[h, k], p.peer(1 - h, k))
                c.start()
                self.first[h, k] = c

    def forward(self):
        p, (s1, r1, s2, r2) = self.p, self.sems
        got, last = self.bufs
        self.second = {}
        for h in (0, 1):
            for k in NEAR:
                self.first[h, k].wait_recv()
            for i in range(4):
                own = self.src_at(0, p.y, i) if h == 0 else self.src_at(1, i, p.x)
                total = own[...].astype(F32)
                for k in NEAR:
                    total = total + got[h, k - 1, i].astype(F32)
                got[h, 0, i] = total.astype(BF16)
            for k in NEAR:
                to = p.at_x(k) if h == 0 else p.at_y(k)
                c = remote(got.at[h, 0, to], last.at[h, k - 1], s2.at[h, k], r2.at[h, k], p.peer(h, k))
                c.start()
                self.second[h, k] = c

    def result(self, h):
        p = self.p
        got, last = self.bufs
        for k in NEAR:
            self.second[h, k].wait_recv()
        total = got[h, 0, p.x if h == 0 else p.y].astype(F32)
        for k in NEAR:
            total = total + last[h, k - 1].astype(F32)
        return total

    def finish(self):
        for c in list(self.first.values()) + list(self.second.values()):
            c.wait_send()


class GatherDp:
    SEMS = [DMA((4,)), DMA((4,)), DMA((4,)), DMA((4,)), DMA]

    def __init__(self, place, src, dst, sems):
        self.p, self.src, self.dst, self.sems = place, src, dst, sems

    def start(self):
        p, (s1, r1, s2, r2, ls) = self.p, self.sems
        self.local = pltpu.make_async_copy(self.src, self.dst.at[p.dp], ls)
        self.local.start()
        self.first = {}
        for k in NEAR:
            c = remote(self.src, self.dst.at[p.dp], s1.at[k], r1.at[k], {"dp": p.zindex(k)})
            c.start()
            self.first[k] = c

    def forward(self):
        p, (s1, r1, s2, r2, ls) = self.p, self.sems
        self.second = []
        for j in (0,) + NEAR:
            if j:
                self.first[j].wait_recv()
            block = p.zindex(-j)
            src = self.src if j == 0 else self.dst.at[block]
            c = remote(src, self.dst.at[block], s2.at[j], r2.at[j], {"dp": p.mate()})
            c.start()
            self.second.append(c)

    def arrive(self):
        self.local.wait()
        for c in self.second:
            c.wait_recv()

    def finish(self):
        for c in list(self.first.values()) + self.second:
            c.wait_send()


class ReduceDp:
    SEMS = [DMA((4,)), DMA((4,)), DMA((4,)), DMA((4,))]

    @staticmethod
    def scratch(rows, cols):
        return [VM((4, rows, cols), BF16), VM((3, rows, cols), BF16)]

    def __init__(self, place, src, bufs, sems):
        self.p, self.src, self.bufs, self.sems = place, src, bufs, sems

    def copy(self, to, k):
        p, (s1, r1, s2, r2) = self.p, self.sems
        return remote(self.src.at[to, 1 - p.core], self.bufs[0].at[to], s1.at[k], r1.at[k], {"dp": p.mate()})

    def send(self, i):
        to = lax.rem(self.p.z + 1 + i, 4)
        self.copy(to, lax.rem(1 + i, 4)).start()

    def forward(self):
        p, (s1, r1, s2, r2) = self.p, self.sems
        got, last = self.bufs
        self.second = {}
        for k in (1, 2, 3, 0):
            to = p.at_z(k)
            self.copy(to, k).wait_recv()
            total = self.src[to, p.core].astype(F32) + got[to].astype(F32)
            got[to] = total.astype(BF16)
            if k:
                c = remote(got.at[to], last.at[k - 1], s2.at[k], r2.at[k], {"dp": p.zindex(k)})
                c.start()
                self.second[k] = c

    def result(self):
        got, last = self.bufs
        total = got[self.p.z].astype(F32)
        for k in NEAR:
            self.second[k].wait_recv()
            total = total + last[k - 1].astype(F32)
        return total

    def sent(self):
        for k in range(4):
            self.copy(self.p.at_z(k), k).wait_send()

    def finish(self):
        for c in self.second.values():
            c.wait_send()


def xy_peers(p):
    return [p.peer(axis, k) for axis in (0, 1) for k in NEAR]


def dp_peers(p):
    return [{"dp": p.dpindex(k)} for k in range(1, 8)]


def shape(dims, kind):
    return jax.ShapeDtypeStruct(dims, kind)


def call(phase, inputs, outs, scratch, cid, name):
    flat, where = [], {}
    for key, entry in scratch.items():
        entries = entry if isinstance(entry, list) else [entry]
        where[key] = (len(flat), len(entries), isinstance(entry, list))
        flat += entries

    def kernel(*refs):
        named = dict(zip(list(inputs) + list(outs), refs))
        tail = refs[len(inputs) + len(outs) :]
        for key, (start, count, many) in where.items():
            named[key] = list(tail[start : start + count]) if many else tail[start]
        phase(types.SimpleNamespace(**named))

    results = pl.pallas_call(
        kernel,
        out_shape=tuple(outs.values()),
        in_specs=[pl.BlockSpec(memory_space=VM)] * len(inputs),
        out_specs=tuple(pl.BlockSpec(memory_space=VM) for _ in outs),
        scratch_shapes=flat,
        name=name,
        compiler_params=pltpu.CompilerParams(
            collective_id=cid, has_side_effects=True, vmem_limit_bytes=63 << 20
        ),
    )(*inputs.values())
    return dict(zip(outs, results))


def dot(left, right):
    return jnp.dot(left, right, preferred_element_type=F32)


def dot_tn(left, right):
    return lax.dot_general(left, right, (((0,), (0,)), ((), ())), preferred_element_type=F32)


def dot_nt(left, right):
    return lax.dot_general(left, right, (((1,), (1,)), ((), ())), preferred_element_type=F32)


def rms_scale(values):
    return lax.rsqrt(jnp.mean(values * values, axis=-1, keepdims=True) + EPSILON)


def row_vector(ref, start):
    return jnp.concatenate([ref[start + i : start + i + 1, :] for i in range(7)], axis=1)


def store_rows(ref, start, vector):
    for i in range(vector.shape[1] // 128):
        ref[start + i : start + i + 1, :] = vector[:, 128 * i : 128 * i + 128]


def build_spread(ref):
    for part in range(7):
        source = lax.broadcasted_iota(jnp.int32, (128, DPAD), 0) + 128 * part
        column = lax.broadcasted_iota(jnp.int32, (128, DPAD), 1)
        inner = column & 7
        owner = ((column >> 3) & 3) * 2 + (column >> 9)
        wanted = (owner * 16 + ((column >> 5) & 15)) * 7 + inner
        ref[128 * part : 128 * part + 128, :] = jnp.where(
            (source == wanted) & (inner < 7), 1.0, 0.0
        ).astype(BF16)


def spread(values, matrix):
    return dot(values, matrix).astype(BF16)


def unspread(values, matrix):
    high = values.astype(BF16)
    low = (values - high.astype(F32)).astype(BF16)
    return dot_nt(high, matrix) + dot_nt(low, matrix)


def lanes(rows):
    return lax.broadcasted_iota(jnp.int32, (rows, 128), 1)


def half_turn(tile):
    first = (lanes(tile.shape[0]) & 63) < 32
    return jnp.where(first, pltpu.roll(tile, 96, 1), pltpu.roll(tile, 32, 1))


def rotate(tile, cosine, signed_sine):
    return tile * cosine + half_turn(tile) * signed_sine


def rotate_back(tile, cosine, signed_sine):
    return tile * cosine - half_turn(tile) * signed_sine


def scatter_heads(tile_of, dst):
    for mb in range(MB):
        for head in range(QUERY_HEADS):
            tile = tile_of(mb, head // 2)
            group = head // GROUP
            if head % 2 != group:
                tile = pltpu.roll(tile, 64, 1)
            tile = jnp.where((lanes(64) >= 64) == (group == 1), tile, 0.0)
            at = (head % 2) * 64
            dst[mb * 7 + head // 2, at : at + 64, :] = tile.astype(BF16)


def collect_heads(transposed, t):
    both = jnp.transpose(transposed)
    even, odd = both[:64], both[64:]
    even = jnp.where(t >= 4, pltpu.roll(even, 64, 1), even)
    odd = jnp.where(t <= 2, pltpu.roll(odd, 64, 1), odd)
    return jnp.where(lanes(64) < 64, even, odd)


def start_all(copies):
    for c in copies:
        c.start()
    return copies


def arrive_all(copies):
    for c in copies:
        c.wait_recv()


def sent_all(copies):
    for c in copies:
        c.wait_send()


class SmallSum:
    SCRATCH = [VM((3, 24, 128), F32), VM((3, 24, 128), F32), VM((7, 24, 128), F32), VM((2, 24, 128), F32)]
    SEMS = [DMA((3, 8)), DMA((3, 8))]

    def __init__(self, place, src, bufs, sems):
        self.p, self.src, self.bufs, self.sems = place, src, bufs, sems
        self.copies = []

    def start(self):
        p, (s, r) = self.p, self.sems
        self.x = start_all([remote(self.src, self.bufs[0].at[k - 1], s.at[0, k], r.at[0, k], p.xpeer(k)) for k in NEAR])

    def along_y(self):
        p, (s, r) = self.p, self.sems
        arrive_all(self.x)
        got, sums = self.bufs[0], self.bufs[3]
        sums[0] = self.src[...] + got[0] + got[1] + got[2]
        self.y = start_all(
            [remote(sums.at[0], self.bufs[1].at[k - 1], s.at[1, k], r.at[1, k], p.ypeer(k)) for k in NEAR]
        )

    def along_dp(self):
        p, (s, r) = self.p, self.sems
        arrive_all(self.y)
        got, sums = self.bufs[1], self.bufs[3]
        sums[1] = sums[0] + got[0] + got[1] + got[2]
        self.d = start_all(
            [
                remote(sums.at[1], self.bufs[2].at[k - 1], s.at[2, k], r.at[2, k], {"dp": p.dpindex(k)})
                for k in range(1, 8)
            ]
        )

    def result(self):
        arrive_all(self.d)
        total = self.bufs[3][1]
        for k in range(7):
            total = total + self.bufs[2][k]
        return total

    def finish(self):
        sent_all(self.x + self.y + self.d)


class ZSum:
    SEMS = [DMA((4,)), DMA((4,))]

    @staticmethod
    def scratch(cols):
        return [VM((4, 8, cols), F32), VM((4, 8, cols), F32)]

    def __init__(self, place, ring, bufs, sems):
        self.p, self.ring, self.bufs, self.sems = place, ring, bufs, sems

    def start(self):
        p, (s, r), (out, got) = self.p, self.sems, self.bufs
        for h in (0, 1):
            part = self.ring.result(h)
            out[2 * h], out[2 * h + 1] = part[:8], part[8:]
        self.copies = start_all(
            [remote(out.at[p.at_z(k)], got.at[p.z], s.at[k], r.at[k], {"dp": p.zindex(k)}) for k in NEAR]
        )
        got[p.z] = out[p.z]

    def result(self):
        arrive_all(self.copies)
        got = self.bufs[1]
        return got[0] + got[1] + got[2] + got[3]

    def finish(self):
        sent_all(self.copies)


def build_columns(big):
    for t in range(5):
        column = lax.broadcasted_iota(jnp.int32, (640, 128), 1) + 128 * t
        source = lax.broadcasted_iota(jnp.int32, (640, 128), 0)
        owner = (column * 1639) >> 16
        inner = column - owner * 40
        big[t, :640, :] = jnp.where((source == owner * 38 + inner) & (inner < 38), 1.0, 0.0).astype(BF16)


def columns_of(big):
    return jnp.concatenate([big[t, :640, :] for t in range(5)], axis=1)


def front(r, p):
    r.attn_src[...] = jnp.zeros_like(r.attn_src)
    r.stage[...] = jnp.zeros_like(r.stage)
    r.down[...] = jnp.zeros_like(r.down)
    r.down[:38, :] = r.w_down_own[...].astype(F32)
    r.attn_src[:7, :896] = r.w_query[...].astype(F32)
    r.attn_src[:7, 896:1024] = r.w_key[...].astype(F32)
    r.attn_src[:7, 1024:1152] = r.w_value[...].astype(F32)
    r.attn_src[:7, 1152:] = r.w_output[...].astype(F32)
    r.small[...] = jnp.zeros_like(r.small)
    me = p.dp * 16 + p.ctx
    flat = lax.broadcasted_iota(jnp.int32, (7, 128), 0) * 128 + lax.broadcasted_iota(jnp.int32, (7, 128), 1)
    for n in range(3):
        total = jnp.zeros((7, 128), F32)
        for i in range(7):
            value = r.vectors[0:1, 7 * n + i : 7 * n + i + 1]
            total = total + jnp.where(flat == me * 7 + i, value, 0.0)
        r.small[7 * n : 7 * n + 7, :] = total
    for n in range(2):
        value = r.vectors[0:1, 21 + n : 22 + n]
        r.small[21 + n : 22 + n, :] = jnp.where(flat[:1] == me, value, 0.0)
    barrier(xy_peers(p) + dp_peers(p))
    attn_copies = start_all(
        [remote(r.attn_src, r.attn_in.at[p.z], r.s_attn.at[k], r.r_attn.at[k], {"dp": p.zindex(k)}) for k in NEAR]
    )
    small = SmallSum(p, r.small, r.small_bufs, r.small_sems)
    small.start()
    place_copies = start_all(
        [remote(r.places, r.places_x.at[p.x], r.s_place.at[0, k], r.r_place.at[0, k], p.xpeer(k)) for k in NEAR]
    )
    r.attn_in[p.z] = r.attn_src[...]
    r.places_x[p.x] = r.places[...]
    build_columns(r.big)
    for n, ref in enumerate((r.w_gate, r.w_up)):
        whole = ref[...].astype(F32)
        for d in range(8):
            r.stage[8 * d : 8 * d + 7, :608] = whole[:, 608 * d : 608 * d + 608]
        wide = dot(r.stage[...].astype(BF16), columns_of(r.big))
        for d in range(8):
            r.gate_up[d, :, 640 * n : 640 * n + 640] = wide[8 * d : 8 * d + 8]
    gu_copies = []
    for k in range(1, 8):
        to = p.dpindex(k)
        gu_copies.append(
            remote(r.gate_up.at[to], r.gu_in.at[p.core, p.z], r.s_gu.at[k], r.r_gu.at[k], {"dp": to})
        )
    start_all(gu_copies)
    r.gu_in[p.core, p.z] = r.gate_up[p.dp]
    cots = GatherDp(p, r.cot, r.cot_all, r.cot_sems)
    cots.start()
    arrive_all(attn_copies)
    for h in (0, 1):
        pair = jnp.concatenate([r.attn_in[2 * h], r.attn_in[2 * h + 1]], axis=0).astype(BF16)
        r.qkv_block[h] = pair[:, :1152]
        r.o_block[h] = pair[:, 1152:]
    ring_qkv = GatherCtx(p, r.qkv_block, lambda b, h: r.w_qkv.at[p.core, b, h], r.qkv_sems, r.qkv_mate)
    ring_qkv.start()
    build_spread(r.spread)
    small.along_y()
    arrive_all(place_copies)
    place_copies2 = start_all(
        [remote(r.places_x, r.places_all.at[p.y], r.s_place.at[1, k], r.r_place.at[1, k], p.ypeer(k)) for k in NEAR]
    )
    r.places_all[p.y] = r.places_x[...]
    ring_qkv.forward()
    ring_o = GatherCtx(p, r.o_block, lambda b, h: r.w_o.at[p.core, b, h], r.o_sems, r.o_mate)
    ring_o.start()
    small.along_dp()
    arrive_all(gu_copies)
    for c in (0, 1):
        r.gu_block[c] = jnp.concatenate([r.gu_in[c, z] for z in range(4)], axis=0).astype(BF16)
    cots.forward()
    residual = r.hidden[...].astype(F32)
    unit_in = residual * rms_scale(residual)
    arrive_all(place_copies2)
    low_lane = lanes(8) < 64
    for c in range(8):
        a, b = r.places_all[(2 * c) // 4, (2 * c) % 4], r.places_all[(2 * c + 1) // 4, (2 * c + 1) % 4]
        r.key_row[:, 128 * c : 128 * c + 128] = jnp.where(low_lane, a, b)
    for mb in range(MB):
        key_places = jnp.transpose(jnp.broadcast_to(r.key_row[mb : mb + 1, :], (128, 1024)))
        r.masked[mb] = jnp.where(key_places <= r.places[mb : mb + 1, :], 0.0, -1e30).astype(BF16)
    r.small_all[...] = small.result()
    r.normed_in[...] = spread((unit_in * row_vector(r.small_all, 0)).astype(BF16), r.spread[...])
    bias_query = row_vector(r.small_all, 7)
    ring_qkv.arrive()
    ring_o.forward()
    cosine, sine = r.cosine[...], r.sine[...]
    lin = dot(r.normed_in[...], r.w_qkv[...].reshape(DPAD, 1152))
    keys = rotate(lin[:, 896:1024] + r.small_all[21:22, :], cosine, sine).astype(BF16)
    values = (lin[:, 1024:] + r.small_all[22:23, :]).astype(BF16)
    for mb in range(MB):
        r.kv[mb, :, :128] = keys[64 * mb : 64 * mb + 64]
        r.kv[mb, :, 128:] = values[64 * mb : 64 * mb + 64]
    ring_kv = GatherCtx(p, r.kv, lambda b, h: r.kv_all.at[h, b // 4, lax.rem(b, 4)], r.kv_sems)
    ring_kv.start()
    query_tiles = []
    for t in range(7):
        tile = lin[:, 128 * t : 128 * t + 128] + bias_query[:, 128 * t : 128 * t + 128]
        query_tiles.append((rotate(tile, cosine, sine).astype(BF16)).astype(F32) * (HEAD_SIZE**-0.5))
    scatter_heads(lambda mb, t: query_tiles[t][64 * mb : 64 * mb + 64], r.heads)
    ring_kv.forward()
    ring_gu = GatherCtx(p, r.gu_block, lambda b, h: r.w_gu.at[h, b], r.gu_sems)
    ring_gu.start()
    down_copies = start_all(
        [remote(r.down, r.down_in.at[p.x], r.s_down.at[0, k], r.r_down.at[0, k], p.xpeer(k)) for k in NEAR]
    )
    r.down_in[p.x] = r.down[...]
    ring_kv.arrive()
    for mb in range(MB):
        r.keys[mb] = r.kv_all[mb, :, :, :, :128].reshape(1024, 128)
        r.values[mb] = r.kv_all[mb, :, :, :, 128:].reshape(1024, 128)
        r.values_t[mb] = jnp.transpose(r.values[mb].astype(F32)).astype(BF16)

    def attend(mb):
        def step(t, carry):
            i = mb * 7 + t
            scores = dot_nt(r.keys[mb], r.heads[i]) + r.masked[mb].astype(F32)
            expo = jnp.exp(scores - jnp.max(scores, axis=0, keepdims=True))
            probs = (expo * (1.0 / jnp.sum(expo, axis=0, keepdims=True))).astype(BF16)
            r.probs[i] = probs
            r.attended[i] = collect_heads(dot(r.values_t[mb], probs), t).astype(BF16)
            return carry

        lax.fori_loop(0, 7, step, 0)

    attend(0)
    ring_gu.forward()
    arrive_all(down_copies)
    own_down = r.w_down.at[pl.ds(pl.multiple_of(160 * p.y, 32), 160)]
    own_down[...] = jnp.concatenate([r.down_in[i] for i in range(4)], axis=0).astype(BF16)
    down_copies2 = start_all(
        [remote(own_down, own_down, r.s_down.at[1, k], r.r_down.at[1, k], p.ypeer(k)) for k in NEAR]
    )
    attend(1)
    attended = jnp.concatenate(
        [jnp.concatenate([r.attended[mb * 7 + t] for t in range(7)], axis=1) for mb in range(MB)], axis=0
    )
    r.attended_wide[...] = spread(attended, r.spread[...])
    ring_o.arrive()
    mixed = residual + dot(r.attended_wide[...], r.w_o[...].reshape(DPAD, D))
    r.mixed[...] = mixed
    unit_mid = mixed * rms_scale(mixed)
    r.normed_mid[...] = spread((unit_mid * row_vector(r.small_all, 14)).astype(BF16), r.spread[...])
    ring_mid = GatherDp(p, r.normed_mid, r.normed_all, r.mid_sems)
    ring_mid.start()
    ring_gu.arrive()
    arrive_all(down_copies2)
    cots.arrive()
    ring_mid.forward()
    for ring in (ring_qkv, ring_o, ring_kv, ring_gu, cots, small):
        ring.finish()
    sent_all(attn_copies + gu_copies + place_copies + place_copies2 + down_copies + down_copies2)
    ring_mid.arrive()
    ring_mid.finish()


FRONT_SCRATCH = {
    "attn_src": VM((8, 2048), F32),
    "stage": VM((64, 640), F32),
    "gate_up": VM((8, 8, 1280), F32),
    "down": VM((40, D), F32),
    "small": VM((24, 128), F32),
    "attn_in": VM((4, 8, 2048), F32),
    "gu_in": VM((2, 4, 8, 1280), F32),
    "down_in": VM((4, 40, D), F32),
    "places_x": VM((4, 8, 128), F32),
    "places_all": VM((4, 4, 8, 128), F32),
    "key_row": VM((8, 1024), F32),
    "masked": VM((2, 1024, 128), BF16),
    "qkv_block": VM((2, 16, 1152), BF16),
    "o_block": VM((2, 16, D), BF16),
    "gu_block": VM((2, 32, 1280), BF16),
    "kv": VM((2, 64, 256), BF16),
    "kv_all": VM((2, 4, 4, 64, 256), BF16),
    "values_t": VM((2, 128, 1024), BF16),
    "attended": VM((14, 64, 128), BF16),
    "normed_mid": VM((128, DPAD), BF16),
    "w_qkv": VM((2, 16, 2, 16, 1152), BF16),
    "w_o": VM((2, 16, 2, 16, D), BF16),
    "w_gu": VM((2, 16, 32, 1280), BF16),
    "w_down": VM((640, D), BF16),
    "small_all": VM((24, 128), F32),
    "cot_all": VM((8, 128, D), BF16),
    "normed_all": VM((8, 128, DPAD), BF16),
    "probs": VM((14, 1024, 128), BF16),
    "heads": VM((14, 128, 128), BF16),
    "keys": VM((2, 1024, 128), BF16),
    "values": VM((2, 1024, 128), BF16),
    "attended_wide": VM((128, DPAD), BF16),
    "normed_in": VM((128, DPAD), BF16),
    "mixed": VM((128, D), F32),
    "spread": VM((D, DPAD), BF16),
    "small_bufs": SmallSum.SCRATCH,
    "small_sems": SmallSum.SEMS,
    "s_attn": DMA((4,)), "r_attn": DMA((4,)), "s_gu": DMA((8,)), "r_gu": DMA((8,)),
    "s_place": DMA((2, 4)), "r_place": DMA((2, 4)), "s_down": DMA((2, 4)), "r_down": DMA((2, 4)),
    "qkv_sems": GatherCtx.SEMS, "qkv_mate": GatherCtx.MATE, "o_sems": GatherCtx.SEMS, "o_mate": GatherCtx.MATE,
    "kv_sems": GatherCtx.SEMS, "gu_sems": GatherCtx.SEMS, "cot_sems": GatherDp.SEMS, "mid_sems": GatherDp.SEMS,
}


def back(r, p):
    red_normed = ReduceDp(p, r.part_normed, r.normed_bufs, r.normed_sems)
    red_out = ReduceDp(p, r.part_normed.at[:, :, :, pl.ds(0, D)], r.out_bufs, r.out_sems)

    def rows_of(ref, to):
        return ref[pl.ds(2 * to, 2)].reshape(256, ref.shape[-1])

    def feed(i, carry):
        to = lax.rem(p.z + 1 + i, 4)
        at = pl.ds(pl.multiple_of(256 * to, 256), 256)
        lin = dot(rows_of(r.normed_all, to), r.w_gu[...].reshape(DPAD, 1280))
        gate, up = lin[:, :640], lin[:, 640:]
        sig = 1.0 / (1.0 + jnp.exp(-gate))
        silu = gate * sig
        hidden = (silu * up).astype(BF16)
        back_hidden = dot_nt(rows_of(r.cot_all, to), r.w_down[...]).astype(BF16).astype(F32)
        grad_gate = (back_hidden * up * sig * (1.0 + gate * (1.0 - sig))).astype(BF16)
        grad_up = (back_hidden * silu).astype(BF16)
        for t in range(5):
            r.big[t, at, :] = grad_gate[:, 128 * t : 128 * t + 128]
            r.big[5 + t, at, :] = grad_up[:, 128 * t : 128 * t + 128]
            r.big[10 + t, at, :] = hidden[:, 128 * t : 128 * t + 128]
        part = dot_nt(jnp.concatenate([grad_gate, grad_up], axis=1), r.w_gu[...].reshape(DPAD, 1280))
        r.part_normed[to] = part.astype(BF16).reshape(2, 128, DPAD)
        red_normed.send(i)
        return carry

    lax.fori_loop(0, 4, feed, 0)
    red_normed.forward()

    def project(i, carry):
        to = lax.rem(p.z + 1 + i, 4)
        at = pl.ds(pl.multiple_of(256 * to, 256), 256)
        hidden = jnp.concatenate([r.big[10 + t, at, :] for t in range(5)], axis=1)
        r.part_normed[to, :, :, :D] = dot(hidden, r.w_down[...]).astype(BF16).reshape(2, 128, D)
        red_out.send(i)
        return carry

    def grad_gate_up(i, carry):
        at = pl.ds(pl.multiple_of(256 * i, 256), 256)
        left = r.normed_all[:, :, at].reshape(1024, 256)
        right = jnp.concatenate([r.big[t] for t in range(10)], axis=1)
        part = dot_tn(left, right).astype(BF16).reshape(2, 4, 32, 1280)
        r.g_gu[i // 2, pl.ds(2 * lax.rem(i, 2), 2)] = part
        return carry

    lax.fori_loop(0, 4, grad_gate_up, 0)
    ring_gu = ReduceCtx(p, lambda h, y, x: r.g_gu.at[h, y, x], r.gu_bufs, r.gu_red_sems)
    ring_gu.start()

    def grad_down(t, carry):
        at = pl.ds(pl.multiple_of(128 * t, 128), 128)
        r.g_down[at, :] = dot_tn(r.big[10 + t], r.cot_all[...].reshape(1024, D)).astype(BF16)
        return carry

    lax.fori_loop(0, 5, grad_down, 0)
    down_copies = start_all(
        [
            remote(
                r.g_down.at[pl.ds(pl.multiple_of(160 * p.at_y(k), 32), 160)],
                r.down_y.at[k - 1], r.s_gdown.at[0, k], r.r_gdown.at[0, k], p.ypeer(k),
            )
            for k in NEAR
        ]
    )
    red_normed.sent()
    lax.fori_loop(0, 4, project, 0)
    gain_mlp = row_vector(r.small_all, 14)
    mixed = r.mixed[...]
    inv_mid = rms_scale(mixed)
    unit_mid = mixed * inv_mid
    r.held[...] = unspread(red_normed.result(), r.spread[...])
    grad_normed = r.held[...]
    store_rows(r.small_grads, 14, jnp.sum(grad_normed * unit_mid, axis=0, keepdims=True))
    scaled = grad_normed * gain_mlp
    r.grad_mixed[...] = r.cot[...].astype(F32) + inv_mid * (
        scaled - unit_mid * jnp.mean(scaled * unit_mid, axis=-1, keepdims=True)
    )
    r.low_b[...] = r.grad_mixed[...].astype(BF16)
    wide = dot_nt(r.low_b[...], r.w_o[...].reshape(DPAD, D)).astype(BF16)
    r.held[...] = dot_nt(wide, r.spread[...])
    scatter_heads(lambda mb, t: r.held[64 * mb : 64 * mb + 64, 128 * t : 128 * t + 128], r.grad_heads)
    for mb in range(MB):
        r.values_t[mb] = jnp.transpose(r.keys[mb].astype(F32)).astype(BF16)
    red_out.forward()

    def attend_back(mb):
        def step(t, carry):
            i = mb * 7 + t
            grad_probs = dot_nt(r.values[mb], r.grad_heads[i])
            probs = r.probs[i].astype(F32)
            weighted = probs * grad_probs
            inner = jnp.sum(weighted, axis=0, keepdims=True)
            grad_scores = (weighted - probs * inner).astype(BF16)
            r.big[i] = grad_scores
            r.grad_query[i] = collect_heads(dot(r.values_t[mb], grad_scores), t)
            return carry

        lax.fori_loop(0, 7, step, 0)

    def grad_key_value(i, carry):
        mb, y = i // 4, lax.rem(i, 4)
        at = pl.ds(pl.multiple_of(256 * y, 256), 256)
        scores = jnp.concatenate([r.big[mb * 7 + t, at, :] for t in range(7)], axis=1)
        probs = jnp.concatenate([r.probs[mb * 7 + t, at, :] for t in range(7)], axis=1)
        grad_keys = dot(scores, r.heads[pl.ds(7 * mb, 7)].reshape(896, 128))
        grad_values = dot(probs, r.grad_heads[pl.ds(7 * mb, 7)].reshape(896, 128))
        r.kv_all[mb, y, :, :, :128] = grad_keys.astype(BF16).reshape(4, 64, 128)
        r.kv_all[mb, y, :, :, 128:] = grad_values.astype(BF16).reshape(4, 64, 128)
        return carry

    attend_back(0)
    attend_back(1)
    lax.fori_loop(0, 8, grad_key_value, 0)

    ring_kv = ReduceCtx(p, lambda h, y, x: r.kv_all.at[h, y, x], r.kv_bufs, r.kv_red_sems)
    ring_kv.start()

    def weight_gradient(left, right, out):
        def step(i, carry):
            at = pl.ds(pl.multiple_of(256 * i, 256), 256)
            part = dot_tn(left[:, at], right[...]).astype(BF16)
            out[i // 2, pl.ds(2 * lax.rem(i, 2), 2)] = part.reshape(2, 4, 2, 16, part.shape[-1])
            return carry

        lax.fori_loop(0, 4, step, 0)

    def to_mate(n, grads, got):
        c = remote(grads.at[1 - p.core], got, r.s_mate.at[n], r.r_mate.at[n], {"dp": p.mate()})
        c.start()
        return c

    def with_mate(c, grads, got):
        c.wait_recv()
        for y in range(4):
            got[y] = (grads[p.core, y].astype(F32) + got[y].astype(F32)).astype(BF16)

    weight_gradient(r.attended_wide, r.low_b, r.g_wo)
    mate_wo = to_mate(0, r.g_wo, r.m_wo)
    cosine, sine = r.cosine[...], r.sine[...]
    for t in range(7):
        tile = jnp.concatenate([r.grad_query[t], r.grad_query[7 + t]], axis=0) * (HEAD_SIZE**-0.5)
        r.low_a[:, 128 * t : 128 * t + 128] = rotate_back(tile, cosine, sine).astype(BF16)
    weight_gradient(r.normed_in, r.low_a, r.g_wq)
    mate_wq = to_mate(1, r.g_wq, r.m_wq)
    ring_gu.forward()
    ring_kv.forward()
    with_mate(mate_wo, r.g_wo, r.m_wo)
    ring_wo = ReduceCtx(p, lambda h, y, x: r.m_wo.at[y, x, h], r.wo_bufs, r.wo_sems)
    ring_wo.start()
    with_mate(mate_wq, r.g_wq, r.m_wq)
    ring_wq = ReduceCtx(p, lambda h, y, x: r.m_wq.at[y, x, h], r.wq_bufs, r.wq_sems)
    ring_wq.start()
    store_rows(r.small_grads, 7, jnp.sum(r.low_a[...].astype(F32), axis=0, keepdims=True))
    kv_sum = jnp.concatenate([ring_kv.result(0), ring_kv.result(1)], axis=0)
    grad_key = rotate_back(kv_sum[:, :128], cosine, sine).astype(BF16)
    r.low_kv[:, :128] = grad_key
    r.low_kv[:, 128:] = kv_sum[:, 128:].astype(BF16)
    weight_gradient(r.normed_in, r.low_kv, r.g_wkv)
    mate_wkv = to_mate(2, r.g_wkv, r.m_wkv)
    bias_kv = jnp.sum(r.low_kv[...].astype(F32), axis=0, keepdims=True)
    store_rows(r.small_grads, 21, bias_kv)
    r.small_grads[23:24, :] = jnp.zeros((1, 128), F32)
    lowered = jnp.concatenate([r.low_a[...], r.low_kv[...]], axis=1)
    r.held[...] = unspread(dot_nt(lowered, r.w_qkv[...].reshape(DPAD, 1152)), r.spread[...])
    residual = r.hidden[...].astype(F32)
    inv_rms = rms_scale(residual)
    unit_in = residual * inv_rms
    store_rows(r.small_grads, 0, jnp.sum(r.held[...] * unit_in, axis=0, keepdims=True))
    small = SmallSum(p, r.small_grads, r.small_bufs2, r.small_sems2)
    small.start()
    with_mate(mate_wkv, r.g_wkv, r.m_wkv)
    ring_wkv = ReduceCtx(p, lambda h, y, x: r.m_wkv.at[y, x, h], r.wkv_bufs, r.wkv_sems)
    ring_wkv.start()
    arrive_all(down_copies)
    total = r.g_down[pl.ds(pl.multiple_of(160 * p.y, 32), 160), :].astype(F32)
    for k in NEAR:
        total = total + r.down_y[k - 1].astype(F32)
    for i in range(4):
        r.down_mid[i] = total[40 * i : 40 * i + 40]
    down_copies2 = start_all(
        [
            remote(r.down_mid.at[p.at_x(k)], r.down_x.at[k - 1], r.s_gdown.at[1, k], r.r_gdown.at[1, k], p.xpeer(k))
            for k in NEAR
        ]
    )
    for h in (0, 1):
        part = ring_gu.result(h)
        for z in range(4):
            r.gu_out[z, h] = part[8 * z : 8 * z + 8]
    gu_copies = []
    for k in range(1, 8):
        to = p.dpindex(k)
        gu_copies.append(
            remote(
                r.gu_out.at[to // 2, lax.rem(to, 2)], r.gu_got.at[p.dp], r.s_ggu.at[k], r.r_ggu.at[k], {"dp": to}
            )
        )
    start_all(gu_copies)
    r.gu_got[p.dp] = r.gu_out[p.z, p.core]
    ring_wo.forward()
    ring_wq.forward()
    small.along_y()
    ring_wkv.forward()
    scaled = r.held[...] * row_vector(r.small_all, 0)
    r.grad_in[...] = r.grad_mixed[...] + inv_rms * (
        scaled - unit_in * jnp.mean(scaled * unit_in, axis=-1, keepdims=True)
    )
    r.layer_out[...] = (mixed + red_out.result()).astype(BF16)
    small.along_dp()
    sum_wo = ZSum(p, ring_wo, r.zo_bufs, r.zo_sems)
    sum_wo.start()
    sum_wq = ZSum(p, ring_wq, r.zq_bufs, r.zq_sems)
    sum_wq.start()
    sum_wkv = ZSum(p, ring_wkv, r.zkv_bufs, r.zkv_sems)
    sum_wkv.start()
    build_columns(r.big)
    arrive_all(gu_copies)
    for n, out in enumerate((r.o_gate, r.o_up)):
        for d in range(8):
            r.stage[8 * d : 8 * d + 8, :] = r.gu_got[d, :, 640 * n : 640 * n + 640]
        wide = r.stage[...]
        high = wide.astype(BF16)
        low = (wide - high.astype(F32)).astype(BF16)
        packed = dot_nt(high, columns_of(r.big)) + dot_nt(low, columns_of(r.big))
        for d in range(8):
            out[:, 608 * d : 608 * d + 608] = packed[8 * d : 8 * d + 7, :608]
    arrive_all(down_copies2)
    final = r.down_mid[p.x] + r.down_x[0] + r.down_x[1] + r.down_x[2]
    r.o_down[...] = final[:38]
    r.o_output[...] = sum_wo.result()[:7]
    r.o_query[...] = sum_wq.result()[:7]
    part = sum_wkv.result()
    r.o_key[...] = part[:7, :128]
    r.o_value[...] = part[:7, 128:]
    total = small.result()
    r.o_small[...] = total
    me = p.dp * 16 + p.ctx
    flat = lax.broadcasted_iota(jnp.int32, (7, 128), 0) * 128 + lax.broadcasted_iota(jnp.int32, (7, 128), 1)
    lane = lax.broadcasted_iota(jnp.int32, (1, 128), 1)

    def pick(block, where):
        return jnp.sum(jnp.sum(jnp.where(where, block, 0.0), axis=0, keepdims=True), axis=1, keepdims=True)

    r.o_mine[...] = jnp.zeros_like(r.o_mine)
    for n in range(3):
        row = jnp.zeros((1, 128), F32)
        for i in range(7):
            row = row + jnp.where(lane == i, pick(total[7 * n : 7 * n + 7], flat == me * 7 + i), 0.0)
        r.o_mine[n : n + 1, :] = row
    r.o_mine[3:4, :] = jnp.broadcast_to(pick(total[22:23], lane == me), (1, 128))
    red_out.sent()
    for ring in (red_normed, red_out, ring_gu, ring_kv, ring_wo, ring_wq, ring_wkv, small, sum_wo, sum_wq, sum_wkv):
        ring.finish()
    sent_all([mate_wo, mate_wq, mate_wkv] + down_copies + down_copies2 + gu_copies)


LAYER_OUTS = {
    "layer_out": shape((128, D), BF16),
    "grad_in": shape((128, D), F32),
    "o_query": shape((7, D), F32),
    "o_key": shape((7, 128), F32),
    "o_value": shape((7, 128), F32),
    "o_output": shape((7, D), F32),
    "o_gate": shape((7, 4864), F32),
    "o_up": shape((7, 4864), F32),
    "o_down": shape((38, D), F32),
    "o_small": shape((24, 128), F32),
    "o_mine": shape((8, 128), F32),
}
BACK_SCRATCH = {
    "big": VM((15, 1024, 128), BF16),
    "part_normed": VM((4, 2, 128, DPAD), BF16),
    "normed_bufs": ReduceDp.scratch(128, DPAD), "normed_sems": ReduceDp.SEMS,
    "out_bufs": ReduceDp.scratch(128, D), "out_sems": ReduceDp.SEMS,
    "g_gu": VM((2, 4, 4, 32, 1280), BF16),
    "gu_bufs": ReduceCtx.scratch(32, 1280), "gu_red_sems": ReduceCtx.SEMS,
    "g_down": VM((640, D), BF16),
    "down_y": VM((3, 160, D), BF16), "down_mid": VM((4, 40, D), F32), "down_x": VM((3, 40, D), F32),
    "grad_mixed": VM((128, D), F32),
    "held": VM((128, D), F32),
    "low_a": VM((128, D), BF16),
    "low_b": VM((128, D), BF16),
    "low_kv": VM((128, 256), BF16),
    "grad_heads": VM((14, 128, 128), BF16),
    "grad_query": VM((14, 64, 128), F32),
    "kv_bufs": ReduceCtx.scratch(64, 256), "kv_red_sems": ReduceCtx.SEMS,
    "g_wo": VM((2, 4, 4, 2, 16, D), BF16), "m_wo": VM((4, 4, 2, 16, D), BF16),
    "g_wq": VM((2, 4, 4, 2, 16, D), BF16), "m_wq": VM((4, 4, 2, 16, D), BF16),
    "g_wkv": VM((2, 4, 4, 2, 16, 256), BF16), "m_wkv": VM((4, 4, 2, 16, 256), BF16),
    "wo_bufs": ReduceCtx.scratch(16, D), "wo_sems": ReduceCtx.SEMS,
    "wq_bufs": ReduceCtx.scratch(16, D), "wq_sems": ReduceCtx.SEMS,
    "wkv_bufs": ReduceCtx.scratch(16, 256), "wkv_sems": ReduceCtx.SEMS,
    "zo_bufs": ZSum.scratch(D), "zo_sems": ZSum.SEMS,
    "zq_bufs": ZSum.scratch(D), "zq_sems": ZSum.SEMS,
    "zkv_bufs": ZSum.scratch(256), "zkv_sems": ZSum.SEMS,
    "small_grads": VM((24, 128), F32),
    "small_bufs2": SmallSum.SCRATCH, "small_sems2": SmallSum.SEMS,
    "gu_out": VM((4, 2, 8, 1280), F32), "gu_got": VM((8, 8, 1280), F32),
    "s_mate": DMA((3,)), "r_mate": DMA((3,)), "s_gdown": DMA((2, 4)), "r_gdown": DMA((2, 4)),
    "s_ggu": DMA((8,)), "r_ggu": DMA((8,)),
}


def layer(r):
    p = Place()
    front(r, p)
    back(r, p)


def body(
    hidden_in, positions, norm_attn, w_query, b_query, w_key, b_key, value_weight, value_bias, w_output,
    norm_mlp, w_gate, w_up, w_down, cotangent,
):
    rows = MB * 64
    places = positions[:, 0]
    freqs = THETA_BASE ** (-jnp.arange(0, HEAD_SIZE, 2).astype(F32) / HEAD_SIZE)
    angles = places.reshape(rows).astype(F32)[:, None] * jnp.tile(freqs, 4)[None, :]
    sign = jnp.tile(jnp.repeat(jnp.array([-1.0, 1.0], F32), HEAD_SIZE // 2), 2)
    vectors = jnp.concatenate([norm_attn, b_query, norm_mlp, b_key, value_bias]).astype(F32)
    inputs = {
        "hidden": hidden_in.reshape(rows, D),
        "cot": cotangent.reshape(rows, D),
        "cosine": jnp.cos(angles),
        "sine": jnp.sin(angles) * sign,
        "w_query": w_query, "w_key": w_key, "w_value": value_weight, "w_output": w_output,
        "w_gate": w_gate, "w_up": w_up, "w_down_own": w_down,
        "vectors": jnp.pad(vectors, (0, 105))[None],
        "places": jnp.pad(jnp.tile(places.astype(F32), (1, 2)), ((0, 6), (0, 0))),
    }
    done = call(layer, inputs, LAYER_OUTS, {**FRONT_SCRATCH, **BACK_SCRATCH}, 0, "layer")
    mine = done["o_mine"]
    return (
        done["layer_out"].reshape(MB, 1, 64, D),
        done["grad_in"].reshape(MB, 1, 64, D),
        mine[0, :7],
        done["o_query"],
        mine[1, :7],
        done["o_key"],
        done["o_small"][21],
        done["o_value"],
        mine[3, :1],
        done["o_output"],
        mine[2, :7],
        done["o_gate"],
        done["o_up"],
        done["o_down"],
    )


def solution(mesh):
    rows = P(("dp", "ctx"), None)
    vector = P(("dp", "ctx"))
    tokens = P(None, "dp", "ctx", None)
    in_specs = (
        tokens, P(None, "dp", "ctx"), vector, rows, vector, rows, vector, rows, vector, rows, vector,
        rows, rows, rows, tokens,
    )
    out_specs = (
        tokens, tokens, vector, rows, vector, rows, P(), rows, vector, rows, vector, rows, rows, rows,
    )
    return jax.shard_map(body, mesh=mesh, in_specs=in_specs, out_specs=out_specs, check_vma=False)
```

```python
import math
import types

import jax
import jax.numpy as jnp
from jax import lax
from jax.experimental import pallas as pl
from jax.experimental.pallas import tpu as pltpu
from jax.sharding import PartitionSpec as P

QUERY_HEADS = 14
KEY_VALUE_HEADS = 2
HEAD_SIZE = 64
GROUP = QUERY_HEADS // KEY_VALUE_HEADS
MB = 2
D = 896
DPAD = 1024
EPSILON = 1e-06
THETA_BASE = 1000000.0
F32 = jnp.float32
BF16 = jnp.bfloat16
MESH = pl.DeviceIdType.MESH
DMA = pltpu.SemaphoreType.DMA
VM = pltpu.VMEM


def remote(src, dst, ss, rs, peer):
    return pltpu.make_async_remote_copy(
        src_ref=src, dst_ref=dst, send_sem=ss, recv_sem=rs, device_id=peer, device_id_type=MESH
    )


def greet(peers):
    sem = pltpu.get_barrier_semaphore()
    for peer in peers:
        pl.semaphore_signal(sem, inc=1, device_id=peer, device_id_type=MESH)


def meet(peers):
    pl.semaphore_wait(pltpu.get_barrier_semaphore(), len(peers))


class Place:
    def __init__(self):
        self.dp = lax.axis_index("dp")
        self.ctx = lax.axis_index("ctx")
        self.y, self.x = self.ctx // 4, lax.rem(self.ctx, 4)
        self.z, self.core = self.dp // 2, lax.rem(self.dp, 2)

    def at_x(self, k):
        return lax.rem(self.x + (k + 4), 4)

    def at_y(self, k):
        return lax.rem(self.y + (k + 4), 4)

    def at_z(self, k):
        return lax.rem(self.z + (k + 4), 4)

    def line(self, axis, k):
        return self.y * 4 + self.at_x(k) if axis == 0 else self.at_y(k) * 4 + self.x

    def xpeer(self, k):
        return {"ctx": self.line(0, k)}

    def ypeer(self, k):
        return {"ctx": self.line(1, k)}

    def peer(self, axis, k):
        return {"ctx": self.line(axis, k)}

    def zindex(self, k):
        return self.at_z(k) * 2 + self.core

    def mate(self):
        return self.z * 2 + 1 - self.core

    def dpindex(self, k):
        return lax.rem(self.dp + k, 8)


NEAR = (1, 3, 2)


class GatherCtx:
    SEMS = [DMA((2, 4)), DMA((2, 4)), DMA((2, 4, 4)), DMA((2, 4, 4)), DMA((2,))]
    MATE = [DMA((2, 4, 4)), DMA((2, 4, 4))]

    def __init__(self, place, src, dst_at, sems, mate=None):
        self.p, self.src, self.dst_at, self.sems, self.mate = place, src, dst_at, sems, mate
        self.mated = []

    def block(self, h, j, k):
        p = self.p
        return p.at_y(-k) * 4 + p.at_x(-j) if h == 0 else p.at_y(-j) * 4 + p.at_x(-k)

    def share(self, h, j, k):
        if self.mate is None:
            return
        dst = self.dst_at(self.block(h, j, k), h)
        src = self.src.at[h] if j == 0 and k == 0 else dst
        c = remote(src, dst, self.mate[0].at[h, j, k], self.mate[1].at[h, j, k], {"dp": self.p.mate()})
        c.start()
        self.mated.append(c)

    def start(self):
        p, (s1, r1, s2, r2, ls) = self.p, self.sems
        self.local = []
        for h in (0, 1):
            c = pltpu.make_async_copy(self.src.at[h], self.dst_at(p.ctx, h), ls.at[h])
            c.start()
            self.local.append(c)
        self.first = {}
        for k in NEAR:
            for h in (0, 1):
                c = remote(self.src.at[h], self.dst_at(p.ctx, h), s1.at[h, k], r1.at[h, k], p.peer(h, k))
                c.start()
                self.first[h, k] = c
        for h in (0, 1):
            self.share(h, 0, 0)

    def forward(self):
        p, (s1, r1, s2, r2, ls) = self.p, self.sems
        self.second = {}
        for j in (0,) + NEAR:
            for h in (0, 1):
                if j:
                    self.first[h, j].wait_recv()
                dst = self.dst_at(p.line(h, -j), h)
                src = self.src.at[h] if j == 0 else dst
                for k in NEAR:
                    c = remote(src, dst, s2.at[h, j, k], r2.at[h, j, k], p.peer(1 - h, k))
                    c.start()
                    self.second[h, j, k] = c
                if j:
                    self.share(h, j, 0)

    def arrive(self):
        for c in self.local:
            c.wait()
        for (h, j, k), c in self.second.items():
            c.wait_recv()
            self.share(h, j, k)
        for c in self.mated:
            c.wait_recv()

    def finish(self):
        for c in list(self.first.values()) + list(self.second.values()) + self.mated:
            c.wait_send()


class ReduceCtx:
    SEMS = [DMA((2, 4)), DMA((2, 4)), DMA((2, 4)), DMA((2, 4))]

    @staticmethod
    def scratch(rows, cols):
        return [VM((2, 3, 4, rows, cols), BF16), VM((2, 3, rows, cols), BF16)]

    def __init__(self, place, src_at, bufs, sems):
        self.p, self.src_at, self.bufs, self.sems = place, src_at, bufs, sems
        self.first = {}

    def start(self, halves=(0, 1)):
        p, (s1, r1, s2, r2) = self.p, self.sems
        got = self.bufs[0]
        every = slice(None)
        for k in NEAR:
            for h in halves:
                src = self.src_at(0, p.at_y(k), every) if h == 0 else self.src_at(1, every, p.at_x(k))
                c = remote(src, got.at[h, k - 1], s1.at[h, k], r1.at[h, k], p.peer(1 - h, k))
                c.start()
                self.first[h, k] = c

    def forward(self):
        p, (s1, r1, s2, r2) = self.p, self.sems
        got, last = self.bufs
        self.second = {}
        for h in (0, 1):
            for k in NEAR:
                self.first[h, k].wait_recv()
            for i in range(4):
                own = self.src_at(0, p.y, i) if h == 0 else self.src_at(1, i, p.x)
                total = own[...].astype(F32)
                for k in NEAR:
                    total = total + got[h, k - 1, i].astype(F32)
                got[h, 0, i] = total.astype(BF16)
            for k in NEAR:
                to = p.at_x(k) if h == 0 else p.at_y(k)
                c = remote(got.at[h, 0, to], last.at[h, k - 1], s2.at[h, k], r2.at[h, k], p.peer(h, k))
                c.start()
                self.second[h, k] = c

    def result(self, h):
        p = self.p
        got, last = self.bufs
        for k in NEAR:
            self.second[h, k].wait_recv()
        total = got[h, 0, p.x if h == 0 else p.y].astype(F32)
        for k in NEAR:
            total = total + last[h, k - 1].astype(F32)
        return total

    def finish(self):
        for c in list(self.first.values()) + list(self.second.values()):
            c.wait_send()


class GatherDp:
    SEMS = [DMA((4,)), DMA((4,)), DMA((4,)), DMA((4,)), DMA]

    def __init__(self, place, src, dst_at, sems):
        self.p, self.src, self.dst_at, self.sems = place, src, dst_at, sems
        rows = src.shape[0]
        self.halves = {1: pl.ds(0, rows // 2), 3: pl.ds(rows // 2, rows // 2)}

    def start(self):
        p, (s1, r1, s2, r2, ls) = self.p, self.sems
        self.local = pltpu.make_async_copy(self.src, self.dst_at(p.dp), ls)
        self.local.start()
        self.first, self.second, self.relayed = {}, {}, {}
        for k in (1, 3):
            c = remote(self.src, self.dst_at(p.dp), s1.at[k], r1.at[k], {"dp": p.zindex(k)})
            c.start()
            self.first[k] = c

    def relay(self):
        p, (s1, r1, s2, r2, ls) = self.p, self.sems
        for k in (1, 3):
            self.first[k].wait_recv()
            part = self.dst_at(p.zindex(-k)).at[self.halves[k]]
            c = remote(part, part, s1.at[k - 1], r1.at[k - 1], {"dp": p.zindex(k)})
            c.start()
            self.relayed[k] = c

    def forward(self, j):
        p, (s1, r1, s2, r2, ls) = self.p, self.sems
        if j == 2:
            for c in self.relayed.values():
                c.wait_recv()
        block = p.zindex(-j)
        src = self.dst_at(block) if j else self.src
        c = remote(src, self.dst_at(block), s2.at[j], r2.at[j], {"dp": p.mate()})
        c.start()
        self.second[j] = c

    def arrive(self, j):
        if j == 0:
            self.local.wait()
        self.second[j].wait_recv()

    def finish(self):
        for c in list(self.first.values()) + list(self.second.values()) + list(self.relayed.values()):
            c.wait_send()


class ReduceDp:
    SEMS = [DMA((4,)), DMA((4,)), DMA((4,)), DMA((4,))]

    @staticmethod
    def scratch(rows, cols):
        return [VM((4, rows, cols), BF16), VM((3, rows, cols), BF16)]

    def __init__(self, place, src, bufs, sems):
        self.p, self.src, self.bufs, self.sems = place, src, bufs, sems
        self.first, self.second = {}, {}

    def send(self, k):
        p, (s1, r1, s2, r2) = self.p, self.sems
        to = p.at_z(k)
        c = remote(self.src.at[to, 1 - p.core], self.bufs[0].at[to], s1.at[k], r1.at[k], {"dp": p.mate()})
        c.start()
        self.first[k] = c

    def forward(self, k):
        p, (s1, r1, s2, r2) = self.p, self.sems
        got, last = self.bufs
        to = p.at_z(k)
        self.first[k].wait_recv()
        total = self.src[to, p.core].astype(F32) + got[to].astype(F32)
        got[to] = total.astype(BF16)
        if k:
            c = remote(got.at[to], last.at[k - 1], s2.at[k], r2.at[k], {"dp": p.zindex(k)})
            c.start()
            self.second[k] = c

    def result(self):
        got, last = self.bufs
        total = got[self.p.z].astype(F32)
        for k in NEAR:
            self.second[k].wait_recv()
            total = total + last[k - 1].astype(F32)
        return total

    def sent(self):
        for c in self.first.values():
            c.wait_send()

    def finish(self):
        for c in self.second.values():
            c.wait_send()


def xy_peers(p):
    return [p.peer(axis, k) for axis in (0, 1) for k in NEAR]


def dp_peers(p):
    return [{"dp": p.dpindex(k)} for k in range(1, 8)]


def shape(dims, kind):
    return jax.ShapeDtypeStruct(dims, kind)


def call(phase, inputs, outs, scratch, cid, name):
    flat, where = [], {}
    for key, entry in scratch.items():
        entries = entry if isinstance(entry, list) else [entry]
        where[key] = (len(flat), len(entries), isinstance(entry, list))
        flat += entries

    def kernel(*refs):
        named = dict(zip(list(inputs) + list(outs), refs))
        tail = refs[len(inputs) + len(outs) :]
        for key, (start, count, many) in where.items():
            named[key] = list(tail[start : start + count]) if many else tail[start]
        phase(types.SimpleNamespace(**named))

    results = pl.pallas_call(
        kernel,
        out_shape=tuple(outs.values()),
        in_specs=[pl.BlockSpec(memory_space=VM)] * len(inputs),
        out_specs=tuple(pl.BlockSpec(memory_space=VM) for _ in outs),
        scratch_shapes=flat,
        name=name,
        compiler_params=pltpu.CompilerParams(
            collective_id=cid, has_side_effects=True, vmem_limit_bytes=63 << 20
        ),
    )(*inputs.values())
    return dict(zip(outs, results))


def dot(left, right):
    return jnp.dot(left, right, preferred_element_type=F32)


def dot_tn(left, right):
    return lax.dot_general(left, right, (((0,), (0,)), ((), ())), preferred_element_type=F32)


def dot_nt(left, right):
    return lax.dot_general(left, right, (((1,), (1,)), ((), ())), preferred_element_type=F32)


def rms_scale(values):
    return lax.rsqrt(jnp.mean(values * values, axis=-1, keepdims=True) + EPSILON)


def row_vector(ref, start):
    return jnp.concatenate([ref[start + i : start + i + 1, :] for i in range(7)], axis=1)


def store_rows(ref, start, vector):
    for i in range(vector.shape[1] // 128):
        ref[start + i : start + i + 1, :] = vector[:, 128 * i : 128 * i + 128]


def build_spread(ref):
    for part in range(7):
        source = lax.broadcasted_iota(jnp.int32, (128, DPAD), 0) + 128 * part
        column = lax.broadcasted_iota(jnp.int32, (128, DPAD), 1)
        inner = column & 7
        owner = ((column >> 3) & 3) * 2 + (column >> 9)
        wanted = (owner * 16 + ((column >> 5) & 15)) * 7 + inner
        ref[128 * part : 128 * part + 128, :] = jnp.where(
            (source == wanted) & (inner < 7), 1.0, 0.0
        ).astype(BF16)


def spread(values, matrix):
    return dot(values, matrix).astype(BF16)


def unspread(values, matrix):
    high = values.astype(BF16)
    low = (values - high.astype(F32)).astype(BF16)
    return dot_nt(high, matrix) + dot_nt(low, matrix)


def lanes(rows):
    return lax.broadcasted_iota(jnp.int32, (rows, 128), 1)


def half_turn(tile):
    first = (lanes(tile.shape[0]) & 63) < 32
    return jnp.where(first, pltpu.roll(tile, 96, 1), pltpu.roll(tile, 32, 1))


def rotate(tile, cosine, signed_sine):
    return tile * cosine + half_turn(tile) * signed_sine


def rotate_back(tile, cosine, signed_sine):
    return tile * cosine - half_turn(tile) * signed_sine


def scatter_heads(tile_of, dst):
    for mb in range(MB):
        for head in range(QUERY_HEADS):
            tile = tile_of(mb, head // 2)
            group = head // GROUP
            if head % 2 != group:
                tile = pltpu.roll(tile, 64, 1)
            tile = jnp.where((lanes(64) >= 64) == (group == 1), tile, 0.0)
            at = (head % 2) * 64
            dst[mb * 7 + head // 2, at : at + 64, :] = tile.astype(BF16)


def collect_heads(transposed, t):
    both = jnp.transpose(transposed)
    even, odd = both[:64], both[64:]
    even = jnp.where(t >= 4, pltpu.roll(even, 64, 1), even)
    odd = jnp.where(t <= 2, pltpu.roll(odd, 64, 1), odd)
    return jnp.where(lanes(64) < 64, even, odd)


def start_all(copies):
    for c in copies:
        c.start()
    return copies


def arrive_all(copies):
    for c in copies:
        c.wait_recv()


def sent_all(copies):
    for c in copies:
        c.wait_send()


class SmallSum:
    SCRATCH = [VM((3, 24, 128), F32), VM((3, 24, 128), F32), VM((7, 24, 128), F32), VM((2, 24, 128), F32)]
    SEMS = [DMA((3, 8)), DMA((3, 8))]

    def __init__(self, place, src, bufs, sems):
        self.p, self.src, self.bufs, self.sems = place, src, bufs, sems
        self.copies = []

    def start(self):
        p, (s, r) = self.p, self.sems
        self.x = start_all([remote(self.src, self.bufs[0].at[k - 1], s.at[0, k], r.at[0, k], p.xpeer(k)) for k in NEAR])

    def along_y(self):
        p, (s, r) = self.p, self.sems
        arrive_all(self.x)
        got, sums = self.bufs[0], self.bufs[3]
        sums[0] = self.src[...] + got[0] + got[1] + got[2]
        self.y = start_all(
            [remote(sums.at[0], self.bufs[1].at[k - 1], s.at[1, k], r.at[1, k], p.ypeer(k)) for k in NEAR]
        )

    def along_dp(self):
        p, (s, r) = self.p, self.sems
        arrive_all(self.y)
        got, sums = self.bufs[1], self.bufs[3]
        sums[1] = sums[0] + got[0] + got[1] + got[2]
        self.d = start_all(
            [
                remote(sums.at[1], self.bufs[2].at[k - 1], s.at[2, k], r.at[2, k], {"dp": p.dpindex(k)})
                for k in range(1, 8)
            ]
        )

    def result(self):
        arrive_all(self.d)
        total = self.bufs[3][1]
        for k in range(7):
            total = total + self.bufs[2][k]
        return total

    def finish(self):
        sent_all(self.x + self.y + self.d)


class ZSum:
    SEMS = [DMA((4,)), DMA((4,))]

    @staticmethod
    def scratch(cols):
        return [VM((4, 8, cols), F32), VM((4, 8, cols), F32)]

    def __init__(self, place, ring, bufs, sems):
        self.p, self.ring, self.bufs, self.sems = place, ring, bufs, sems

    def start(self):
        p, (s, r), (out, got) = self.p, self.sems, self.bufs
        for h in (0, 1):
            part = self.ring.result(h)
            out[2 * h], out[2 * h + 1] = part[:8], part[8:]
        self.copies = start_all(
            [remote(out.at[p.at_z(k)], got.at[p.z], s.at[k], r.at[k], {"dp": p.zindex(k)}) for k in NEAR]
        )
        got[p.z] = out[p.z]

    def result(self):
        arrive_all(self.copies)
        got = self.bufs[1]
        return got[0] + got[1] + got[2] + got[3]

    def finish(self):
        sent_all(self.copies)


def build_columns(big):
    for t in range(5):
        column = lax.broadcasted_iota(jnp.int32, (640, 128), 1) + 128 * t
        source = lax.broadcasted_iota(jnp.int32, (640, 128), 0)
        owner = (column * 1639) >> 16
        inner = column - owner * 40
        big[t, :640, :] = jnp.where((source == owner * 38 + inner) & (inner < 38), 1.0, 0.0).astype(BF16)


def columns_of(big):
    return jnp.concatenate([big[t, :640, :] for t in range(5)], axis=1)


def front(r, p):
    peers = xy_peers(p) + dp_peers(p)
    greet(peers)
    r.attn_src[...] = jnp.zeros_like(r.attn_src)
    r.stage[...] = jnp.zeros_like(r.stage)
    r.down[...] = jnp.zeros_like(r.down)
    r.down[:38, :] = r.w_down_own[...].astype(F32)
    r.attn_src[:7, :896] = r.w_query[...].astype(F32)
    r.attn_src[:7, 896:1024] = r.w_key[...].astype(F32)
    r.attn_src[:7, 1024:1152] = r.w_value[...].astype(F32)
    r.attn_src[:7, 1152:] = r.w_output[...].astype(F32)
    r.small[...] = jnp.zeros_like(r.small)
    me = p.dp * 16 + p.ctx
    flat = lax.broadcasted_iota(jnp.int32, (7, 128), 0) * 128 + lax.broadcasted_iota(jnp.int32, (7, 128), 1)
    for n, ref in enumerate((r.norm_attn, r.b_query, r.norm_mlp)):
        vector = ref[...].astype(F32)[None]
        total = jnp.zeros((7, 128), F32)
        for i in range(7):
            total = total + jnp.where(flat == me * 7 + i, vector[:, i : i + 1], 0.0)
        r.small[7 * n : 7 * n + 7, :] = total
    for n, ref in enumerate((r.b_key, r.value_bias)):
        r.small[21 + n : 22 + n, :] = jnp.where(flat[:1] == me, ref[...].astype(F32)[None], 0.0)
    r.places[...] = jnp.zeros_like(r.places)
    for at in (0, 64):
        r.places[:MB, at : at + 64] = r.positions[:, 0].astype(F32)
    meet(peers)
    attn_copies = start_all(
        [remote(r.attn_src, r.attn_in.at[p.z], r.s_attn.at[k], r.r_attn.at[k], {"dp": p.zindex(k)}) for k in NEAR]
    )
    small = SmallSum(p, r.small, r.small_bufs, r.small_sems)
    small.start()
    place_copies = start_all(
        [remote(r.places, r.places_x.at[p.x], r.s_place.at[0, k], r.r_place.at[0, k], p.xpeer(k)) for k in NEAR]
    )
    r.attn_in[p.z] = r.attn_src[...]
    r.places_x[p.x] = r.places[...]
    build_columns(r.big)
    for n, ref in enumerate((r.w_gate, r.w_up)):
        whole = ref[...].astype(F32)
        for d in range(8):
            r.stage[8 * d : 8 * d + 7, :608] = whole[:, 608 * d : 608 * d + 608]
        wide = dot(r.stage[...].astype(BF16), columns_of(r.big))
        for d in range(8):
            r.gate_up[d, :, 640 * n : 640 * n + 640] = wide[8 * d : 8 * d + 8]
    gu_copies = []
    for k in range(1, 8):
        to = p.dpindex(k)
        gu_copies.append(
            remote(r.gate_up.at[to], r.gu_in.at[p.core, p.z], r.s_gu.at[k], r.r_gu.at[k], {"dp": to})
        )
    start_all(gu_copies)
    r.gu_in[p.core, p.z] = r.gate_up[p.dp]
    cots = GatherDp(p, r.cot, lambda b: r.cot_all.at[b], r.cot_sems)
    cots.start()
    arrive_all(attn_copies)
    for h in (0, 1):
        pair = jnp.concatenate([r.attn_in[2 * h], r.attn_in[2 * h + 1]], axis=0).astype(BF16)
        r.qkv_block[h] = pair[:, :1152]
        r.o_block[h] = pair[:, 1152:]
    ring_qkv = GatherCtx(p, r.qkv_block, lambda b, h: r.w_qkv.at[p.core, b, h], r.qkv_sems, r.qkv_mate)
    ring_qkv.start()
    small.along_y()
    arrive_all(place_copies)
    place_copies2 = start_all(
        [remote(r.places_x, r.places_all.at[p.y], r.s_place.at[1, k], r.r_place.at[1, k], p.ypeer(k)) for k in NEAR]
    )
    r.places_all[p.y] = r.places_x[...]
    ring_qkv.forward()
    ring_o = GatherCtx(p, r.o_block, lambda b, h: r.w_o.at[p.core, b, h], r.o_sems, r.o_mate)
    ring_o.start()
    build_spread(r.spread)
    inner = lanes(1) & 63
    freqs = jnp.exp((inner & 31).astype(F32) * (-math.log(THETA_BASE) / 32))
    sign = jnp.where(inner < 32, -1.0, 1.0)
    for mb in range(MB):
        angles = jnp.transpose(jnp.broadcast_to(r.places[mb : mb + 1, :], (128, 128)))[:64] * freqs
        r.cosine[64 * mb : 64 * mb + 64, :] = jnp.cos(angles)
        r.sine[64 * mb : 64 * mb + 64, :] = jnp.sin(angles) * sign
    small.along_dp()
    arrive_all(gu_copies)
    for c in (0, 1):
        r.gu_block[c] = jnp.concatenate([r.gu_in[c, z] for z in range(4)], axis=0).astype(BF16)
    cots.relay()
    for j in (0, 1, 3):
        cots.forward(j)
    residual = r.hidden[...].astype(F32)
    unit_in = residual * rms_scale(residual)
    arrive_all(place_copies2)
    low_lane = lanes(8) < 64
    for c in range(8):
        a, b = r.places_all[(2 * c) // 4, (2 * c) % 4], r.places_all[(2 * c + 1) // 4, (2 * c + 1) % 4]
        r.key_row[:, 128 * c : 128 * c + 128] = jnp.where(low_lane, a, b)
    for mb in range(MB):
        key_places = jnp.transpose(jnp.broadcast_to(r.key_row[mb : mb + 1, :], (128, 1024)))
        r.masked[mb] = jnp.where(key_places <= r.places[mb : mb + 1, :], 0.0, -1e30).astype(BF16)
    r.small_all[...] = small.result()
    r.normed_in[...] = spread((unit_in * row_vector(r.small_all, 0)).astype(BF16), r.spread[...])
    bias_query = row_vector(r.small_all, 7)
    ring_qkv.arrive()
    ring_o.forward()
    ring_gu = GatherCtx(p, r.gu_block, lambda b, h: r.w_gu.at[h, b], r.gu_sems)
    ring_gu.start()
    down_copies = start_all(
        [remote(r.down, r.down_in.at[p.x], r.s_down.at[0, k], r.r_down.at[0, k], p.xpeer(k)) for k in NEAR]
    )
    r.down_in[p.x] = r.down[...]
    cosine, sine = r.cosine[...], r.sine[...]
    lin = dot(r.normed_in[...], r.w_qkv[:, :, :, :, 896:].reshape(DPAD, 256))
    keys = rotate(lin[:, :128] + r.small_all[21:22, :], cosine, sine).astype(BF16)
    values = (lin[:, 128:] + r.small_all[22:23, :]).astype(BF16)
    for mb in range(MB):
        r.kv[mb, :, :128] = keys[64 * mb : 64 * mb + 64]
        r.kv[mb, :, 128:] = values[64 * mb : 64 * mb + 64]
    ring_kv = GatherCtx(p, r.kv, lambda b, h: r.kv_all.at[h, b // 4, lax.rem(b, 4)], r.kv_sems)
    ring_kv.start()
    lin = dot(r.normed_in[...], r.w_qkv[:, :, :, :, :896].reshape(DPAD, D))
    query_tiles = []
    for t in range(7):
        tile = lin[:, 128 * t : 128 * t + 128] + bias_query[:, 128 * t : 128 * t + 128]
        query_tiles.append((rotate(tile, cosine, sine).astype(BF16)).astype(F32) * (HEAD_SIZE**-0.5))
    scatter_heads(lambda mb, t: query_tiles[t][64 * mb : 64 * mb + 64], r.heads)
    ring_kv.forward()
    ring_gu.forward()
    arrive_all(down_copies)
    own_down = r.w_down.at[pl.ds(pl.multiple_of(160 * p.y, 32), 160)]
    own_down[...] = jnp.concatenate([r.down_in[i] for i in range(4)], axis=0).astype(BF16)
    down_copies2 = start_all(
        [remote(own_down, own_down, r.s_down.at[1, k], r.r_down.at[1, k], p.ypeer(k)) for k in NEAR]
    )
    ring_kv.arrive()
    for mb in range(MB):
        r.keys[mb] = r.kv_all[mb, :, :, :, :128].reshape(1024, 128)
        r.values[mb] = r.kv_all[mb, :, :, :, 128:].reshape(1024, 128)
        r.values_t[mb] = jnp.transpose(r.values[mb].astype(F32)).astype(BF16)

    def attend(mb):
        def step(t, carry):
            i = mb * 7 + t
            scores = dot_nt(r.keys[mb], r.heads[i]) + r.masked[mb].astype(F32)
            expo = jnp.exp(scores - jnp.max(scores, axis=0, keepdims=True))
            probs = (expo * (1.0 / jnp.sum(expo, axis=0, keepdims=True))).astype(BF16)
            r.probs[i] = probs
            r.attended[i] = collect_heads(dot(r.values_t[mb], probs), t).astype(BF16)
            return carry

        lax.fori_loop(0, 7, step, 0)

    gain_mlp = row_vector(r.small_all, 14)
    rings = []

    def finish_rows(mb):
        at = slice(64 * mb, 64 * mb + 64)
        attended = jnp.concatenate([r.attended[mb * 7 + t] for t in range(7)], axis=1)
        r.attended_wide[at, :] = spread(attended, r.spread[...])
        mixed = residual[at] + dot(r.attended_wide[at, :], r.w_o[...].reshape(DPAD, D))
        r.mixed[at, :] = mixed
        unit_mid = mixed * rms_scale(mixed)
        r.normed_mid[mb] = spread((unit_mid * gain_mlp).astype(BF16), r.spread[...])
        ring = GatherDp(p, r.normed_mid.at[mb], lambda b: r.normed_all.at[b, mb], r.mid_sems[5 * mb : 5 * mb + 5])
        ring.start()
        ring.forward(0)
        rings.append(ring)

    attend(0)
    ring_o.arrive()
    finish_rows(0)
    cots.forward(2)
    attend(1)
    finish_rows(1)
    rings[0].relay()
    ring_gu.arrive()
    arrive_all(down_copies2)
    for j in range(4):
        cots.arrive(j)
    for ring in (ring_qkv, ring_o, ring_kv, ring_gu, cots, small):
        ring.finish()
    sent_all(attn_copies + gu_copies + place_copies + place_copies2 + down_copies + down_copies2)
    return rings


FRONT_SCRATCH = {
    "places": VM((8, 128), F32),
    "cosine": VM((128, 128), F32),
    "sine": VM((128, 128), F32),
    "attn_src": VM((8, 2048), F32),
    "stage": VM((64, 640), F32),
    "gate_up": VM((8, 8, 1280), F32),
    "down": VM((40, D), F32),
    "small": VM((24, 128), F32),
    "attn_in": VM((4, 8, 2048), F32),
    "gu_in": VM((2, 4, 8, 1280), F32),
    "down_in": VM((4, 40, D), F32),
    "places_x": VM((4, 8, 128), F32),
    "places_all": VM((4, 4, 8, 128), F32),
    "key_row": VM((8, 1024), F32),
    "masked": VM((2, 1024, 128), BF16),
    "qkv_block": VM((2, 16, 1152), BF16),
    "o_block": VM((2, 16, D), BF16),
    "gu_block": VM((2, 32, 1280), BF16),
    "kv": VM((2, 64, 256), BF16),
    "kv_all": VM((2, 4, 4, 64, 256), BF16),
    "values_t": VM((2, 128, 1024), BF16),
    "attended": VM((14, 64, 128), BF16),
    "normed_mid": VM((2, 64, DPAD), BF16),
    "w_qkv": VM((2, 16, 2, 16, 1152), BF16),
    "w_o": VM((2, 16, 2, 16, D), BF16),
    "w_gu": VM((2, 16, 32, 1280), BF16),
    "w_down": VM((640, D), BF16),
    "small_all": VM((24, 128), F32),
    "cot_all": VM((8, 128, D), BF16),
    "normed_all": VM((8, 2, 64, DPAD), BF16),
    "probs": VM((14, 1024, 128), BF16),
    "heads": VM((14, 128, 128), BF16),
    "keys": VM((2, 1024, 128), BF16),
    "values": VM((2, 1024, 128), BF16),
    "attended_wide": VM((128, DPAD), BF16),
    "normed_in": VM((128, DPAD), BF16),
    "mixed": VM((128, D), F32),
    "spread": VM((D, DPAD), BF16),
    "small_bufs": SmallSum.SCRATCH,
    "small_sems": SmallSum.SEMS,
    "s_attn": DMA((4,)), "r_attn": DMA((4,)), "s_gu": DMA((8,)), "r_gu": DMA((8,)),
    "s_place": DMA((2, 4)), "r_place": DMA((2, 4)), "s_down": DMA((2, 4)), "r_down": DMA((2, 4)),
    "qkv_sems": GatherCtx.SEMS, "qkv_mate": GatherCtx.MATE, "o_sems": GatherCtx.SEMS, "o_mate": GatherCtx.MATE,
    "kv_sems": GatherCtx.SEMS, "gu_sems": GatherCtx.SEMS, "cot_sems": GatherDp.SEMS, "mid_sems": GatherDp.SEMS * 2,
}


def back(r, p, rings):
    red_normed = ReduceDp(p, r.part_normed, r.normed_bufs, r.normed_sems)
    red_out = ReduceDp(p, r.part_normed.at[:, :, :, pl.ds(0, D)], r.out_bufs, r.out_sems)

    def rows_of(ref, to):
        return ref[pl.ds(2 * to, 2)].reshape(256, ref.shape[-1])

    def feed(k, carry):
        to = lax.rem(p.z + k, 4)
        at = pl.ds(pl.multiple_of(256 * to, 256), 256)
        lin = dot(rows_of(r.normed_all, to), r.w_gu[...].reshape(DPAD, 1280))
        gate, up = lin[:, :640], lin[:, 640:]
        sig = 1.0 / (1.0 + jnp.exp(-gate))
        silu = gate * sig
        hidden = (silu * up).astype(BF16)
        back_hidden = dot_nt(rows_of(r.cot_all, to), r.w_down[...]).astype(BF16).astype(F32)
        grad_gate = (back_hidden * up * sig * (1.0 + gate * (1.0 - sig))).astype(BF16)
        grad_up = (back_hidden * silu).astype(BF16)
        for t in range(5):
            r.big[t, at, :] = grad_gate[:, 128 * t : 128 * t + 128]
            r.big[5 + t, at, :] = grad_up[:, 128 * t : 128 * t + 128]
            r.big[10 + t, at, :] = hidden[:, 128 * t : 128 * t + 128]
        part = dot_nt(jnp.concatenate([grad_gate, grad_up], axis=1), r.w_gu[...].reshape(DPAD, 1280))
        r.part_normed[to] = part.astype(BF16).reshape(2, 128, DPAD)
        return carry

    def feed_block(j):
        k = (4 - j) % 4
        for ring in rings:
            ring.arrive(j)
        lax.fori_loop(k, k + 1, feed, 0)
        red_normed.send(k)

    def pass_on(j):
        for ring in rings:
            ring.forward(j)

    feed_block(0)
    rings[1].relay()
    pass_on(1)
    pass_on(3)
    feed_block(1)
    feed_block(3)
    pass_on(2)
    red_normed.forward(3)
    red_normed.forward(1)
    feed_block(2)
    red_normed.forward(2)
    red_normed.forward(0)

    def project(k, carry):
        to = lax.rem(p.z + k, 4)
        at = pl.ds(pl.multiple_of(256 * to, 256), 256)
        hidden = jnp.concatenate([r.big[10 + t, at, :] for t in range(5)], axis=1)
        r.part_normed[to, :, :, :D] = dot(hidden, r.w_down[...]).astype(BF16).reshape(2, 128, D)
        return carry

    def grad_gate_up(i, carry):
        at = pl.ds(pl.multiple_of(256 * i, 256), 256)
        left = r.normed_all[:, :, :, at].reshape(1024, 256)
        right = jnp.concatenate([r.big[t] for t in range(10)], axis=1)
        part = dot_tn(left, right).astype(BF16).reshape(2, 4, 32, 1280)
        r.g_gu[i // 2, pl.ds(2 * lax.rem(i, 2), 2)] = part
        return carry

    lax.fori_loop(0, 4, grad_gate_up, 0)
    ring_gu = ReduceCtx(p, lambda h, y, x: r.g_gu.at[h, y, x], r.gu_bufs, r.gu_red_sems)
    ring_gu.start()

    def grad_down(t, carry):
        at = pl.ds(pl.multiple_of(128 * t, 128), 128)
        r.g_down[at, :] = dot_tn(r.big[10 + t], r.cot_all[...].reshape(1024, D)).astype(BF16)
        return carry

    lax.fori_loop(0, 5, grad_down, 0)
    down_copies = start_all(
        [
            remote(
                r.g_down.at[pl.ds(pl.multiple_of(160 * p.at_y(k), 32), 160)],
                r.down_y.at[k - 1], r.s_gdown.at[0, k], r.r_gdown.at[0, k], p.ypeer(k),
            )
            for k in NEAR
        ]
    )
    red_normed.sent()
    for k in NEAR + (0,):
        lax.fori_loop(k, k + 1, project, 0)
        red_out.send(k)
    gain_mlp = row_vector(r.small_all, 14)
    mixed = r.mixed[...]
    inv_mid = rms_scale(mixed)
    unit_mid = mixed * inv_mid
    r.held[...] = unspread(red_normed.result(), r.spread[...])
    grad_normed = r.held[...]
    store_rows(r.small_grads, 14, jnp.sum(grad_normed * unit_mid, axis=0, keepdims=True))
    scaled = grad_normed * gain_mlp
    r.grad_mixed[...] = r.cot[...].astype(F32) + inv_mid * (
        scaled - unit_mid * jnp.mean(scaled * unit_mid, axis=-1, keepdims=True)
    )
    r.low_b[...] = r.grad_mixed[...].astype(BF16)
    wide = dot_nt(r.low_b[...], r.w_o[...].reshape(DPAD, D)).astype(BF16)
    r.held[...] = dot_nt(wide, r.spread[...])
    scatter_heads(lambda mb, t: r.held[64 * mb : 64 * mb + 64, 128 * t : 128 * t + 128], r.grad_heads)
    for mb in range(MB):
        r.values_t[mb] = jnp.transpose(r.keys[mb].astype(F32)).astype(BF16)
    for k in NEAR + (0,):
        red_out.forward(k)

    def attend_back(mb):
        def step(t, carry):
            i = mb * 7 + t
            grad_probs = dot_nt(r.values[mb], r.grad_heads[i])
            probs = r.probs[i].astype(F32)
            weighted = probs * grad_probs
            inner = jnp.sum(weighted, axis=0, keepdims=True)
            grad_scores = (weighted - probs * inner).astype(BF16)
            r.big[i] = grad_scores
            r.grad_query[i] = collect_heads(dot(r.values_t[mb], grad_scores), t)
            return carry

        lax.fori_loop(0, 7, step, 0)

    def grad_key_value(i, carry):
        mb, y = i // 4, lax.rem(i, 4)
        at = pl.ds(pl.multiple_of(256 * y, 256), 256)
        scores = jnp.concatenate([r.big[mb * 7 + t, at, :] for t in range(7)], axis=1)
        probs = jnp.concatenate([r.probs[mb * 7 + t, at, :] for t in range(7)], axis=1)
        grad_keys = dot(scores, r.heads[pl.ds(7 * mb, 7)].reshape(896, 128))
        grad_values = dot(probs, r.grad_heads[pl.ds(7 * mb, 7)].reshape(896, 128))
        r.kv_all[mb, y, :, :, :128] = grad_keys.astype(BF16).reshape(4, 64, 128)
        r.kv_all[mb, y, :, :, 128:] = grad_values.astype(BF16).reshape(4, 64, 128)
        return carry

    ring_kv = ReduceCtx(p, lambda h, y, x: r.kv_all.at[h, y, x], r.kv_bufs, r.kv_red_sems)
    for mb in range(MB):
        attend_back(mb)
        lax.fori_loop(4 * mb, 4 * mb + 4, grad_key_value, 0)
        ring_kv.start((mb,))
    ring_gu.forward()

    def weight_gradient(left, right, out):
        def step(i, carry):
            at = pl.ds(pl.multiple_of(256 * i, 256), 256)
            part = dot_tn(left[:, at], right[...]).astype(BF16)
            out[i // 2, pl.ds(2 * lax.rem(i, 2), 2)] = part.reshape(2, 4, 2, 16, part.shape[-1])
            return carry

        lax.fori_loop(0, 4, step, 0)

    def to_mate(n, grads, got):
        c = remote(grads.at[1 - p.core], got, r.s_mate.at[n], r.r_mate.at[n], {"dp": p.mate()})
        c.start()
        return c

    def with_mate(c, grads, got):
        c.wait_recv()
        for y in range(4):
            got[y] = (grads[p.core, y].astype(F32) + got[y].astype(F32)).astype(BF16)

    weight_gradient(r.attended_wide, r.low_b, r.g_wo)
    mate_wo = to_mate(0, r.g_wo, r.m_wo)
    ring_kv.forward()
    build_columns(r.big)
    r.layer_out[...] = (mixed + red_out.result()).astype(BF16)
    cosine, sine = r.cosine[...], r.sine[...]
    for t in range(7):
        tile = jnp.concatenate([r.grad_query[t], r.grad_query[7 + t]], axis=0) * (HEAD_SIZE**-0.5)
        r.low_a[:, 128 * t : 128 * t + 128] = rotate_back(tile, cosine, sine).astype(BF16)
    weight_gradient(r.normed_in, r.low_a, r.g_wq)
    mate_wq = to_mate(1, r.g_wq, r.m_wq)
    with_mate(mate_wo, r.g_wo, r.m_wo)
    ring_wo = ReduceCtx(p, lambda h, y, x: r.m_wo.at[y, x, h], r.wo_bufs, r.wo_sems)
    ring_wo.start()
    with_mate(mate_wq, r.g_wq, r.m_wq)
    ring_wq = ReduceCtx(p, lambda h, y, x: r.m_wq.at[y, x, h], r.wq_bufs, r.wq_sems)
    ring_wq.start()
    store_rows(r.small_grads, 7, jnp.sum(r.low_a[...].astype(F32), axis=0, keepdims=True))
    kv_sum = jnp.concatenate([ring_kv.result(0), ring_kv.result(1)], axis=0)
    grad_key = rotate_back(kv_sum[:, :128], cosine, sine).astype(BF16)
    r.low_kv[:, :128] = grad_key
    r.low_kv[:, 128:] = kv_sum[:, 128:].astype(BF16)
    weight_gradient(r.normed_in, r.low_kv, r.g_wkv)
    mate_wkv = to_mate(2, r.g_wkv, r.m_wkv)
    ring_wo.forward()
    with_mate(mate_wkv, r.g_wkv, r.m_wkv)
    ring_wkv = ReduceCtx(p, lambda h, y, x: r.m_wkv.at[y, x, h], r.wkv_bufs, r.wkv_sems)
    ring_wkv.start()
    bias_kv = jnp.sum(r.low_kv[...].astype(F32), axis=0, keepdims=True)
    store_rows(r.small_grads, 21, bias_kv)
    r.small_grads[23:24, :] = jnp.zeros((1, 128), F32)
    lowered = jnp.concatenate([r.low_a[...], r.low_kv[...]], axis=1)
    r.held[...] = unspread(dot_nt(lowered, r.w_qkv[...].reshape(DPAD, 1152)), r.spread[...])
    residual = r.hidden[...].astype(F32)
    inv_rms = rms_scale(residual)
    unit_in = residual * inv_rms
    store_rows(r.small_grads, 0, jnp.sum(r.held[...] * unit_in, axis=0, keepdims=True))
    small = SmallSum(p, r.small_grads, r.small_bufs2, r.small_sems2)
    small.start()
    ring_wkv.forward()
    ring_wq.forward()
    for h in (0, 1):
        part = ring_gu.result(h)
        for z in range(4):
            r.gu_out[z, h] = part[8 * z : 8 * z + 8]
    gu_copies = []
    for k in range(1, 8):
        to = p.dpindex(k)
        gu_copies.append(
            remote(
                r.gu_out.at[to // 2, lax.rem(to, 2)], r.gu_got.at[p.dp], r.s_ggu.at[k], r.r_ggu.at[k], {"dp": to}
            )
        )
    start_all(gu_copies)
    r.gu_got[p.dp] = r.gu_out[p.z, p.core]
    small.along_y()
    arrive_all(down_copies)
    total = r.g_down[pl.ds(pl.multiple_of(160 * p.y, 32), 160), :].astype(F32)
    for k in NEAR:
        total = total + r.down_y[k - 1].astype(F32)
    for i in range(4):
        r.down_mid[i] = total[40 * i : 40 * i + 40]
    down_copies2 = start_all(
        [
            remote(r.down_mid.at[p.at_x(k)], r.down_x.at[k - 1], r.s_gdown.at[1, k], r.r_gdown.at[1, k], p.xpeer(k))
            for k in NEAR
        ]
    )
    scaled = r.held[...] * row_vector(r.small_all, 0)
    r.grad_in[...] = r.grad_mixed[...] + inv_rms * (
        scaled - unit_in * jnp.mean(scaled * unit_in, axis=-1, keepdims=True)
    )
    small.along_dp()
    sum_wo = ZSum(p, ring_wo, r.zo_bufs, r.zo_sems)
    sum_wo.start()
    sum_wq = ZSum(p, ring_wq, r.zq_bufs, r.zq_sems)
    sum_wq.start()
    sum_wkv = ZSum(p, ring_wkv, r.zkv_bufs, r.zkv_sems)
    sum_wkv.start()
    arrive_all(gu_copies)
    for n, out in enumerate((r.o_gate, r.o_up)):
        for d in range(8):
            r.stage[8 * d : 8 * d + 8, :] = r.gu_got[d, :, 640 * n : 640 * n + 640]
        wide = r.stage[...]
        high = wide.astype(BF16)
        low = (wide - high.astype(F32)).astype(BF16)
        packed = dot_nt(high, columns_of(r.big)) + dot_nt(low, columns_of(r.big))
        for d in range(8):
            out[:, 608 * d : 608 * d + 608] = packed[8 * d : 8 * d + 7, :608]
    arrive_all(down_copies2)
    final = r.down_mid[p.x] + r.down_x[0] + r.down_x[1] + r.down_x[2]
    r.o_down[...] = final[:38]
    r.o_output[...] = sum_wo.result()[:7]
    r.o_query[...] = sum_wq.result()[:7]
    part = sum_wkv.result()
    r.o_key[...] = part[:7, :128]
    r.o_value[...] = part[:7, 128:]
    total = small.result()
    r.o_small[...] = total
    me = p.dp * 16 + p.ctx
    flat = lax.broadcasted_iota(jnp.int32, (7, 128), 0) * 128 + lax.broadcasted_iota(jnp.int32, (7, 128), 1)
    lane = lax.broadcasted_iota(jnp.int32, (1, 128), 1)

    def pick(block, where):
        return jnp.sum(jnp.sum(jnp.where(where, block, 0.0), axis=0, keepdims=True), axis=1, keepdims=True)

    r.o_mine[...] = jnp.zeros_like(r.o_mine)
    for n in range(3):
        row = jnp.zeros((1, 128), F32)
        for i in range(7):
            row = row + jnp.where(lane == i, pick(total[7 * n : 7 * n + 7], flat == me * 7 + i), 0.0)
        r.o_mine[n : n + 1, :] = row
    r.o_mine[3:4, :] = jnp.broadcast_to(pick(total[22:23], lane == me), (1, 128))
    red_out.sent()
    for ring in (*rings, red_normed, red_out, ring_gu, ring_kv, ring_wo, ring_wq, ring_wkv, small, sum_wo, sum_wq, sum_wkv):
        ring.finish()
    sent_all([mate_wo, mate_wq, mate_wkv] + down_copies + down_copies2 + gu_copies)


LAYER_OUTS = {
    "layer_out": shape((128, D), BF16),
    "grad_in": shape((128, D), F32),
    "o_query": shape((7, D), F32),
    "o_key": shape((7, 128), F32),
    "o_value": shape((7, 128), F32),
    "o_output": shape((7, D), F32),
    "o_gate": shape((7, 4864), F32),
    "o_up": shape((7, 4864), F32),
    "o_down": shape((38, D), F32),
    "o_small": shape((24, 128), F32),
    "o_mine": shape((8, 128), F32),
}
BACK_SCRATCH = {
    "big": VM((15, 1024, 128), BF16),
    "part_normed": VM((4, 2, 128, DPAD), BF16),
    "normed_bufs": ReduceDp.scratch(128, DPAD), "normed_sems": ReduceDp.SEMS,
    "out_bufs": ReduceDp.scratch(128, D), "out_sems": ReduceDp.SEMS,
    "g_gu": VM((2, 4, 4, 32, 1280), BF16),
    "gu_bufs": ReduceCtx.scratch(32, 1280), "gu_red_sems": ReduceCtx.SEMS,
    "g_down": VM((640, D), BF16),
    "down_y": VM((3, 160, D), BF16), "down_mid": VM((4, 40, D), F32), "down_x": VM((3, 40, D), F32),
    "grad_mixed": VM((128, D), F32),
    "held": VM((128, D), F32),
    "low_a": VM((128, D), BF16),
    "low_b": VM((128, D), BF16),
    "low_kv": VM((128, 256), BF16),
    "grad_heads": VM((14, 128, 128), BF16),
    "grad_query": VM((14, 64, 128), F32),
    "kv_bufs": ReduceCtx.scratch(64, 256), "kv_red_sems": ReduceCtx.SEMS,
    "g_wo": VM((2, 4, 4, 2, 16, D), BF16), "m_wo": VM((4, 4, 2, 16, D), BF16),
    "g_wq": VM((2, 4, 4, 2, 16, D), BF16), "m_wq": VM((4, 4, 2, 16, D), BF16),
    "g_wkv": VM((2, 4, 4, 2, 16, 256), BF16), "m_wkv": VM((4, 4, 2, 16, 256), BF16),
    "wo_bufs": ReduceCtx.scratch(16, D), "wo_sems": ReduceCtx.SEMS,
    "wq_bufs": ReduceCtx.scratch(16, D), "wq_sems": ReduceCtx.SEMS,
    "wkv_bufs": ReduceCtx.scratch(16, 256), "wkv_sems": ReduceCtx.SEMS,
    "zo_bufs": ZSum.scratch(D), "zo_sems": ZSum.SEMS,
    "zq_bufs": ZSum.scratch(D), "zq_sems": ZSum.SEMS,
    "zkv_bufs": ZSum.scratch(256), "zkv_sems": ZSum.SEMS,
    "small_grads": VM((24, 128), F32),
    "small_bufs2": SmallSum.SCRATCH, "small_sems2": SmallSum.SEMS,
    "gu_out": VM((4, 2, 8, 1280), F32), "gu_got": VM((8, 8, 1280), F32),
    "s_mate": DMA((3,)), "r_mate": DMA((3,)), "s_gdown": DMA((2, 4)), "r_gdown": DMA((2, 4)),
    "s_ggu": DMA((8,)), "r_ggu": DMA((8,)),
}


WHOLE = ("layer_out", "grad_in", "o_query", "o_key", "o_value", "o_output", "o_gate", "o_up", "o_down")
VECTORS = {"norm_attn": 7, "b_query": 7, "norm_mlp": 7, "b_value": 1, "b_key": 128}


def finish(done):
    def kernel(*refs):
        count = len(WHOLE)
        sources, (mine, sums) = refs[:count], refs[count : count + 2]
        targets, vectors = refs[count + 2 : 2 * count + 2], refs[2 * count + 2 :]
        for source, target in zip(sources, targets):
            target[...] = source[...]
        for n in range(3):
            vectors[n][...] = mine[n, :7]
        vectors[3][...] = mine[3, :1]
        vectors[4][...] = sums[21]

    fast = pl.BlockSpec(memory_space=VM)
    results = pl.pallas_call(
        kernel,
        out_shape=tuple(LAYER_OUTS[key] for key in WHOLE) + tuple(shape((n,), F32) for n in VECTORS.values()),
        in_specs=[fast] * (len(WHOLE) + 2),
        out_specs=tuple([fast] * (len(WHOLE) + len(VECTORS))),
        name="finish",
        compiler_params=pltpu.CompilerParams(vmem_limit_bytes=63 << 20),
    )(*(done[key] for key in WHOLE), done["o_mine"], done["o_small"])
    return dict(zip(WHOLE + tuple(VECTORS), results))


def layer(r):
    p = Place()
    back(r, p, front(r, p))


def body(
    hidden_in, positions, norm_attn, w_query, b_query, w_key, b_key, value_weight, value_bias, w_output,
    norm_mlp, w_gate, w_up, w_down, cotangent,
):
    rows = MB * 64
    inputs = {
        "hidden": hidden_in.reshape(rows, D),
        "cot": cotangent.reshape(rows, D),
        "positions": positions,
        "norm_attn": norm_attn, "b_query": b_query, "norm_mlp": norm_mlp, "b_key": b_key, "value_bias": value_bias,
        "w_query": w_query, "w_key": w_key, "w_value": value_weight, "w_output": w_output,
        "w_gate": w_gate, "w_up": w_up, "w_down_own": w_down,
    }
    done = call(layer, inputs, LAYER_OUTS, {**FRONT_SCRATCH, **BACK_SCRATCH}, 0, "layer")
    done = finish(done)
    return (
        done["layer_out"].reshape(MB, 1, 64, D),
        done["grad_in"].reshape(MB, 1, 64, D),
        done["norm_attn"],
        done["o_query"],
        done["b_query"],
        done["o_key"],
        done["b_key"],
        done["o_value"],
        done["b_value"],
        done["o_output"],
        done["norm_mlp"],
        done["o_gate"],
        done["o_up"],
        done["o_down"],
    )


def solution(mesh):
    rows = P(("dp", "ctx"), None)
    vector = P(("dp", "ctx"))
    tokens = P(None, "dp", "ctx", None)
    in_specs = (
        tokens, P(None, "dp", "ctx"), vector, rows, vector, rows, vector, rows, vector, rows, vector,
        rows, rows, rows, tokens,
    )
    out_specs = (
        tokens, tokens, vector, rows, vector, rows, P(), rows, vector, rows, vector, rows, rows, rows,
    )
    return jax.shard_map(body, mesh=mesh, in_specs=in_specs, out_specs=out_specs, check_vma=False)
```

```python
import math
import types

import jax
import jax.numpy as jnp
from jax import lax
from jax.experimental import pallas as pl
from jax.experimental.pallas import tpu as pltpu
from jax.sharding import PartitionSpec as P

QUERY_HEADS = 14
KEY_VALUE_HEADS = 2
HEAD_SIZE = 64
GROUP = QUERY_HEADS // KEY_VALUE_HEADS
MB = 2
D = 896
DPAD = 1024
EPSILON = 1e-06
THETA_BASE = 1000000.0
F32 = jnp.float32
BF16 = jnp.bfloat16
MESH = pl.DeviceIdType.MESH
DMA = pltpu.SemaphoreType.DMA
VM = pltpu.VMEM


def remote(src, dst, ss, rs, peer):
    return pltpu.make_async_remote_copy(
        src_ref=src, dst_ref=dst, send_sem=ss, recv_sem=rs, device_id=peer, device_id_type=MESH
    )


def greet(peers):
    sem = pltpu.get_barrier_semaphore()
    for peer in peers:
        pl.semaphore_signal(sem, inc=1, device_id=peer, device_id_type=MESH)


def meet(peers):
    pl.semaphore_wait(pltpu.get_barrier_semaphore(), len(peers))


class Place:
    def __init__(self):
        self.dp = lax.axis_index("dp")
        self.ctx = lax.axis_index("ctx")
        self.y, self.x = self.ctx // 4, lax.rem(self.ctx, 4)
        self.z, self.core = self.dp // 2, lax.rem(self.dp, 2)

    def at_x(self, k):
        return lax.rem(self.x + (k + 4), 4)

    def at_y(self, k):
        return lax.rem(self.y + (k + 4), 4)

    def at_z(self, k):
        return lax.rem(self.z + (k + 4), 4)

    def line(self, axis, k):
        return self.y * 4 + self.at_x(k) if axis == 0 else self.at_y(k) * 4 + self.x

    def xpeer(self, k):
        return {"ctx": self.line(0, k)}

    def ypeer(self, k):
        return {"ctx": self.line(1, k)}

    def peer(self, axis, k):
        return {"ctx": self.line(axis, k)}

    def zindex(self, k):
        return self.at_z(k) * 2 + self.core

    def mate(self):
        return self.z * 2 + 1 - self.core

    def dpindex(self, k):
        return lax.rem(self.dp + k, 8)


NEAR = (1, 3, 2)


class GatherCtx:
    SEMS = [DMA((2, 4)), DMA((2, 4)), DMA((2, 4, 4)), DMA((2, 4, 4)), DMA((2,))]
    MATE = [DMA((2, 4, 4)), DMA((2, 4, 4))]

    def __init__(self, place, src, dst_at, sems, mate=None):
        self.p, self.src, self.dst_at, self.sems, self.mate = place, src, dst_at, sems, mate
        self.mated = []

    def block(self, h, j, k):
        p = self.p
        return p.at_y(-k) * 4 + p.at_x(-j) if h == 0 else p.at_y(-j) * 4 + p.at_x(-k)

    def share(self, h, j, k):
        if self.mate is None:
            return
        dst = self.dst_at(self.block(h, j, k), h)
        src = self.src.at[h] if j == 0 and k == 0 else dst
        c = remote(src, dst, self.mate[0].at[h, j, k], self.mate[1].at[h, j, k], {"dp": self.p.mate()})
        c.start()
        self.mated.append(c)

    def start(self):
        p, (s1, r1, s2, r2, ls) = self.p, self.sems
        self.local = []
        for h in (0, 1):
            c = pltpu.make_async_copy(self.src.at[h], self.dst_at(p.ctx, h), ls.at[h])
            c.start()
            self.local.append(c)
        self.first = {}
        for k in NEAR:
            for h in (0, 1):
                c = remote(self.src.at[h], self.dst_at(p.ctx, h), s1.at[h, k], r1.at[h, k], p.peer(h, k))
                c.start()
                self.first[h, k] = c
        for h in (0, 1):
            self.share(h, 0, 0)

    def forward(self):
        p, (s1, r1, s2, r2, ls) = self.p, self.sems
        self.second = {}
        for j in (0,) + NEAR:
            for h in (0, 1):
                if j:
                    self.first[h, j].wait_recv()
                dst = self.dst_at(p.line(h, -j), h)
                src = self.src.at[h] if j == 0 else dst
                for k in NEAR:
                    c = remote(src, dst, s2.at[h, j, k], r2.at[h, j, k], p.peer(1 - h, k))
                    c.start()
                    self.second[h, j, k] = c
                if j:
                    self.share(h, j, 0)

    def arrive(self):
        for c in self.local:
            c.wait()
        for (h, j, k), c in self.second.items():
            c.wait_recv()
            self.share(h, j, k)
        for c in self.mated:
            c.wait_recv()

    def finish(self):
        for c in list(self.first.values()) + list(self.second.values()) + self.mated:
            c.wait_send()


class ReduceCtx:
    SEMS = [DMA((2, 4)), DMA((2, 4)), DMA((2, 4)), DMA((2, 4))]

    @staticmethod
    def scratch(rows, cols):
        return [VM((2, 3, 4, rows, cols), BF16), VM((2, 3, rows, cols), BF16)]

    def __init__(self, place, src_at, bufs, sems):
        self.p, self.src_at, self.bufs, self.sems = place, src_at, bufs, sems
        self.first = {}

    def start(self, halves=(0, 1)):
        p, (s1, r1, s2, r2) = self.p, self.sems
        got = self.bufs[0]
        every = slice(None)
        for k in NEAR:
            for h in halves:
                src = self.src_at(0, p.at_y(k), every) if h == 0 else self.src_at(1, every, p.at_x(k))
                c = remote(src, got.at[h, k - 1], s1.at[h, k], r1.at[h, k], p.peer(1 - h, k))
                c.start()
                self.first[h, k] = c

    def forward(self):
        p, (s1, r1, s2, r2) = self.p, self.sems
        got, last = self.bufs
        self.second = {}
        for h in (0, 1):
            for k in NEAR:
                self.first[h, k].wait_recv()
            for i in range(4):
                own = self.src_at(0, p.y, i) if h == 0 else self.src_at(1, i, p.x)
                total = own[...].astype(F32)
                for k in NEAR:
                    total = total + got[h, k - 1, i].astype(F32)
                got[h, 0, i] = total.astype(BF16)
            for k in NEAR:
                to = p.at_x(k) if h == 0 else p.at_y(k)
                c = remote(got.at[h, 0, to], last.at[h, k - 1], s2.at[h, k], r2.at[h, k], p.peer(h, k))
                c.start()
                self.second[h, k] = c

    def result(self, h):
        p = self.p
        got, last = self.bufs
        for k in NEAR:
            self.second[h, k].wait_recv()
        total = got[h, 0, p.x if h == 0 else p.y].astype(F32)
        for k in NEAR:
            total = total + last[h, k - 1].astype(F32)
        return total

    def finish(self):
        for c in list(self.first.values()) + list(self.second.values()):
            c.wait_send()


class GatherDp:
    SEMS = [DMA((4,)), DMA((4,)), DMA((4,)), DMA((4,)), DMA]

    def __init__(self, place, src, dst_at, sems):
        self.p, self.src, self.dst_at, self.sems = place, src, dst_at, sems
        rows = src.shape[0]
        self.halves = {1: pl.ds(0, rows // 2), 3: pl.ds(rows // 2, rows // 2)}

    def start(self):
        p, (s1, r1, s2, r2, ls) = self.p, self.sems
        self.local = pltpu.make_async_copy(self.src, self.dst_at(p.dp), ls)
        self.local.start()
        self.first, self.second, self.relayed = {}, {}, {}
        for k in (1, 3):
            c = remote(self.src, self.dst_at(p.dp), s1.at[k], r1.at[k], {"dp": p.zindex(k)})
            c.start()
            self.first[k] = c

    def relay(self):
        p, (s1, r1, s2, r2, ls) = self.p, self.sems
        for k in (1, 3):
            self.first[k].wait_recv()
            part = self.dst_at(p.zindex(-k)).at[self.halves[k]]
            c = remote(part, part, s1.at[k - 1], r1.at[k - 1], {"dp": p.zindex(k)})
            c.start()
            self.relayed[k] = c

    def forward(self, j):
        p, (s1, r1, s2, r2, ls) = self.p, self.sems
        if j == 2:
            for c in self.relayed.values():
                c.wait_recv()
        block = p.zindex(-j)
        src = self.dst_at(block) if j else self.src
        c = remote(src, self.dst_at(block), s2.at[j], r2.at[j], {"dp": p.mate()})
        c.start()
        self.second[j] = c

    def arrive(self, j):
        if j == 0:
            self.local.wait()
        self.second[j].wait_recv()

    def finish(self):
        for c in list(self.first.values()) + list(self.second.values()) + list(self.relayed.values()):
            c.wait_send()


class ReduceDp:
    SEMS = [DMA((4,)), DMA((4,)), DMA((4,)), DMA((4,))]

    @staticmethod
    def scratch(rows, cols):
        return [VM((4, rows, cols), BF16), VM((3, rows, cols), BF16)]

    def __init__(self, place, src, bufs, sems):
        self.p, self.src, self.bufs, self.sems = place, src, bufs, sems
        self.first, self.second = {}, {}

    def send(self, k):
        p, (s1, r1, s2, r2) = self.p, self.sems
        to = p.at_z(k)
        c = remote(self.src.at[to, 1 - p.core], self.bufs[0].at[to], s1.at[k], r1.at[k], {"dp": p.mate()})
        c.start()
        self.first[k] = c

    def forward(self, k):
        p, (s1, r1, s2, r2) = self.p, self.sems
        got, last = self.bufs
        to = p.at_z(k)
        self.first[k].wait_recv()
        total = self.src[to, p.core].astype(F32) + got[to].astype(F32)
        got[to] = total.astype(BF16)
        if k:
            c = remote(got.at[to], last.at[k - 1], s2.at[k], r2.at[k], {"dp": p.zindex(k)})
            c.start()
            self.second[k] = c

    def result(self):
        got, last = self.bufs
        total = got[self.p.z].astype(F32)
        for k in NEAR:
            self.second[k].wait_recv()
            total = total + last[k - 1].astype(F32)
        return total

    def sent(self):
        for c in self.first.values():
            c.wait_send()

    def finish(self):
        for c in self.second.values():
            c.wait_send()


def xy_peers(p):
    return [p.peer(axis, k) for axis in (0, 1) for k in NEAR]


def dp_peers(p):
    return [{"dp": p.dpindex(k)} for k in range(1, 8)]


def shape(dims, kind):
    return jax.ShapeDtypeStruct(dims, kind)


def call(phase, inputs, outs, scratch, cid, name):
    flat, where = [], {}
    for key, entry in scratch.items():
        entries = entry if isinstance(entry, list) else [entry]
        where[key] = (len(flat), len(entries), isinstance(entry, list))
        flat += entries

    def kernel(*refs):
        named = dict(zip(list(inputs) + list(outs), refs))
        tail = refs[len(inputs) + len(outs) :]
        for key, (start, count, many) in where.items():
            named[key] = list(tail[start : start + count]) if many else tail[start]
        phase(types.SimpleNamespace(**named))

    results = pl.pallas_call(
        kernel,
        out_shape=tuple(outs.values()),
        in_specs=[pl.BlockSpec(memory_space=VM)] * len(inputs),
        out_specs=tuple(pl.BlockSpec(memory_space=VM) for _ in outs),
        scratch_shapes=flat,
        name=name,
        compiler_params=pltpu.CompilerParams(
            collective_id=cid, has_side_effects=True, vmem_limit_bytes=63 << 20
        ),
    )(*inputs.values())
    return dict(zip(outs, results))


def dot(left, right):
    return jnp.dot(left, right, preferred_element_type=F32)


def dot_tn(left, right):
    return lax.dot_general(left, right, (((0,), (0,)), ((), ())), preferred_element_type=F32)


def dot_nt(left, right):
    return lax.dot_general(left, right, (((1,), (1,)), ((), ())), preferred_element_type=F32)


def rms_scale(values):
    return lax.rsqrt(jnp.mean(values * values, axis=-1, keepdims=True) + EPSILON)


def row_vector(ref, start):
    return jnp.concatenate([ref[start + i : start + i + 1, :] for i in range(7)], axis=1)


def store_rows(ref, start, vector):
    for i in range(vector.shape[1] // 128):
        ref[start + i : start + i + 1, :] = vector[:, 128 * i : 128 * i + 128]


def build_spread(ref):
    for part in range(7):
        source = lax.broadcasted_iota(jnp.int32, (128, DPAD), 0) + 128 * part
        column = lax.broadcasted_iota(jnp.int32, (128, DPAD), 1)
        inner = column & 7
        owner = ((column >> 3) & 3) * 2 + (column >> 9)
        wanted = (owner * 16 + ((column >> 5) & 15)) * 7 + inner
        ref[128 * part : 128 * part + 128, :] = jnp.where(
            (source == wanted) & (inner < 7), 1.0, 0.0
        ).astype(BF16)


def spread(values, matrix):
    return dot(values, matrix).astype(BF16)


def unspread(values, matrix):
    high = values.astype(BF16)
    low = (values - high.astype(F32)).astype(BF16)
    return dot_nt(high, matrix) + dot_nt(low, matrix)


def lanes(rows):
    return lax.broadcasted_iota(jnp.int32, (rows, 128), 1)


def half_turn(tile):
    first = (lanes(tile.shape[0]) & 63) < 32
    return jnp.where(first, pltpu.roll(tile, 96, 1), pltpu.roll(tile, 32, 1))


def rotate(tile, cosine, signed_sine):
    return tile * cosine + half_turn(tile) * signed_sine


def rotate_back(tile, cosine, signed_sine):
    return tile * cosine - half_turn(tile) * signed_sine


def scatter_heads(tile_of, dst):
    for mb in range(MB):
        for head in range(QUERY_HEADS):
            tile = tile_of(mb, head // 2)
            group = head // GROUP
            if head % 2 != group:
                tile = pltpu.roll(tile, 64, 1)
            tile = jnp.where((lanes(64) >= 64) == (group == 1), tile, 0.0)
            at = (head % 2) * 64
            dst[mb * 7 + head // 2, at : at + 64, :] = tile.astype(BF16)


def collect_heads(transposed, t):
    both = jnp.transpose(transposed)
    even, odd = both[:64], both[64:]
    even = jnp.where(t >= 4, pltpu.roll(even, 64, 1), even)
    odd = jnp.where(t <= 2, pltpu.roll(odd, 64, 1), odd)
    return jnp.where(lanes(64) < 64, even, odd)


def start_all(copies):
    for c in copies:
        c.start()
    return copies


def arrive_all(copies):
    for c in copies:
        c.wait_recv()


def sent_all(copies):
    for c in copies:
        c.wait_send()


class SmallSum:
    SCRATCH = [VM((3, 24, 128), F32), VM((3, 24, 128), F32), VM((7, 24, 128), F32), VM((2, 24, 128), F32)]
    SEMS = [DMA((3, 8)), DMA((3, 8))]

    def __init__(self, place, src, bufs, sems):
        self.p, self.src, self.bufs, self.sems = place, src, bufs, sems
        self.copies = []

    def start(self):
        p, (s, r) = self.p, self.sems
        self.x = start_all([remote(self.src, self.bufs[0].at[k - 1], s.at[0, k], r.at[0, k], p.xpeer(k)) for k in NEAR])

    def along_y(self):
        p, (s, r) = self.p, self.sems
        arrive_all(self.x)
        got, sums = self.bufs[0], self.bufs[3]
        sums[0] = self.src[...] + got[0] + got[1] + got[2]
        self.y = start_all(
            [remote(sums.at[0], self.bufs[1].at[k - 1], s.at[1, k], r.at[1, k], p.ypeer(k)) for k in NEAR]
        )

    def along_dp(self):
        p, (s, r) = self.p, self.sems
        arrive_all(self.y)
        got, sums = self.bufs[1], self.bufs[3]
        sums[1] = sums[0] + got[0] + got[1] + got[2]
        self.d = start_all(
            [
                remote(sums.at[1], self.bufs[2].at[k - 1], s.at[2, k], r.at[2, k], {"dp": p.dpindex(k)})
                for k in range(1, 8)
            ]
        )

    def result(self):
        arrive_all(self.d)
        total = self.bufs[3][1]
        for k in range(7):
            total = total + self.bufs[2][k]
        return total

    def finish(self):
        sent_all(self.x + self.y + self.d)


class ZSum:
    SEMS = [DMA((4,)), DMA((4,))]

    @staticmethod
    def scratch(cols):
        return [VM((4, 8, cols), F32), VM((4, 8, cols), F32)]

    def __init__(self, place, ring, bufs, sems):
        self.p, self.ring, self.bufs, self.sems = place, ring, bufs, sems

    def start(self):
        p, (s, r), (out, got) = self.p, self.sems, self.bufs
        for h in (0, 1):
            part = self.ring.result(h)
            out[2 * h], out[2 * h + 1] = part[:8], part[8:]
        self.copies = start_all(
            [remote(out.at[p.at_z(k)], got.at[p.z], s.at[k], r.at[k], {"dp": p.zindex(k)}) for k in NEAR]
        )
        got[p.z] = out[p.z]

    def result(self):
        arrive_all(self.copies)
        got = self.bufs[1]
        return got[0] + got[1] + got[2] + got[3]

    def finish(self):
        sent_all(self.copies)


def build_columns(big):
    for t in range(5):
        column = lax.broadcasted_iota(jnp.int32, (640, 128), 1) + 128 * t
        source = lax.broadcasted_iota(jnp.int32, (640, 128), 0)
        owner = (column * 1639) >> 16
        inner = column - owner * 40
        big[t, :640, :] = jnp.where((source == owner * 38 + inner) & (inner < 38), 1.0, 0.0).astype(BF16)


def columns_of(big):
    return jnp.concatenate([big[t, :640, :] for t in range(5)], axis=1)


def front(r, p):
    peers = xy_peers(p) + dp_peers(p)
    greet(peers)
    r.attn_src[...] = jnp.zeros_like(r.attn_src)
    r.stage[...] = jnp.zeros_like(r.stage)
    r.down[...] = jnp.zeros_like(r.down)
    r.down[:38, :] = r.w_down_own[...].astype(F32)
    r.attn_src[:7, :896] = r.w_query[...].astype(F32)
    r.attn_src[:7, 896:1024] = r.w_key[...].astype(F32)
    r.attn_src[:7, 1024:1152] = r.w_value[...].astype(F32)
    r.attn_src[:7, 1152:] = r.w_output[...].astype(F32)
    r.small[...] = jnp.zeros_like(r.small)
    me = p.dp * 16 + p.ctx
    flat = lax.broadcasted_iota(jnp.int32, (7, 128), 0) * 128 + lax.broadcasted_iota(jnp.int32, (7, 128), 1)
    for n, ref in enumerate((r.norm_attn, r.b_query, r.norm_mlp)):
        vector = ref[...].astype(F32)[None]
        total = jnp.zeros((7, 128), F32)
        for i in range(7):
            total = total + jnp.where(flat == me * 7 + i, vector[:, i : i + 1], 0.0)
        r.small[7 * n : 7 * n + 7, :] = total
    for n, ref in enumerate((r.b_key, r.value_bias)):
        r.small[21 + n : 22 + n, :] = jnp.where(flat[:1] == me, ref[...].astype(F32)[None], 0.0)
    r.places[...] = jnp.zeros_like(r.places)
    for at in (0, 64):
        r.places[:MB, at : at + 64] = r.positions[:, 0].astype(F32)
    meet(peers)
    attn_copies = start_all(
        [remote(r.attn_src, r.attn_in.at[p.z], r.s_attn.at[k], r.r_attn.at[k], {"dp": p.zindex(k)}) for k in NEAR]
    )
    small = SmallSum(p, r.small, r.small_bufs, r.small_sems)
    small.start()
    place_copies = start_all(
        [remote(r.places, r.places_x.at[p.x], r.s_place.at[0, k], r.r_place.at[0, k], p.xpeer(k)) for k in NEAR]
    )
    r.attn_in[p.z] = r.attn_src[...]
    r.places_x[p.x] = r.places[...]
    build_columns(r.big)
    for n, ref in enumerate((r.w_gate, r.w_up)):
        whole = ref[...].astype(F32)
        for d in range(8):
            r.stage[8 * d : 8 * d + 7, :608] = whole[:, 608 * d : 608 * d + 608]
        wide = dot(r.stage[...].astype(BF16), columns_of(r.big))
        for d in range(8):
            r.gate_up[d, :, 640 * n : 640 * n + 640] = wide[8 * d : 8 * d + 8]
    gu_copies = []
    for k in range(1, 8):
        to = p.dpindex(k)
        gu_copies.append(
            remote(r.gate_up.at[to], r.gu_in.at[p.core, p.z], r.s_gu.at[k], r.r_gu.at[k], {"dp": to})
        )
    start_all(gu_copies)
    r.gu_in[p.core, p.z] = r.gate_up[p.dp]
    cots = GatherDp(p, r.cot, lambda b: r.cot_all.at[b], r.cot_sems)
    cots.start()
    arrive_all(attn_copies)
    for h in (0, 1):
        pair = jnp.concatenate([r.attn_in[2 * h], r.attn_in[2 * h + 1]], axis=0).astype(BF16)
        r.qkv_block[h] = pair[:, :1152]
        r.o_block[h] = pair[:, 1152:]
    ring_qkv = GatherCtx(p, r.qkv_block, lambda b, h: r.w_qkv.at[p.core, b, h], r.qkv_sems, r.qkv_mate)
    ring_qkv.start()
    small.along_y()
    arrive_all(place_copies)
    place_copies2 = start_all(
        [remote(r.places_x, r.places_all.at[p.y], r.s_place.at[1, k], r.r_place.at[1, k], p.ypeer(k)) for k in NEAR]
    )
    r.places_all[p.y] = r.places_x[...]
    ring_qkv.forward()
    ring_o = GatherCtx(p, r.o_block, lambda b, h: r.w_o.at[p.core, b, h], r.o_sems, r.o_mate)
    ring_o.start()
    build_spread(r.spread)
    inner = lanes(1) & 63
    freqs = jnp.exp((inner & 31).astype(F32) * (-math.log(THETA_BASE) / 32))
    sign = jnp.where(inner < 32, -1.0, 1.0)
    for mb in range(MB):
        angles = jnp.transpose(jnp.broadcast_to(r.places[mb : mb + 1, :], (128, 128)))[:64] * freqs
        r.cosine[64 * mb : 64 * mb + 64, :] = jnp.cos(angles)
        r.sine[64 * mb : 64 * mb + 64, :] = jnp.sin(angles) * sign
    small.along_dp()
    arrive_all(gu_copies)
    for c in (0, 1):
        r.gu_block[c] = jnp.concatenate([r.gu_in[c, z] for z in range(4)], axis=0).astype(BF16)
    ring_gu = GatherCtx(p, r.gu_block, lambda b, h: r.w_gu.at[h, b], r.gu_sems)
    ring_gu.start()
    down_copies = start_all(
        [remote(r.down, r.down_in.at[p.x], r.s_down.at[0, k], r.r_down.at[0, k], p.xpeer(k)) for k in NEAR]
    )
    r.down_in[p.x] = r.down[...]
    cots.relay()
    for j in (0, 1, 3):
        cots.forward(j)
    residual = r.hidden[...].astype(F32)
    unit_in = residual * rms_scale(residual)
    arrive_all(place_copies2)
    low_lane = lanes(8) < 64
    for c in range(8):
        a, b = r.places_all[(2 * c) // 4, (2 * c) % 4], r.places_all[(2 * c + 1) // 4, (2 * c + 1) % 4]
        r.key_row[:, 128 * c : 128 * c + 128] = jnp.where(low_lane, a, b)
    for mb in range(MB):
        key_places = jnp.transpose(jnp.broadcast_to(r.key_row[mb : mb + 1, :], (128, 1024)))
        r.masked[mb] = jnp.where(key_places <= r.places[mb : mb + 1, :], 0.0, -1e30).astype(BF16)
    r.small_all[...] = small.result()
    r.normed_in[...] = spread((unit_in * row_vector(r.small_all, 0)).astype(BF16), r.spread[...])
    bias_query = row_vector(r.small_all, 7)
    ring_qkv.arrive()
    ring_o.forward()
    cosine, sine = r.cosine[...], r.sine[...]
    lin = dot(r.normed_in[...], r.w_qkv[:, :, :, :, 896:].reshape(DPAD, 256))
    keys = rotate(lin[:, :128] + r.small_all[21:22, :], cosine, sine).astype(BF16)
    values = (lin[:, 128:] + r.small_all[22:23, :]).astype(BF16)
    for mb in range(MB):
        r.kv[mb, :, :128] = keys[64 * mb : 64 * mb + 64]
        r.kv[mb, :, 128:] = values[64 * mb : 64 * mb + 64]
    ring_kv = GatherCtx(p, r.kv, lambda b, h: r.kv_all.at[h, b // 4, lax.rem(b, 4)], r.kv_sems)
    ring_kv.start()
    lin = dot(r.normed_in[...], r.w_qkv[:, :, :, :, :896].reshape(DPAD, D))
    query_tiles = []
    for t in range(7):
        tile = lin[:, 128 * t : 128 * t + 128] + bias_query[:, 128 * t : 128 * t + 128]
        query_tiles.append((rotate(tile, cosine, sine).astype(BF16)).astype(F32) * (HEAD_SIZE**-0.5))
    scatter_heads(lambda mb, t: query_tiles[t][64 * mb : 64 * mb + 64], r.heads)
    ring_kv.forward()
    ring_gu.forward()
    arrive_all(down_copies)
    own_down = r.w_down.at[pl.ds(pl.multiple_of(160 * p.y, 32), 160)]
    own_down[...] = jnp.concatenate([r.down_in[i] for i in range(4)], axis=0).astype(BF16)
    down_copies2 = start_all(
        [remote(own_down, own_down, r.s_down.at[1, k], r.r_down.at[1, k], p.ypeer(k)) for k in NEAR]
    )
    ring_kv.arrive()
    for mb in range(MB):
        r.keys[mb] = r.kv_all[mb, :, :, :, :128].reshape(1024, 128)
        r.values[mb] = r.kv_all[mb, :, :, :, 128:].reshape(1024, 128)
        r.values_t[mb] = jnp.transpose(r.values[mb].astype(F32)).astype(BF16)

    def attend(mb):
        def step(t, carry):
            i = mb * 7 + t
            scores = dot_nt(r.keys[mb], r.heads[i]) + r.masked[mb].astype(F32)
            expo = jnp.exp(scores - jnp.max(scores, axis=0, keepdims=True))
            probs = (expo * (1.0 / jnp.sum(expo, axis=0, keepdims=True))).astype(BF16)
            r.probs[i] = probs
            r.attended[i] = collect_heads(dot(r.values_t[mb], probs), t).astype(BF16)
            return carry

        lax.fori_loop(0, 7, step, 0)

    gain_mlp = row_vector(r.small_all, 14)
    rings = []

    def finish_rows(mb):
        at = slice(64 * mb, 64 * mb + 64)
        attended = jnp.concatenate([r.attended[mb * 7 + t] for t in range(7)], axis=1)
        r.attended_wide[at, :] = spread(attended, r.spread[...])
        mixed = residual[at] + dot(r.attended_wide[at, :], r.w_o[...].reshape(DPAD, D))
        r.mixed[at, :] = mixed
        unit_mid = mixed * rms_scale(mixed)
        r.normed_mid[mb] = spread((unit_mid * gain_mlp).astype(BF16), r.spread[...])
        ring = GatherDp(p, r.normed_mid.at[mb], lambda b: r.normed_all.at[b, mb], r.mid_sems[5 * mb : 5 * mb + 5])
        ring.start()
        ring.forward(0)
        rings.append(ring)

    attend(0)
    ring_o.arrive()
    finish_rows(0)
    cots.forward(2)
    attend(1)
    finish_rows(1)
    rings[0].relay()
    ring_gu.arrive()
    arrive_all(down_copies2)
    for j in range(4):
        cots.arrive(j)
    for ring in (ring_qkv, ring_o, ring_kv, ring_gu, cots, small):
        ring.finish()
    sent_all(attn_copies + gu_copies + place_copies + place_copies2 + down_copies + down_copies2)
    return rings


FRONT_SCRATCH = {
    "places": VM((8, 128), F32),
    "cosine": VM((128, 128), F32),
    "sine": VM((128, 128), F32),
    "attn_src": VM((8, 2048), F32),
    "stage": VM((64, 640), F32),
    "gate_up": VM((8, 8, 1280), F32),
    "down": VM((40, D), F32),
    "small": VM((24, 128), F32),
    "attn_in": VM((4, 8, 2048), F32),
    "gu_in": VM((2, 4, 8, 1280), F32),
    "down_in": VM((4, 40, D), F32),
    "places_x": VM((4, 8, 128), F32),
    "places_all": VM((4, 4, 8, 128), F32),
    "key_row": VM((8, 1024), F32),
    "masked": VM((2, 1024, 128), BF16),
    "qkv_block": VM((2, 16, 1152), BF16),
    "o_block": VM((2, 16, D), BF16),
    "gu_block": VM((2, 32, 1280), BF16),
    "kv": VM((2, 64, 256), BF16),
    "kv_all": VM((2, 4, 4, 64, 256), BF16),
    "values_t": VM((2, 128, 1024), BF16),
    "attended": VM((14, 64, 128), BF16),
    "normed_mid": VM((2, 64, DPAD), BF16),
    "w_qkv": VM((2, 16, 2, 16, 1152), BF16),
    "w_o": VM((2, 16, 2, 16, D), BF16),
    "w_gu": VM((2, 16, 32, 1280), BF16),
    "w_down": VM((640, D), BF16),
    "small_all": VM((24, 128), F32),
    "cot_all": VM((8, 128, D), BF16),
    "normed_all": VM((8, 2, 64, DPAD), BF16),
    "probs": VM((14, 1024, 128), BF16),
    "heads": VM((14, 128, 128), BF16),
    "keys": VM((2, 1024, 128), BF16),
    "values": VM((2, 1024, 128), BF16),
    "attended_wide": VM((128, DPAD), BF16),
    "normed_in": VM((128, DPAD), BF16),
    "mixed": VM((128, D), F32),
    "spread": VM((D, DPAD), BF16),
    "small_bufs": SmallSum.SCRATCH,
    "small_sems": SmallSum.SEMS,
    "s_attn": DMA((4,)), "r_attn": DMA((4,)), "s_gu": DMA((8,)), "r_gu": DMA((8,)),
    "s_place": DMA((2, 4)), "r_place": DMA((2, 4)), "s_down": DMA((2, 4)), "r_down": DMA((2, 4)),
    "qkv_sems": GatherCtx.SEMS, "qkv_mate": GatherCtx.MATE, "o_sems": GatherCtx.SEMS, "o_mate": GatherCtx.MATE,
    "kv_sems": GatherCtx.SEMS, "gu_sems": GatherCtx.SEMS, "cot_sems": GatherDp.SEMS, "mid_sems": GatherDp.SEMS * 2,
}


def back(r, p, rings):
    red_normed = ReduceDp(p, r.part_normed, r.normed_bufs, r.normed_sems)
    red_out = ReduceDp(p, r.part_normed.at[:, :, :, pl.ds(0, D)], r.out_bufs, r.out_sems)

    def rows_of(ref, to):
        return ref[pl.ds(2 * to, 2)].reshape(256, ref.shape[-1])

    def feed(k, carry):
        to = lax.rem(p.z + k, 4)
        at = pl.ds(pl.multiple_of(256 * to, 256), 256)
        lin = dot(rows_of(r.normed_all, to), r.w_gu[...].reshape(DPAD, 1280))
        gate, up = lin[:, :640], lin[:, 640:]
        sig = 1.0 / (1.0 + jnp.exp(-gate))
        silu = gate * sig
        hidden = (silu * up).astype(BF16)
        back_hidden = dot_nt(rows_of(r.cot_all, to), r.w_down[...]).astype(BF16).astype(F32)
        grad_gate = (back_hidden * up * sig * (1.0 + gate * (1.0 - sig))).astype(BF16)
        grad_up = (back_hidden * silu).astype(BF16)
        for t in range(5):
            r.big[t, at, :] = grad_gate[:, 128 * t : 128 * t + 128]
            r.big[5 + t, at, :] = grad_up[:, 128 * t : 128 * t + 128]
            r.big[10 + t, at, :] = hidden[:, 128 * t : 128 * t + 128]
        part = dot_nt(jnp.concatenate([grad_gate, grad_up], axis=1), r.w_gu[...].reshape(DPAD, 1280))
        r.part_normed[to] = part.astype(BF16).reshape(2, 128, DPAD)
        return carry

    def feed_block(j):
        k = (4 - j) % 4
        for ring in rings:
            ring.arrive(j)
        lax.fori_loop(k, k + 1, feed, 0)
        red_normed.send(k)

    def pass_on(j):
        for ring in rings:
            ring.forward(j)

    feed_block(0)
    rings[1].relay()
    pass_on(1)
    pass_on(3)
    feed_block(1)
    feed_block(3)
    pass_on(2)
    red_normed.forward(3)
    red_normed.forward(1)
    feed_block(2)
    red_normed.forward(2)
    red_normed.forward(0)

    def project(k, carry):
        to = lax.rem(p.z + k, 4)
        at = pl.ds(pl.multiple_of(256 * to, 256), 256)
        hidden = jnp.concatenate([r.big[10 + t, at, :] for t in range(5)], axis=1)
        r.part_normed[to, :, :, :D] = dot(hidden, r.w_down[...]).astype(BF16).reshape(2, 128, D)
        return carry

    def grad_gate_up(i, carry):
        at = pl.ds(pl.multiple_of(256 * i, 256), 256)
        left = r.normed_all[:, :, :, at].reshape(1024, 256)
        right = jnp.concatenate([r.big[t] for t in range(10)], axis=1)
        part = dot_tn(left, right).astype(BF16).reshape(2, 4, 32, 1280)
        r.g_gu[i // 2, pl.ds(2 * lax.rem(i, 2), 2)] = part
        return carry

    lax.fori_loop(0, 4, grad_gate_up, 0)
    ring_gu = ReduceCtx(p, lambda h, y, x: r.g_gu.at[h, y, x], r.gu_bufs, r.gu_red_sems)
    ring_gu.start()

    def grad_down(t, carry):
        at = pl.ds(pl.multiple_of(128 * t, 128), 128)
        r.g_down[at, :] = dot_tn(r.big[10 + t], r.cot_all[...].reshape(1024, D)).astype(BF16)
        return carry

    lax.fori_loop(0, 5, grad_down, 0)
    down_copies = start_all(
        [
            remote(
                r.g_down.at[pl.ds(pl.multiple_of(160 * p.at_y(k), 32), 160)],
                r.down_y.at[k - 1], r.s_gdown.at[0, k], r.r_gdown.at[0, k], p.ypeer(k),
            )
            for k in NEAR
        ]
    )
    red_normed.sent()
    for k in NEAR + (0,):
        lax.fori_loop(k, k + 1, project, 0)
        red_out.send(k)
    gain_mlp = row_vector(r.small_all, 14)
    mixed = r.mixed[...]
    inv_mid = rms_scale(mixed)
    unit_mid = mixed * inv_mid
    r.held[...] = unspread(red_normed.result(), r.spread[...])
    grad_normed = r.held[...]
    store_rows(r.small_grads, 14, jnp.sum(grad_normed * unit_mid, axis=0, keepdims=True))
    scaled = grad_normed * gain_mlp
    r.grad_mixed[...] = r.cot[...].astype(F32) + inv_mid * (
        scaled - unit_mid * jnp.mean(scaled * unit_mid, axis=-1, keepdims=True)
    )
    r.low_b[...] = r.grad_mixed[...].astype(BF16)
    wide = dot_nt(r.low_b[...], r.w_o[...].reshape(DPAD, D)).astype(BF16)
    r.held[...] = dot_nt(wide, r.spread[...])
    scatter_heads(lambda mb, t: r.held[64 * mb : 64 * mb + 64, 128 * t : 128 * t + 128], r.grad_heads)
    for mb in range(MB):
        r.values_t[mb] = jnp.transpose(r.keys[mb].astype(F32)).astype(BF16)
    for k in NEAR + (0,):
        red_out.forward(k)

    def attend_back(mb):
        def step(t, carry):
            i = mb * 7 + t
            grad_probs = dot_nt(r.values[mb], r.grad_heads[i])
            probs = r.probs[i].astype(F32)
            weighted = probs * grad_probs
            inner = jnp.sum(weighted, axis=0, keepdims=True)
            grad_scores = (weighted - probs * inner).astype(BF16)
            r.big[i] = grad_scores
            r.grad_query[i] = collect_heads(dot(r.values_t[mb], grad_scores), t)
            return carry

        lax.fori_loop(0, 7, step, 0)

    def grad_key_value(i, carry):
        mb, y = i // 4, lax.rem(i, 4)
        at = pl.ds(pl.multiple_of(256 * y, 256), 256)
        scores = jnp.concatenate([r.big[mb * 7 + t, at, :] for t in range(7)], axis=1)
        probs = jnp.concatenate([r.probs[mb * 7 + t, at, :] for t in range(7)], axis=1)
        grad_keys = dot(scores, r.heads[pl.ds(7 * mb, 7)].reshape(896, 128))
        grad_values = dot(probs, r.grad_heads[pl.ds(7 * mb, 7)].reshape(896, 128))
        r.kv_all[mb, y, :, :, :128] = grad_keys.astype(BF16).reshape(4, 64, 128)
        r.kv_all[mb, y, :, :, 128:] = grad_values.astype(BF16).reshape(4, 64, 128)
        return carry

    ring_kv = ReduceCtx(p, lambda h, y, x: r.kv_all.at[h, y, x], r.kv_bufs, r.kv_red_sems)
    for mb in range(MB):
        attend_back(mb)
        lax.fori_loop(4 * mb, 4 * mb + 4, grad_key_value, 0)
        ring_kv.start((mb,))
    ring_gu.forward()

    def weight_gradient(left, right, out):
        def step(i, carry):
            at = pl.ds(pl.multiple_of(256 * i, 256), 256)
            part = dot_tn(left[:, at], right[...]).astype(BF16)
            out[i // 2, pl.ds(2 * lax.rem(i, 2), 2)] = part.reshape(2, 4, 2, 16, part.shape[-1])
            return carry

        lax.fori_loop(0, 4, step, 0)

    def to_mate(n, grads, got):
        c = remote(grads.at[1 - p.core], got, r.s_mate.at[n], r.r_mate.at[n], {"dp": p.mate()})
        c.start()
        return c

    def with_mate(c, grads, got):
        c.wait_recv()
        for y in range(4):
            got[y] = (grads[p.core, y].astype(F32) + got[y].astype(F32)).astype(BF16)

    weight_gradient(r.attended_wide, r.low_b, r.g_wo)
    mate_wo = to_mate(0, r.g_wo, r.m_wo)
    ring_kv.forward()
    build_columns(r.big)
    r.layer_out[...] = (mixed + red_out.result()).astype(BF16)
    cosine, sine = r.cosine[...], r.sine[...]
    for t in range(7):
        tile = jnp.concatenate([r.grad_query[t], r.grad_query[7 + t]], axis=0) * (HEAD_SIZE**-0.5)
        r.low_a[:, 128 * t : 128 * t + 128] = rotate_back(tile, cosine, sine).astype(BF16)
    weight_gradient(r.normed_in, r.low_a, r.g_wq)
    mate_wq = to_mate(1, r.g_wq, r.m_wq)
    with_mate(mate_wo, r.g_wo, r.m_wo)
    ring_wo = ReduceCtx(p, lambda h, y, x: r.m_wo.at[y, x, h], r.wo_bufs, r.wo_sems)
    ring_wo.start()
    with_mate(mate_wq, r.g_wq, r.m_wq)
    ring_wq = ReduceCtx(p, lambda h, y, x: r.m_wq.at[y, x, h], r.wq_bufs, r.wq_sems)
    ring_wq.start()
    store_rows(r.small_grads, 7, jnp.sum(r.low_a[...].astype(F32), axis=0, keepdims=True))
    kv_sum = jnp.concatenate([ring_kv.result(0), ring_kv.result(1)], axis=0)
    grad_key = rotate_back(kv_sum[:, :128], cosine, sine).astype(BF16)
    r.low_kv[:, :128] = grad_key
    r.low_kv[:, 128:] = kv_sum[:, 128:].astype(BF16)
    weight_gradient(r.normed_in, r.low_kv, r.g_wkv)
    mate_wkv = to_mate(2, r.g_wkv, r.m_wkv)
    ring_wo.forward()
    with_mate(mate_wkv, r.g_wkv, r.m_wkv)
    ring_wkv = ReduceCtx(p, lambda h, y, x: r.m_wkv.at[y, x, h], r.wkv_bufs, r.wkv_sems)
    ring_wkv.start()
    bias_kv = jnp.sum(r.low_kv[...].astype(F32), axis=0, keepdims=True)
    store_rows(r.small_grads, 21, bias_kv)
    r.small_grads[23:24, :] = jnp.zeros((1, 128), F32)
    lowered = jnp.concatenate([r.low_a[...], r.low_kv[...]], axis=1)
    r.held[...] = unspread(dot_nt(lowered, r.w_qkv[...].reshape(DPAD, 1152)), r.spread[...])
    residual = r.hidden[...].astype(F32)
    inv_rms = rms_scale(residual)
    unit_in = residual * inv_rms
    store_rows(r.small_grads, 0, jnp.sum(r.held[...] * unit_in, axis=0, keepdims=True))
    small = SmallSum(p, r.small_grads, r.small_bufs2, r.small_sems2)
    small.start()
    ring_wkv.forward()
    ring_wq.forward()
    for h in (0, 1):
        part = ring_gu.result(h)
        for z in range(4):
            r.gu_out[z, h] = part[8 * z : 8 * z + 8]
    gu_copies = []
    for k in range(1, 8):
        to = p.dpindex(k)
        gu_copies.append(
            remote(
                r.gu_out.at[to // 2, lax.rem(to, 2)], r.gu_got.at[p.dp], r.s_ggu.at[k], r.r_ggu.at[k], {"dp": to}
            )
        )
    start_all(gu_copies)
    r.gu_got[p.dp] = r.gu_out[p.z, p.core]
    small.along_y()
    arrive_all(down_copies)
    total = r.g_down[pl.ds(pl.multiple_of(160 * p.y, 32), 160), :].astype(F32)
    for k in NEAR:
        total = total + r.down_y[k - 1].astype(F32)
    for i in range(4):
        r.down_mid[i] = total[40 * i : 40 * i + 40]
    down_copies2 = start_all(
        [
            remote(r.down_mid.at[p.at_x(k)], r.down_x.at[k - 1], r.s_gdown.at[1, k], r.r_gdown.at[1, k], p.xpeer(k))
            for k in NEAR
        ]
    )
    scaled = r.held[...] * row_vector(r.small_all, 0)
    r.grad_in[...] = r.grad_mixed[...] + inv_rms * (
        scaled - unit_in * jnp.mean(scaled * unit_in, axis=-1, keepdims=True)
    )
    small.along_dp()
    sum_wo = ZSum(p, ring_wo, r.zo_bufs, r.zo_sems)
    sum_wo.start()
    sum_wq = ZSum(p, ring_wq, r.zq_bufs, r.zq_sems)
    sum_wq.start()
    sum_wkv = ZSum(p, ring_wkv, r.zkv_bufs, r.zkv_sems)
    sum_wkv.start()
    arrive_all(gu_copies)
    for n, out in enumerate((r.o_gate, r.o_up)):
        for d in range(8):
            r.stage[8 * d : 8 * d + 8, :] = r.gu_got[d, :, 640 * n : 640 * n + 640]
        wide = r.stage[...]
        high = wide.astype(BF16)
        low = (wide - high.astype(F32)).astype(BF16)
        packed = dot_nt(high, columns_of(r.big)) + dot_nt(low, columns_of(r.big))
        for d in range(8):
            out[:, 608 * d : 608 * d + 608] = packed[8 * d : 8 * d + 7, :608]
    arrive_all(down_copies2)
    final = r.down_mid[p.x] + r.down_x[0] + r.down_x[1] + r.down_x[2]
    r.o_down[...] = final[:38]
    r.o_output[...] = sum_wo.result()[:7]
    r.o_query[...] = sum_wq.result()[:7]
    part = sum_wkv.result()
    r.o_key[...] = part[:7, :128]
    r.o_value[...] = part[:7, 128:]
    total = small.result()
    r.o_small[...] = total
    me = p.dp * 16 + p.ctx
    flat = lax.broadcasted_iota(jnp.int32, (7, 128), 0) * 128 + lax.broadcasted_iota(jnp.int32, (7, 128), 1)
    lane = lax.broadcasted_iota(jnp.int32, (1, 128), 1)

    def pick(block, where):
        return jnp.sum(jnp.sum(jnp.where(where, block, 0.0), axis=0, keepdims=True), axis=1, keepdims=True)

    r.o_mine[...] = jnp.zeros_like(r.o_mine)
    for n in range(3):
        row = jnp.zeros((1, 128), F32)
        for i in range(7):
            row = row + jnp.where(lane == i, pick(total[7 * n : 7 * n + 7], flat == me * 7 + i), 0.0)
        r.o_mine[n : n + 1, :] = row
    r.o_mine[3:4, :] = jnp.broadcast_to(pick(total[22:23], lane == me), (1, 128))
    red_out.sent()
    for ring in (*rings, red_normed, red_out, ring_gu, ring_kv, ring_wo, ring_wq, ring_wkv, small, sum_wo, sum_wq, sum_wkv):
        ring.finish()
    sent_all([mate_wo, mate_wq, mate_wkv] + down_copies + down_copies2 + gu_copies)


LAYER_OUTS = {
    "layer_out": shape((128, D), BF16),
    "grad_in": shape((128, D), F32),
    "o_query": shape((7, D), F32),
    "o_key": shape((7, 128), F32),
    "o_value": shape((7, 128), F32),
    "o_output": shape((7, D), F32),
    "o_gate": shape((7, 4864), F32),
    "o_up": shape((7, 4864), F32),
    "o_down": shape((38, D), F32),
    "o_small": shape((24, 128), F32),
    "o_mine": shape((8, 128), F32),
}
BACK_SCRATCH = {
    "big": VM((15, 1024, 128), BF16),
    "part_normed": VM((4, 2, 128, DPAD), BF16),
    "normed_bufs": ReduceDp.scratch(128, DPAD), "normed_sems": ReduceDp.SEMS,
    "out_bufs": ReduceDp.scratch(128, D), "out_sems": ReduceDp.SEMS,
    "g_gu": VM((2, 4, 4, 32, 1280), BF16),
    "gu_bufs": ReduceCtx.scratch(32, 1280), "gu_red_sems": ReduceCtx.SEMS,
    "g_down": VM((640, D), BF16),
    "down_y": VM((3, 160, D), BF16), "down_mid": VM((4, 40, D), F32), "down_x": VM((3, 40, D), F32),
    "grad_mixed": VM((128, D), F32),
    "held": VM((128, D), F32),
    "low_a": VM((128, D), BF16),
    "low_b": VM((128, D), BF16),
    "low_kv": VM((128, 256), BF16),
    "grad_heads": VM((14, 128, 128), BF16),
    "grad_query": VM((14, 64, 128), F32),
    "kv_bufs": ReduceCtx.scratch(64, 256), "kv_red_sems": ReduceCtx.SEMS,
    "g_wo": VM((2, 4, 4, 2, 16, D), BF16), "m_wo": VM((4, 4, 2, 16, D), BF16),
    "g_wq": VM((2, 4, 4, 2, 16, D), BF16), "m_wq": VM((4, 4, 2, 16, D), BF16),
    "g_wkv": VM((2, 4, 4, 2, 16, 256), BF16), "m_wkv": VM((4, 4, 2, 16, 256), BF16),
    "wo_bufs": ReduceCtx.scratch(16, D), "wo_sems": ReduceCtx.SEMS,
    "wq_bufs": ReduceCtx.scratch(16, D), "wq_sems": ReduceCtx.SEMS,
    "wkv_bufs": ReduceCtx.scratch(16, 256), "wkv_sems": ReduceCtx.SEMS,
    "zo_bufs": ZSum.scratch(D), "zo_sems": ZSum.SEMS,
    "zq_bufs": ZSum.scratch(D), "zq_sems": ZSum.SEMS,
    "zkv_bufs": ZSum.scratch(256), "zkv_sems": ZSum.SEMS,
    "small_grads": VM((24, 128), F32),
    "small_bufs2": SmallSum.SCRATCH, "small_sems2": SmallSum.SEMS,
    "gu_out": VM((4, 2, 8, 1280), F32), "gu_got": VM((8, 8, 1280), F32),
    "s_mate": DMA((3,)), "r_mate": DMA((3,)), "s_gdown": DMA((2, 4)), "r_gdown": DMA((2, 4)),
    "s_ggu": DMA((8,)), "r_ggu": DMA((8,)),
}


WHOLE = ("layer_out", "grad_in", "o_query", "o_key", "o_value", "o_output", "o_gate", "o_up", "o_down")
VECTORS = {"norm_attn": 7, "b_query": 7, "norm_mlp": 7, "b_value": 1, "b_key": 128}


def finish(done):
    def kernel(*refs):
        count = len(WHOLE)
        sources, (mine, sums) = refs[:count], refs[count : count + 2]
        targets, vectors = refs[count + 2 : 2 * count + 2], refs[2 * count + 2 :]
        for source, target in zip(sources, targets):
            target[...] = source[...]
        for n in range(3):
            vectors[n][...] = mine[n, :7]
        vectors[3][...] = mine[3, :1]
        vectors[4][...] = sums[21]

    fast = pl.BlockSpec(memory_space=VM)
    results = pl.pallas_call(
        kernel,
        out_shape=tuple(LAYER_OUTS[key] for key in WHOLE) + tuple(shape((n,), F32) for n in VECTORS.values()),
        in_specs=[fast] * (len(WHOLE) + 2),
        out_specs=tuple([fast] * (len(WHOLE) + len(VECTORS))),
        name="finish",
        compiler_params=pltpu.CompilerParams(vmem_limit_bytes=63 << 20),
    )(*(done[key] for key in WHOLE), done["o_mine"], done["o_small"])
    return dict(zip(WHOLE + tuple(VECTORS), results))


def layer(r):
    p = Place()
    back(r, p, front(r, p))


def body(
    hidden_in, positions, norm_attn, w_query, b_query, w_key, b_key, value_weight, value_bias, w_output,
    norm_mlp, w_gate, w_up, w_down, cotangent,
):
    rows = MB * 64
    inputs = {
        "hidden": hidden_in.reshape(rows, D),
        "cot": cotangent.reshape(rows, D),
        "positions": positions,
        "norm_attn": norm_attn, "b_query": b_query, "norm_mlp": norm_mlp, "b_key": b_key, "value_bias": value_bias,
        "w_query": w_query, "w_key": w_key, "w_value": value_weight, "w_output": w_output,
        "w_gate": w_gate, "w_up": w_up, "w_down_own": w_down,
    }
    done = call(layer, inputs, LAYER_OUTS, {**FRONT_SCRATCH, **BACK_SCRATCH}, 0, "layer")
    done = finish(done)
    return (
        done["layer_out"].reshape(MB, 1, 64, D),
        done["grad_in"].reshape(MB, 1, 64, D),
        done["norm_attn"],
        done["o_query"],
        done["b_query"],
        done["o_key"],
        done["b_key"],
        done["o_value"],
        done["b_value"],
        done["o_output"],
        done["norm_mlp"],
        done["o_gate"],
        done["o_up"],
        done["o_down"],
    )


def solution(mesh):
    rows = P(("dp", "ctx"), None)
    vector = P(("dp", "ctx"))
    tokens = P(None, "dp", "ctx", None)
    in_specs = (
        tokens, P(None, "dp", "ctx"), vector, rows, vector, rows, vector, rows, vector, rows, vector,
        rows, rows, rows, tokens,
    )
    out_specs = (
        tokens, tokens, vector, rows, vector, rows, P(), rows, vector, rows, vector, rows, rows, rows,
    )
    return jax.shard_map(body, mesh=mesh, in_specs=in_specs, out_specs=out_specs, check_vma=False)
```

```python
import math
import types

import jax
import jax.numpy as jnp
from jax import lax
from jax.experimental import pallas as pl
from jax.experimental.pallas import tpu as pltpu
from jax.sharding import PartitionSpec as P

QUERY_HEADS = 14
KEY_VALUE_HEADS = 2
HEAD_SIZE = 64
GROUP = QUERY_HEADS // KEY_VALUE_HEADS
MB = 2
D = 896
DPAD = 1024
EPSILON = 1e-06
THETA_BASE = 1000000.0
F32 = jnp.float32
BF16 = jnp.bfloat16
MESH = pl.DeviceIdType.MESH
DMA = pltpu.SemaphoreType.DMA
VM = pltpu.VMEM


def remote(src, dst, ss, rs, peer):
    return pltpu.make_async_remote_copy(
        src_ref=src, dst_ref=dst, send_sem=ss, recv_sem=rs, device_id=peer, device_id_type=MESH
    )


def greet(peers):
    sem = pltpu.get_barrier_semaphore()
    for peer in peers:
        pl.semaphore_signal(sem, inc=1, device_id=peer, device_id_type=MESH)


def meet(peers):
    pl.semaphore_wait(pltpu.get_barrier_semaphore(), len(peers))


class Place:
    def __init__(self):
        self.dp = lax.axis_index("dp")
        self.ctx = lax.axis_index("ctx")
        self.y, self.x = self.ctx // 4, lax.rem(self.ctx, 4)
        self.z, self.core = self.dp // 2, lax.rem(self.dp, 2)

    def at_x(self, k):
        return lax.rem(self.x + (k + 4), 4)

    def at_y(self, k):
        return lax.rem(self.y + (k + 4), 4)

    def at_z(self, k):
        return lax.rem(self.z + (k + 4), 4)

    def line(self, axis, k):
        return self.y * 4 + self.at_x(k) if axis == 0 else self.at_y(k) * 4 + self.x

    def xpeer(self, k):
        return {"ctx": self.line(0, k)}

    def ypeer(self, k):
        return {"ctx": self.line(1, k)}

    def peer(self, axis, k):
        return {"ctx": self.line(axis, k)}

    def zindex(self, k):
        return self.at_z(k) * 2 + self.core

    def mate(self):
        return self.z * 2 + 1 - self.core

    def dpindex(self, k):
        return lax.rem(self.dp + k, 8)


NEAR = (1, 3, 2)


class GatherCtx:
    SEMS = [DMA((2, 4)), DMA((2, 4)), DMA((2, 4, 4)), DMA((2, 4, 4)), DMA((2,))]
    MATE = [DMA((2, 4, 4)), DMA((2, 4, 4))]

    def __init__(self, place, src, dst_at, sems, mate=None):
        self.p, self.src, self.dst_at, self.sems, self.mate = place, src, dst_at, sems, mate
        self.mated = []

    def block(self, h, j, k):
        p = self.p
        return p.at_y(-k) * 4 + p.at_x(-j) if h == 0 else p.at_y(-j) * 4 + p.at_x(-k)

    def share(self, h, j, k):
        if self.mate is None:
            return
        dst = self.dst_at(self.block(h, j, k), h)
        src = self.src.at[h] if j == 0 and k == 0 else dst
        c = remote(src, dst, self.mate[0].at[h, j, k], self.mate[1].at[h, j, k], {"dp": self.p.mate()})
        c.start()
        self.mated.append(c)

    def start(self):
        p, (s1, r1, s2, r2, ls) = self.p, self.sems
        self.local = []
        for h in (0, 1):
            c = pltpu.make_async_copy(self.src.at[h], self.dst_at(p.ctx, h), ls.at[h])
            c.start()
            self.local.append(c)
        self.first = {}
        for k in NEAR:
            for h in (0, 1):
                c = remote(self.src.at[h], self.dst_at(p.ctx, h), s1.at[h, k], r1.at[h, k], p.peer(h, k))
                c.start()
                self.first[h, k] = c
        for h in (0, 1):
            self.share(h, 0, 0)

    def forward(self):
        p, (s1, r1, s2, r2, ls) = self.p, self.sems
        self.second = {}
        for j in (0,) + NEAR:
            for h in (0, 1):
                if j:
                    self.first[h, j].wait_recv()
                dst = self.dst_at(p.line(h, -j), h)
                src = self.src.at[h] if j == 0 else dst
                for k in NEAR:
                    c = remote(src, dst, s2.at[h, j, k], r2.at[h, j, k], p.peer(1 - h, k))
                    c.start()
                    self.second[h, j, k] = c
                if j:
                    self.share(h, j, 0)

    def arrive(self):
        for c in self.local:
            c.wait()
        for (h, j, k), c in self.second.items():
            c.wait_recv()
            self.share(h, j, k)
        for c in self.mated:
            c.wait_recv()

    def finish(self):
        for c in list(self.first.values()) + list(self.second.values()) + self.mated:
            c.wait_send()


class ReduceCtx:
    SEMS = [DMA((2, 4)), DMA((2, 4)), DMA((2, 4)), DMA((2, 4))]

    @staticmethod
    def scratch(rows, cols):
        return [VM((2, 3, 4, rows, cols), BF16), VM((2, 3, rows, cols), BF16)]

    def __init__(self, place, src_at, bufs, sems):
        self.p, self.src_at, self.bufs, self.sems = place, src_at, bufs, sems
        self.first = {}

    def start(self, halves=(0, 1)):
        p, (s1, r1, s2, r2) = self.p, self.sems
        got = self.bufs[0]
        every = slice(None)
        for k in NEAR:
            for h in halves:
                src = self.src_at(0, p.at_y(k), every) if h == 0 else self.src_at(1, every, p.at_x(k))
                c = remote(src, got.at[h, k - 1], s1.at[h, k], r1.at[h, k], p.peer(1 - h, k))
                c.start()
                self.first[h, k] = c

    def forward(self):
        p, (s1, r1, s2, r2) = self.p, self.sems
        got, last = self.bufs
        self.second = {}
        for h in (0, 1):
            for k in NEAR:
                self.first[h, k].wait_recv()
            for i in range(4):
                own = self.src_at(0, p.y, i) if h == 0 else self.src_at(1, i, p.x)
                total = own[...].astype(F32)
                for k in NEAR:
                    total = total + got[h, k - 1, i].astype(F32)
                got[h, 0, i] = total.astype(BF16)
            for k in NEAR:
                to = p.at_x(k) if h == 0 else p.at_y(k)
                c = remote(got.at[h, 0, to], last.at[h, k - 1], s2.at[h, k], r2.at[h, k], p.peer(h, k))
                c.start()
                self.second[h, k] = c

    def result(self, h):
        p = self.p
        got, last = self.bufs
        for k in NEAR:
            self.second[h, k].wait_recv()
        total = got[h, 0, p.x if h == 0 else p.y].astype(F32)
        for k in NEAR:
            total = total + last[h, k - 1].astype(F32)
        return total

    def finish(self):
        for c in list(self.first.values()) + list(self.second.values()):
            c.wait_send()


class GatherDp:
    SEMS = [DMA((4,)), DMA((4,)), DMA((4,)), DMA((4,)), DMA]

    def __init__(self, place, src, dst_at, sems):
        self.p, self.src, self.dst_at, self.sems = place, src, dst_at, sems
        rows = src.shape[0]
        self.halves = {1: pl.ds(0, rows // 2), 3: pl.ds(rows // 2, rows // 2)}

    def start(self):
        p, (s1, r1, s2, r2, ls) = self.p, self.sems
        self.local = pltpu.make_async_copy(self.src, self.dst_at(p.dp), ls)
        self.local.start()
        self.first, self.second, self.relayed = {}, {}, {}
        for k in (1, 3):
            c = remote(self.src, self.dst_at(p.dp), s1.at[k], r1.at[k], {"dp": p.zindex(k)})
            c.start()
            self.first[k] = c

    def relay(self):
        p, (s1, r1, s2, r2, ls) = self.p, self.sems
        for k in (1, 3):
            self.first[k].wait_recv()
            part = self.dst_at(p.zindex(-k)).at[self.halves[k]]
            c = remote(part, part, s1.at[k - 1], r1.at[k - 1], {"dp": p.zindex(k)})
            c.start()
            self.relayed[k] = c

    def forward(self, j):
        p, (s1, r1, s2, r2, ls) = self.p, self.sems
        if j == 2:
            for c in self.relayed.values():
                c.wait_recv()
        block = p.zindex(-j)
        src = self.dst_at(block) if j else self.src
        c = remote(src, self.dst_at(block), s2.at[j], r2.at[j], {"dp": p.mate()})
        c.start()
        self.second[j] = c

    def arrive(self, j):
        if j == 0:
            self.local.wait()
        self.second[j].wait_recv()

    def finish(self):
        for c in list(self.first.values()) + list(self.second.values()) + list(self.relayed.values()):
            c.wait_send()


class ReduceDp:
    SEMS = [DMA((4,)), DMA((4,)), DMA((4,)), DMA((4,))]

    @staticmethod
    def scratch(rows, cols):
        return [VM((4, rows, cols), BF16), VM((3, rows, cols), BF16)]

    def __init__(self, place, src, bufs, sems):
        self.p, self.src, self.bufs, self.sems = place, src, bufs, sems
        self.first, self.second = {}, {}

    def send(self, k):
        p, (s1, r1, s2, r2) = self.p, self.sems
        to = p.at_z(k)
        c = remote(self.src.at[to, 1 - p.core], self.bufs[0].at[to], s1.at[k], r1.at[k], {"dp": p.mate()})
        c.start()
        self.first[k] = c

    def forward(self, k):
        p, (s1, r1, s2, r2) = self.p, self.sems
        got, last = self.bufs
        to = p.at_z(k)
        self.first[k].wait_recv()
        total = self.src[to, p.core].astype(F32) + got[to].astype(F32)
        got[to] = total.astype(BF16)
        if k:
            c = remote(got.at[to], last.at[k - 1], s2.at[k], r2.at[k], {"dp": p.zindex(k)})
            c.start()
            self.second[k] = c

    def result(self):
        got, last = self.bufs
        total = got[self.p.z].astype(F32)
        for k in NEAR:
            self.second[k].wait_recv()
            total = total + last[k - 1].astype(F32)
        return total

    def sent(self):
        for c in self.first.values():
            c.wait_send()

    def finish(self):
        for c in self.second.values():
            c.wait_send()


def xy_peers(p):
    return [p.peer(axis, k) for axis in (0, 1) for k in NEAR]


def dp_peers(p):
    return [{"dp": p.dpindex(k)} for k in range(1, 8)]


def shape(dims, kind):
    return jax.ShapeDtypeStruct(dims, kind)


def call(phase, inputs, outs, scratch, cid, name):
    flat, where = [], {}
    for key, entry in scratch.items():
        entries = entry if isinstance(entry, list) else [entry]
        where[key] = (len(flat), len(entries), isinstance(entry, list))
        flat += entries

    def kernel(*refs):
        named = dict(zip(list(inputs) + list(outs), refs))
        tail = refs[len(inputs) + len(outs) :]
        for key, (start, count, many) in where.items():
            named[key] = list(tail[start : start + count]) if many else tail[start]
        phase(types.SimpleNamespace(**named))

    results = pl.pallas_call(
        kernel,
        out_shape=tuple(outs.values()),
        in_specs=[pl.BlockSpec(memory_space=VM)] * len(inputs),
        out_specs=tuple(pl.BlockSpec(memory_space=VM) for _ in outs),
        scratch_shapes=flat,
        name=name,
        compiler_params=pltpu.CompilerParams(
            collective_id=cid, has_side_effects=True, vmem_limit_bytes=63 << 20
        ),
    )(*inputs.values())
    return dict(zip(outs, results))


def dot(left, right):
    return jnp.dot(left, right, preferred_element_type=F32)


def dot_tn(left, right):
    return lax.dot_general(left, right, (((0,), (0,)), ((), ())), preferred_element_type=F32)


def dot_nt(left, right):
    return lax.dot_general(left, right, (((1,), (1,)), ((), ())), preferred_element_type=F32)


def rms_scale(values):
    return lax.rsqrt(jnp.mean(values * values, axis=-1, keepdims=True) + EPSILON)


def row_vector(ref, start):
    return jnp.concatenate([ref[start + i : start + i + 1, :] for i in range(7)], axis=1)


def store_rows(ref, start, vector):
    for i in range(vector.shape[1] // 128):
        ref[start + i : start + i + 1, :] = vector[:, 128 * i : 128 * i + 128]


def build_spread(ref):
    for part in range(7):
        source = lax.broadcasted_iota(jnp.int32, (128, DPAD), 0) + 128 * part
        column = lax.broadcasted_iota(jnp.int32, (128, DPAD), 1)
        inner = column & 7
        owner = ((column >> 3) & 3) * 2 + (column >> 9)
        wanted = (owner * 16 + ((column >> 5) & 15)) * 7 + inner
        ref[128 * part : 128 * part + 128, :] = jnp.where(
            (source == wanted) & (inner < 7), 1.0, 0.0
        ).astype(BF16)


def spread(values, matrix):
    return dot(values, matrix).astype(BF16)


def unspread(values, matrix):
    high = values.astype(BF16)
    low = (values - high.astype(F32)).astype(BF16)
    return dot_nt(high, matrix) + dot_nt(low, matrix)


def lanes(rows):
    return lax.broadcasted_iota(jnp.int32, (rows, 128), 1)


def half_turn(tile):
    first = (lanes(tile.shape[0]) & 63) < 32
    return jnp.where(first, pltpu.roll(tile, 96, 1), pltpu.roll(tile, 32, 1))


def rotate(tile, cosine, signed_sine):
    return tile * cosine + half_turn(tile) * signed_sine


def rotate_back(tile, cosine, signed_sine):
    return tile * cosine - half_turn(tile) * signed_sine


def scatter_heads(tile_of, dst):
    for mb in range(MB):
        for head in range(QUERY_HEADS):
            tile = tile_of(mb, head // 2)
            group = head // GROUP
            if head % 2 != group:
                tile = pltpu.roll(tile, 64, 1)
            tile = jnp.where((lanes(64) >= 64) == (group == 1), tile, 0.0)
            at = (head % 2) * 64
            dst[mb * 7 + head // 2, at : at + 64, :] = tile.astype(BF16)


def collect_heads(transposed, t):
    both = jnp.transpose(transposed)
    even, odd = both[:64], both[64:]
    even = jnp.where(t >= 4, pltpu.roll(even, 64, 1), even)
    odd = jnp.where(t <= 2, pltpu.roll(odd, 64, 1), odd)
    return jnp.where(lanes(64) < 64, even, odd)


def start_all(copies):
    for c in copies:
        c.start()
    return copies


def arrive_all(copies):
    for c in copies:
        c.wait_recv()


def sent_all(copies):
    for c in copies:
        c.wait_send()


class SmallSum:
    SCRATCH = [VM((3, 24, 128), F32), VM((3, 24, 128), F32), VM((7, 24, 128), F32), VM((2, 24, 128), F32)]
    SEMS = [DMA((3, 8)), DMA((3, 8))]

    def __init__(self, place, src, bufs, sems):
        self.p, self.src, self.bufs, self.sems = place, src, bufs, sems
        self.copies = []

    def start(self):
        p, (s, r) = self.p, self.sems
        self.x = start_all([remote(self.src, self.bufs[0].at[k - 1], s.at[0, k], r.at[0, k], p.xpeer(k)) for k in NEAR])

    def along_y(self):
        p, (s, r) = self.p, self.sems
        arrive_all(self.x)
        got, sums = self.bufs[0], self.bufs[3]
        sums[0] = self.src[...] + got[0] + got[1] + got[2]
        self.y = start_all(
            [remote(sums.at[0], self.bufs[1].at[k - 1], s.at[1, k], r.at[1, k], p.ypeer(k)) for k in NEAR]
        )

    def along_dp(self):
        p, (s, r) = self.p, self.sems
        arrive_all(self.y)
        got, sums = self.bufs[1], self.bufs[3]
        sums[1] = sums[0] + got[0] + got[1] + got[2]
        self.d = start_all(
            [
                remote(sums.at[1], self.bufs[2].at[k - 1], s.at[2, k], r.at[2, k], {"dp": p.dpindex(k)})
                for k in range(1, 8)
            ]
        )

    def result(self):
        arrive_all(self.d)
        total = self.bufs[3][1]
        for k in range(7):
            total = total + self.bufs[2][k]
        return total

    def finish(self):
        sent_all(self.x + self.y + self.d)


class ZSum:
    SEMS = [DMA((4,)), DMA((4,))]

    @staticmethod
    def scratch(cols):
        return [VM((4, 8, cols), F32), VM((4, 8, cols), F32)]

    def __init__(self, place, ring, bufs, sems):
        self.p, self.ring, self.bufs, self.sems = place, ring, bufs, sems

    def start(self):
        p, (s, r), (out, got) = self.p, self.sems, self.bufs
        for h in (0, 1):
            part = self.ring.result(h)
            out[2 * h], out[2 * h + 1] = part[:8], part[8:]
        self.copies = start_all(
            [remote(out.at[p.at_z(k)], got.at[p.z], s.at[k], r.at[k], {"dp": p.zindex(k)}) for k in NEAR]
        )
        got[p.z] = out[p.z]

    def result(self):
        arrive_all(self.copies)
        got = self.bufs[1]
        return got[0] + got[1] + got[2] + got[3]

    def finish(self):
        sent_all(self.copies)


def build_columns(big):
    for t in range(5):
        column = lax.broadcasted_iota(jnp.int32, (640, 128), 1) + 128 * t
        source = lax.broadcasted_iota(jnp.int32, (640, 128), 0)
        owner = (column * 1639) >> 16
        inner = column - owner * 40
        big[t, :640, :] = jnp.where((source == owner * 38 + inner) & (inner < 38), 1.0, 0.0).astype(BF16)


def columns_of(big):
    return jnp.concatenate([big[t, :640, :] for t in range(5)], axis=1)


def front(r, p):
    peers = xy_peers(p) + dp_peers(p)
    greet(peers)
    r.attn_src[...] = jnp.zeros_like(r.attn_src)
    r.stage[...] = jnp.zeros_like(r.stage)
    r.down[...] = jnp.zeros_like(r.down)
    r.down[:38, :] = r.w_down_own[...].astype(F32)
    r.attn_src[:7, :896] = r.w_query[...].astype(F32)
    r.attn_src[:7, 896:1024] = r.w_key[...].astype(F32)
    r.attn_src[:7, 1024:1152] = r.w_value[...].astype(F32)
    r.attn_src[:7, 1152:] = r.w_output[...].astype(F32)
    r.small[...] = jnp.zeros_like(r.small)
    me = p.dp * 16 + p.ctx
    flat = lax.broadcasted_iota(jnp.int32, (7, 128), 0) * 128 + lax.broadcasted_iota(jnp.int32, (7, 128), 1)
    for n, ref in enumerate((r.norm_attn, r.b_query, r.norm_mlp)):
        vector = ref[...].astype(F32)[None]
        total = jnp.zeros((7, 128), F32)
        for i in range(7):
            total = total + jnp.where(flat == me * 7 + i, vector[:, i : i + 1], 0.0)
        r.small[7 * n : 7 * n + 7, :] = total
    for n, ref in enumerate((r.b_key, r.value_bias)):
        r.small[21 + n : 22 + n, :] = jnp.where(flat[:1] == me, ref[...].astype(F32)[None], 0.0)
    r.places[...] = jnp.zeros_like(r.places)
    for at in (0, 64):
        r.places[:MB, at : at + 64] = r.positions[:, 0].astype(F32)
    meet(peers)
    attn_copies = start_all(
        [remote(r.attn_src, r.attn_in.at[p.z], r.s_attn.at[k], r.r_attn.at[k], {"dp": p.zindex(k)}) for k in NEAR]
    )
    small = SmallSum(p, r.small, r.small_bufs, r.small_sems)
    small.start()
    place_copies = start_all(
        [remote(r.places, r.places_x.at[p.x], r.s_place.at[0, k], r.r_place.at[0, k], p.xpeer(k)) for k in NEAR]
    )
    r.attn_in[p.z] = r.attn_src[...]
    r.places_x[p.x] = r.places[...]
    build_columns(r.big)
    for n, ref in enumerate((r.w_gate, r.w_up)):
        whole = ref[...].astype(F32)
        for d in range(8):
            r.stage[8 * d : 8 * d + 7, :608] = whole[:, 608 * d : 608 * d + 608]
        wide = dot(r.stage[...].astype(BF16), columns_of(r.big))
        for d in range(8):
            r.gate_up[d, :, 640 * n : 640 * n + 640] = wide[8 * d : 8 * d + 8]
    gu_copies = []
    for k in range(1, 8):
        to = p.dpindex(k)
        gu_copies.append(
            remote(r.gate_up.at[to], r.gu_in.at[p.core, p.z], r.s_gu.at[k], r.r_gu.at[k], {"dp": to})
        )
    start_all(gu_copies)
    r.gu_in[p.core, p.z] = r.gate_up[p.dp]
    cots = GatherDp(p, r.cot, lambda b: r.cot_all.at[b], r.cot_sems)
    cots.start()
    arrive_all(attn_copies)
    for h in (0, 1):
        pair = jnp.concatenate([r.attn_in[2 * h], r.attn_in[2 * h + 1]], axis=0).astype(BF16)
        r.qkv_block[h] = pair[:, :1152]
        r.o_block[h] = pair[:, 1152:]
    ring_qkv = GatherCtx(p, r.qkv_block, lambda b, h: r.w_qkv.at[p.core, b, h], r.qkv_sems, r.qkv_mate)
    ring_qkv.start()
    small.along_y()
    arrive_all(place_copies)
    place_copies2 = start_all(
        [remote(r.places_x, r.places_all.at[p.y], r.s_place.at[1, k], r.r_place.at[1, k], p.ypeer(k)) for k in NEAR]
    )
    r.places_all[p.y] = r.places_x[...]
    ring_qkv.forward()
    ring_o = GatherCtx(p, r.o_block, lambda b, h: r.w_o.at[p.core, b, h], r.o_sems, r.o_mate)
    ring_o.start()
    build_spread(r.spread)
    inner = lanes(1) & 63
    freqs = jnp.exp((inner & 31).astype(F32) * (-math.log(THETA_BASE) / 32))
    sign = jnp.where(inner < 32, -1.0, 1.0)
    for mb in range(MB):
        angles = jnp.transpose(jnp.broadcast_to(r.places[mb : mb + 1, :], (128, 128)))[:64] * freqs
        r.cosine[64 * mb : 64 * mb + 64, :] = jnp.cos(angles)
        r.sine[64 * mb : 64 * mb + 64, :] = jnp.sin(angles) * sign
    small.along_dp()
    arrive_all(gu_copies)
    for c in (0, 1):
        r.gu_block[c] = jnp.concatenate([r.gu_in[c, z] for z in range(4)], axis=0).astype(BF16)
    ring_gu = GatherCtx(p, r.gu_block, lambda b, h: r.w_gu.at[h, b], r.gu_sems)
    ring_gu.start()
    down_copies = start_all(
        [remote(r.down, r.down_in.at[p.x], r.s_down.at[0, k], r.r_down.at[0, k], p.xpeer(k)) for k in NEAR]
    )
    r.down_in[p.x] = r.down[...]
    cots.relay()
    for j in (0, 1, 3):
        cots.forward(j)
    residual = r.hidden[...].astype(F32)
    unit_in = residual * rms_scale(residual)
    arrive_all(place_copies2)
    low_lane = lanes(8) < 64
    for c in range(8):
        a, b = r.places_all[(2 * c) // 4, (2 * c) % 4], r.places_all[(2 * c + 1) // 4, (2 * c + 1) % 4]
        r.key_row[:, 128 * c : 128 * c + 128] = jnp.where(low_lane, a, b)
    for mb in range(MB):
        key_places = jnp.transpose(jnp.broadcast_to(r.key_row[mb : mb + 1, :], (128, 1024)))
        r.masked[mb] = jnp.where(key_places <= r.places[mb : mb + 1, :], 0.0, -1e30).astype(BF16)
    r.small_all[...] = small.result()
    r.normed_in[...] = spread((unit_in * row_vector(r.small_all, 0)).astype(BF16), r.spread[...])
    bias_query = row_vector(r.small_all, 7)
    ring_qkv.arrive()
    ring_o.forward()
    cosine, sine = r.cosine[...], r.sine[...]
    lin = dot(r.normed_in[...], r.w_qkv[:, :, :, :, 896:].reshape(DPAD, 256))
    keys = rotate(lin[:, :128] + r.small_all[21:22, :], cosine, sine).astype(BF16)
    values = (lin[:, 128:] + r.small_all[22:23, :]).astype(BF16)
    for mb in range(MB):
        r.kv[mb, :, :128] = keys[64 * mb : 64 * mb + 64]
        r.kv[mb, :, 128:] = values[64 * mb : 64 * mb + 64]
    ring_kv = GatherCtx(p, r.kv, lambda b, h: r.kv_all.at[h, b // 4, lax.rem(b, 4)], r.kv_sems)
    ring_kv.start()
    lin = dot(r.normed_in[...], r.w_qkv[:, :, :, :, :896].reshape(DPAD, D))
    query_tiles = []
    for t in range(7):
        tile = lin[:, 128 * t : 128 * t + 128] + bias_query[:, 128 * t : 128 * t + 128]
        query_tiles.append((rotate(tile, cosine, sine).astype(BF16)).astype(F32) * (HEAD_SIZE**-0.5))
    scatter_heads(lambda mb, t: query_tiles[t][64 * mb : 64 * mb + 64], r.heads)
    ring_kv.forward()
    ring_gu.forward()
    arrive_all(down_copies)
    own_down = r.w_down.at[pl.ds(pl.multiple_of(160 * p.y, 32), 160)]
    own_down[...] = jnp.concatenate([r.down_in[i] for i in range(4)], axis=0).astype(BF16)
    down_copies2 = start_all(
        [remote(own_down, own_down, r.s_down.at[1, k], r.r_down.at[1, k], p.ypeer(k)) for k in NEAR]
    )
    ring_kv.arrive()
    for mb in range(MB):
        r.keys[mb] = r.kv_all[mb, :, :, :, :128].reshape(1024, 128)
        r.values[mb] = r.kv_all[mb, :, :, :, 128:].reshape(1024, 128)
        r.values_t[mb] = jnp.transpose(r.values[mb].astype(F32)).astype(BF16)

    def attend(mb):
        def step(t, carry):
            i = mb * 7 + t
            scores = dot_nt(r.keys[mb], r.heads[i]) + r.masked[mb].astype(F32)
            expo = jnp.exp(scores - jnp.max(scores, axis=0, keepdims=True))
            probs = (expo * (1.0 / jnp.sum(expo, axis=0, keepdims=True))).astype(BF16)
            r.probs[i] = probs
            r.attended[i] = collect_heads(dot(r.values_t[mb], probs), t).astype(BF16)
            return carry

        lax.fori_loop(0, 7, step, 0)

    gain_mlp = row_vector(r.small_all, 14)
    rings = []

    def finish_rows(mb):
        at = slice(64 * mb, 64 * mb + 64)
        attended = jnp.concatenate([r.attended[mb * 7 + t] for t in range(7)], axis=1)
        r.attended_wide[at, :] = spread(attended, r.spread[...])
        mixed = residual[at] + dot(r.attended_wide[at, :], r.w_o[...].reshape(DPAD, D))
        r.mixed[at, :] = mixed
        unit_mid = mixed * rms_scale(mixed)
        r.normed_mid[mb] = spread((unit_mid * gain_mlp).astype(BF16), r.spread[...])
        ring = GatherDp(p, r.normed_mid.at[mb], lambda b: r.normed_all.at[b, mb], r.mid_sems[5 * mb : 5 * mb + 5])
        ring.start()
        ring.forward(0)
        rings.append(ring)

    attend(0)
    ring_o.arrive()
    finish_rows(0)
    cots.forward(2)
    attend(1)
    finish_rows(1)
    rings[0].relay()
    ring_gu.arrive()
    arrive_all(down_copies2)
    for j in range(4):
        cots.arrive(j)
    for ring in (ring_qkv, ring_o, ring_kv, ring_gu, cots, small):
        ring.finish()
    sent_all(attn_copies + gu_copies + place_copies + place_copies2 + down_copies + down_copies2)
    return rings


FRONT_SCRATCH = {
    "places": VM((8, 128), F32),
    "cosine": VM((128, 128), F32),
    "sine": VM((128, 128), F32),
    "attn_src": VM((8, 2048), F32),
    "stage": VM((64, 640), F32),
    "gate_up": VM((8, 8, 1280), F32),
    "down": VM((40, D), F32),
    "small": VM((24, 128), F32),
    "attn_in": VM((4, 8, 2048), F32),
    "gu_in": VM((2, 4, 8, 1280), F32),
    "down_in": VM((4, 40, D), F32),
    "places_x": VM((4, 8, 128), F32),
    "places_all": VM((4, 4, 8, 128), F32),
    "key_row": VM((8, 1024), F32),
    "masked": VM((2, 1024, 128), BF16),
    "qkv_block": VM((2, 16, 1152), BF16),
    "o_block": VM((2, 16, D), BF16),
    "gu_block": VM((2, 32, 1280), BF16),
    "kv": VM((2, 64, 256), BF16),
    "kv_all": VM((2, 4, 4, 64, 256), BF16),
    "values_t": VM((2, 128, 1024), BF16),
    "attended": VM((14, 64, 128), BF16),
    "normed_mid": VM((2, 64, DPAD), BF16),
    "w_qkv": VM((2, 16, 2, 16, 1152), BF16),
    "w_o": VM((2, 16, 2, 16, D), BF16),
    "w_gu": VM((2, 16, 32, 1280), BF16),
    "w_down": VM((640, D), BF16),
    "small_all": VM((24, 128), F32),
    "cot_all": VM((8, 128, D), BF16),
    "normed_all": VM((8, 2, 64, DPAD), BF16),
    "probs": VM((14, 1024, 128), BF16),
    "heads": VM((14, 128, 128), BF16),
    "keys": VM((2, 1024, 128), BF16),
    "values": VM((2, 1024, 128), BF16),
    "attended_wide": VM((128, DPAD), BF16),
    "normed_in": VM((128, DPAD), BF16),
    "mixed": VM((128, D), F32),
    "spread": VM((D, DPAD), BF16),
    "small_bufs": SmallSum.SCRATCH,
    "small_sems": SmallSum.SEMS,
    "s_attn": DMA((4,)), "r_attn": DMA((4,)), "s_gu": DMA((8,)), "r_gu": DMA((8,)),
    "s_place": DMA((2, 4)), "r_place": DMA((2, 4)), "s_down": DMA((2, 4)), "r_down": DMA((2, 4)),
    "qkv_sems": GatherCtx.SEMS, "qkv_mate": GatherCtx.MATE, "o_sems": GatherCtx.SEMS, "o_mate": GatherCtx.MATE,
    "kv_sems": GatherCtx.SEMS, "gu_sems": GatherCtx.SEMS, "cot_sems": GatherDp.SEMS, "mid_sems": GatherDp.SEMS * 2,
}


def back(r, p, rings):
    red_normed = ReduceDp(p, r.part_normed, r.normed_bufs, r.normed_sems)
    red_out = ReduceDp(p, r.part_normed.at[:, :, :, pl.ds(0, D)], r.out_bufs, r.out_sems)

    def rows_of(ref, to):
        return ref[pl.ds(2 * to, 2)].reshape(256, ref.shape[-1])

    def feed(k, carry):
        to = lax.rem(p.z + k, 4)
        at = pl.ds(pl.multiple_of(256 * to, 256), 256)
        lin = dot(rows_of(r.normed_all, to), r.w_gu[...].reshape(DPAD, 1280))
        gate, up = lin[:, :640], lin[:, 640:]
        sig = 1.0 / (1.0 + jnp.exp(-gate))
        silu = gate * sig
        hidden = (silu * up).astype(BF16)
        back_hidden = dot_nt(rows_of(r.cot_all, to), r.w_down[...]).astype(BF16).astype(F32)
        grad_gate = (back_hidden * up * sig * (1.0 + gate * (1.0 - sig))).astype(BF16)
        grad_up = (back_hidden * silu).astype(BF16)
        for t in range(5):
            r.big[t, at, :] = grad_gate[:, 128 * t : 128 * t + 128]
            r.big[5 + t, at, :] = grad_up[:, 128 * t : 128 * t + 128]
            r.big[10 + t, at, :] = hidden[:, 128 * t : 128 * t + 128]
        part = dot_nt(jnp.concatenate([grad_gate, grad_up], axis=1), r.w_gu[...].reshape(DPAD, 1280))
        r.part_normed[to] = part.astype(BF16).reshape(2, 128, DPAD)
        return carry

    def feed_block(j):
        k = (4 - j) % 4
        for ring in rings:
            ring.arrive(j)
        lax.fori_loop(k, k + 1, feed, 0)
        red_normed.send(k)

    def pass_on(j):
        for ring in rings:
            ring.forward(j)

    feed_block(0)
    rings[1].relay()
    pass_on(1)
    pass_on(3)
    feed_block(1)
    feed_block(3)
    pass_on(2)
    red_normed.forward(3)
    red_normed.forward(1)
    feed_block(2)
    red_normed.forward(2)
    red_normed.forward(0)

    def project(k, carry):
        to = lax.rem(p.z + k, 4)
        at = pl.ds(pl.multiple_of(256 * to, 256), 256)
        hidden = jnp.concatenate([r.big[10 + t, at, :] for t in range(5)], axis=1)
        r.part_normed[to, :, :, :D] = dot(hidden, r.w_down[...]).astype(BF16).reshape(2, 128, D)
        return carry

    def grad_gate_up(i, carry):
        at = pl.ds(pl.multiple_of(256 * i, 256), 256)
        left = r.normed_all[:, :, :, at].reshape(1024, 256)
        right = jnp.concatenate([r.big[t] for t in range(10)], axis=1)
        part = dot_tn(left, right).astype(BF16).reshape(2, 4, 32, 1280)
        r.g_gu[i // 2, pl.ds(2 * lax.rem(i, 2), 2)] = part
        return carry

    ring_gu = ReduceCtx(p, lambda h, y, x: r.g_gu.at[h, y, x], r.gu_bufs, r.gu_red_sems)
    for half in (0, 1):
        lax.fori_loop(2 * half, 2 * half + 2, grad_gate_up, 0)
        ring_gu.start((half,))

    def grad_down(t, carry):
        at = pl.ds(pl.multiple_of(128 * t, 128), 128)
        r.g_down[at, :] = dot_tn(r.big[10 + t], r.cot_all[...].reshape(1024, D)).astype(BF16)
        return carry

    lax.fori_loop(0, 5, grad_down, 0)
    down_copies = start_all(
        [
            remote(
                r.g_down.at[pl.ds(pl.multiple_of(160 * p.at_y(k), 32), 160)],
                r.down_y.at[k - 1], r.s_gdown.at[0, k], r.r_gdown.at[0, k], p.ypeer(k),
            )
            for k in NEAR
        ]
    )
    red_normed.sent()
    for k in NEAR + (0,):
        lax.fori_loop(k, k + 1, project, 0)
        red_out.send(k)
    gain_mlp = row_vector(r.small_all, 14)
    mixed = r.mixed[...]
    inv_mid = rms_scale(mixed)
    unit_mid = mixed * inv_mid
    r.held[...] = unspread(red_normed.result(), r.spread[...])
    grad_normed = r.held[...]
    store_rows(r.small_grads, 14, jnp.sum(grad_normed * unit_mid, axis=0, keepdims=True))
    scaled = grad_normed * gain_mlp
    r.grad_mixed[...] = r.cot[...].astype(F32) + inv_mid * (
        scaled - unit_mid * jnp.mean(scaled * unit_mid, axis=-1, keepdims=True)
    )
    r.low_b[...] = r.grad_mixed[...].astype(BF16)
    wide = dot_nt(r.low_b[...], r.w_o[...].reshape(DPAD, D)).astype(BF16)
    r.held[...] = dot_nt(wide, r.spread[...])
    scatter_heads(lambda mb, t: r.held[64 * mb : 64 * mb + 64, 128 * t : 128 * t + 128], r.grad_heads)
    for mb in range(MB):
        r.values_t[mb] = jnp.transpose(r.keys[mb].astype(F32)).astype(BF16)
    for k in NEAR + (0,):
        red_out.forward(k)

    def attend_back(mb):
        def step(t, carry):
            i = mb * 7 + t
            grad_probs = dot_nt(r.values[mb], r.grad_heads[i])
            probs = r.probs[i].astype(F32)
            weighted = probs * grad_probs
            inner = jnp.sum(weighted, axis=0, keepdims=True)
            grad_scores = (weighted - probs * inner).astype(BF16)
            r.big[i] = grad_scores
            r.grad_query[i] = collect_heads(dot(r.values_t[mb], grad_scores), t)
            return carry

        lax.fori_loop(0, 7, step, 0)

    def grad_key_value(i, carry):
        mb, y = i // 4, lax.rem(i, 4)
        at = pl.ds(pl.multiple_of(256 * y, 256), 256)
        scores = jnp.concatenate([r.big[mb * 7 + t, at, :] for t in range(7)], axis=1)
        probs = jnp.concatenate([r.probs[mb * 7 + t, at, :] for t in range(7)], axis=1)
        grad_keys = dot(scores, r.heads[pl.ds(7 * mb, 7)].reshape(896, 128))
        grad_values = dot(probs, r.grad_heads[pl.ds(7 * mb, 7)].reshape(896, 128))
        r.kv_all[mb, y, :, :, :128] = grad_keys.astype(BF16).reshape(4, 64, 128)
        r.kv_all[mb, y, :, :, 128:] = grad_values.astype(BF16).reshape(4, 64, 128)
        return carry

    ring_kv = ReduceCtx(p, lambda h, y, x: r.kv_all.at[h, y, x], r.kv_bufs, r.kv_red_sems)
    for mb in range(MB):
        attend_back(mb)
        lax.fori_loop(4 * mb, 4 * mb + 4, grad_key_value, 0)
        ring_kv.start((mb,))
    ring_gu.forward()

    def weight_gradient(left, right, out):
        def step(i, carry):
            at = pl.ds(pl.multiple_of(256 * i, 256), 256)
            part = dot_tn(left[:, at], right[...]).astype(BF16)
            out[i // 2, pl.ds(2 * lax.rem(i, 2), 2)] = part.reshape(2, 4, 2, 16, part.shape[-1])
            return carry

        lax.fori_loop(0, 4, step, 0)

    def to_mate(n, grads, got):
        c = remote(grads.at[1 - p.core], got, r.s_mate.at[n], r.r_mate.at[n], {"dp": p.mate()})
        c.start()
        return c

    def with_mate(c, grads, got):
        c.wait_recv()
        for y in range(4):
            got[y] = (grads[p.core, y].astype(F32) + got[y].astype(F32)).astype(BF16)

    weight_gradient(r.attended_wide, r.low_b, r.g_wo)
    mate_wo = to_mate(0, r.g_wo, r.m_wo)
    ring_kv.forward()
    build_columns(r.big)
    r.layer_out[...] = (mixed + red_out.result()).astype(BF16)
    cosine, sine = r.cosine[...], r.sine[...]
    for t in range(7):
        tile = jnp.concatenate([r.grad_query[t], r.grad_query[7 + t]], axis=0) * (HEAD_SIZE**-0.5)
        r.low_a[:, 128 * t : 128 * t + 128] = rotate_back(tile, cosine, sine).astype(BF16)
    weight_gradient(r.normed_in, r.low_a, r.g_wq)
    mate_wq = to_mate(1, r.g_wq, r.m_wq)
    with_mate(mate_wo, r.g_wo, r.m_wo)
    ring_wo = ReduceCtx(p, lambda h, y, x: r.m_wo.at[y, x, h], r.wo_bufs, r.wo_sems)
    ring_wo.start()
    with_mate(mate_wq, r.g_wq, r.m_wq)
    ring_wq = ReduceCtx(p, lambda h, y, x: r.m_wq.at[y, x, h], r.wq_bufs, r.wq_sems)
    ring_wq.start()
    store_rows(r.small_grads, 7, jnp.sum(r.low_a[...].astype(F32), axis=0, keepdims=True))
    kv_sum = jnp.concatenate([ring_kv.result(0), ring_kv.result(1)], axis=0)
    grad_key = rotate_back(kv_sum[:, :128], cosine, sine).astype(BF16)
    r.low_kv[:, :128] = grad_key
    r.low_kv[:, 128:] = kv_sum[:, 128:].astype(BF16)
    weight_gradient(r.normed_in, r.low_kv, r.g_wkv)
    mate_wkv = to_mate(2, r.g_wkv, r.m_wkv)
    ring_wo.forward()
    with_mate(mate_wkv, r.g_wkv, r.m_wkv)
    ring_wkv = ReduceCtx(p, lambda h, y, x: r.m_wkv.at[y, x, h], r.wkv_bufs, r.wkv_sems)
    ring_wkv.start()
    bias_kv = jnp.sum(r.low_kv[...].astype(F32), axis=0, keepdims=True)
    store_rows(r.small_grads, 21, bias_kv)
    r.small_grads[23:24, :] = jnp.zeros((1, 128), F32)
    lowered = jnp.concatenate([r.low_a[...], r.low_kv[...]], axis=1)
    r.held[...] = unspread(dot_nt(lowered, r.w_qkv[...].reshape(DPAD, 1152)), r.spread[...])
    residual = r.hidden[...].astype(F32)
    inv_rms = rms_scale(residual)
    unit_in = residual * inv_rms
    store_rows(r.small_grads, 0, jnp.sum(r.held[...] * unit_in, axis=0, keepdims=True))
    small = SmallSum(p, r.small_grads, r.small_bufs2, r.small_sems2)
    small.start()
    ring_wkv.forward()
    ring_wq.forward()
    for h in (0, 1):
        part = ring_gu.result(h)
        for z in range(4):
            r.gu_out[z, h] = part[8 * z : 8 * z + 8]
    gu_copies = []
    for k in range(1, 8):
        to = p.dpindex(k)
        gu_copies.append(
            remote(
                r.gu_out.at[to // 2, lax.rem(to, 2)], r.gu_got.at[p.dp], r.s_ggu.at[k], r.r_ggu.at[k], {"dp": to}
            )
        )
    start_all(gu_copies)
    r.gu_got[p.dp] = r.gu_out[p.z, p.core]
    small.along_y()
    arrive_all(down_copies)
    total = r.g_down[pl.ds(pl.multiple_of(160 * p.y, 32), 160), :].astype(F32)
    for k in NEAR:
        total = total + r.down_y[k - 1].astype(F32)
    for i in range(4):
        r.down_mid[i] = total[40 * i : 40 * i + 40]
    down_copies2 = start_all(
        [
            remote(r.down_mid.at[p.at_x(k)], r.down_x.at[k - 1], r.s_gdown.at[1, k], r.r_gdown.at[1, k], p.xpeer(k))
            for k in NEAR
        ]
    )
    scaled = r.held[...] * row_vector(r.small_all, 0)
    r.grad_in[...] = r.grad_mixed[...] + inv_rms * (
        scaled - unit_in * jnp.mean(scaled * unit_in, axis=-1, keepdims=True)
    )
    small.along_dp()
    sum_wo = ZSum(p, ring_wo, r.zo_bufs, r.zo_sems)
    sum_wo.start()
    sum_wq = ZSum(p, ring_wq, r.zq_bufs, r.zq_sems)
    sum_wq.start()
    sum_wkv = ZSum(p, ring_wkv, r.zkv_bufs, r.zkv_sems)
    sum_wkv.start()
    arrive_all(gu_copies)
    for n, out in enumerate((r.o_gate, r.o_up)):
        for d in range(8):
            r.stage[8 * d : 8 * d + 8, :] = r.gu_got[d, :, 640 * n : 640 * n + 640]
        wide = r.stage[...]
        high = wide.astype(BF16)
        low = (wide - high.astype(F32)).astype(BF16)
        packed = dot_nt(high, columns_of(r.big)) + dot_nt(low, columns_of(r.big))
        for d in range(8):
            out[:, 608 * d : 608 * d + 608] = packed[8 * d : 8 * d + 7, :608]
    arrive_all(down_copies2)
    final = r.down_mid[p.x] + r.down_x[0] + r.down_x[1] + r.down_x[2]
    r.o_down[...] = final[:38]
    r.o_output[...] = sum_wo.result()[:7]
    r.o_query[...] = sum_wq.result()[:7]
    part = sum_wkv.result()
    r.o_key[...] = part[:7, :128]
    r.o_value[...] = part[:7, 128:]
    total = small.result()
    r.o_small[...] = total
    me = p.dp * 16 + p.ctx
    flat = lax.broadcasted_iota(jnp.int32, (7, 128), 0) * 128 + lax.broadcasted_iota(jnp.int32, (7, 128), 1)
    lane = lax.broadcasted_iota(jnp.int32, (1, 128), 1)

    def pick(block, where):
        return jnp.sum(jnp.sum(jnp.where(where, block, 0.0), axis=0, keepdims=True), axis=1, keepdims=True)

    r.o_mine[...] = jnp.zeros_like(r.o_mine)
    for n in range(3):
        row = jnp.zeros((1, 128), F32)
        for i in range(7):
            row = row + jnp.where(lane == i, pick(total[7 * n : 7 * n + 7], flat == me * 7 + i), 0.0)
        r.o_mine[n : n + 1, :] = row
    r.o_mine[3:4, :] = jnp.broadcast_to(pick(total[22:23], lane == me), (1, 128))
    red_out.sent()
    for ring in (*rings, red_normed, red_out, ring_gu, ring_kv, ring_wo, ring_wq, ring_wkv, small, sum_wo, sum_wq, sum_wkv):
        ring.finish()
    sent_all([mate_wo, mate_wq, mate_wkv] + down_copies + down_copies2 + gu_copies)


LAYER_OUTS = {
    "layer_out": shape((128, D), BF16),
    "grad_in": shape((128, D), F32),
    "o_query": shape((7, D), F32),
    "o_key": shape((7, 128), F32),
    "o_value": shape((7, 128), F32),
    "o_output": shape((7, D), F32),
    "o_gate": shape((7, 4864), F32),
    "o_up": shape((7, 4864), F32),
    "o_down": shape((38, D), F32),
    "o_small": shape((24, 128), F32),
    "o_mine": shape((8, 128), F32),
}
BACK_SCRATCH = {
    "big": VM((15, 1024, 128), BF16),
    "part_normed": VM((4, 2, 128, DPAD), BF16),
    "normed_bufs": ReduceDp.scratch(128, DPAD), "normed_sems": ReduceDp.SEMS,
    "out_bufs": ReduceDp.scratch(128, D), "out_sems": ReduceDp.SEMS,
    "g_gu": VM((2, 4, 4, 32, 1280), BF16),
    "gu_bufs": ReduceCtx.scratch(32, 1280), "gu_red_sems": ReduceCtx.SEMS,
    "g_down": VM((640, D), BF16),
    "down_y": VM((3, 160, D), BF16), "down_mid": VM((4, 40, D), F32), "down_x": VM((3, 40, D), F32),
    "grad_mixed": VM((128, D), F32),
    "held": VM((128, D), F32),
    "low_a": VM((128, D), BF16),
    "low_b": VM((128, D), BF16),
    "low_kv": VM((128, 256), BF16),
    "grad_heads": VM((14, 128, 128), BF16),
    "grad_query": VM((14, 64, 128), F32),
    "kv_bufs": ReduceCtx.scratch(64, 256), "kv_red_sems": ReduceCtx.SEMS,
    "g_wo": VM((2, 4, 4, 2, 16, D), BF16), "m_wo": VM((4, 4, 2, 16, D), BF16),
    "g_wq": VM((2, 4, 4, 2, 16, D), BF16), "m_wq": VM((4, 4, 2, 16, D), BF16),
    "g_wkv": VM((2, 4, 4, 2, 16, 256), BF16), "m_wkv": VM((4, 4, 2, 16, 256), BF16),
    "wo_bufs": ReduceCtx.scratch(16, D), "wo_sems": ReduceCtx.SEMS,
    "wq_bufs": ReduceCtx.scratch(16, D), "wq_sems": ReduceCtx.SEMS,
    "wkv_bufs": ReduceCtx.scratch(16, 256), "wkv_sems": ReduceCtx.SEMS,
    "zo_bufs": ZSum.scratch(D), "zo_sems": ZSum.SEMS,
    "zq_bufs": ZSum.scratch(D), "zq_sems": ZSum.SEMS,
    "zkv_bufs": ZSum.scratch(256), "zkv_sems": ZSum.SEMS,
    "small_grads": VM((24, 128), F32),
    "small_bufs2": SmallSum.SCRATCH, "small_sems2": SmallSum.SEMS,
    "gu_out": VM((4, 2, 8, 1280), F32), "gu_got": VM((8, 8, 1280), F32),
    "s_mate": DMA((3,)), "r_mate": DMA((3,)), "s_gdown": DMA((2, 4)), "r_gdown": DMA((2, 4)),
    "s_ggu": DMA((8,)), "r_ggu": DMA((8,)),
}


WHOLE = ("layer_out", "grad_in", "o_query", "o_key", "o_value", "o_output", "o_gate", "o_up", "o_down")
VECTORS = {"norm_attn": 7, "b_query": 7, "norm_mlp": 7, "b_value": 1, "b_key": 128}


def finish(done):
    def kernel(*refs):
        count = len(WHOLE)
        sources, (mine, sums) = refs[:count], refs[count : count + 2]
        targets, vectors = refs[count + 2 : 2 * count + 2], refs[2 * count + 2 :]
        for source, target in zip(sources, targets):
            target[...] = source[...]
        for n in range(3):
            vectors[n][...] = mine[n, :7]
        vectors[3][...] = mine[3, :1]
        vectors[4][...] = sums[21]

    fast = pl.BlockSpec(memory_space=VM)
    results = pl.pallas_call(
        kernel,
        out_shape=tuple(LAYER_OUTS[key] for key in WHOLE) + tuple(shape((n,), F32) for n in VECTORS.values()),
        in_specs=[fast] * (len(WHOLE) + 2),
        out_specs=tuple([fast] * (len(WHOLE) + len(VECTORS))),
        name="finish",
        compiler_params=pltpu.CompilerParams(vmem_limit_bytes=63 << 20),
    )(*(done[key] for key in WHOLE), done["o_mine"], done["o_small"])
    return dict(zip(WHOLE + tuple(VECTORS), results))


def layer(r):
    p = Place()
    back(r, p, front(r, p))


def body(
    hidden_in, positions, norm_attn, w_query, b_query, w_key, b_key, value_weight, value_bias, w_output,
    norm_mlp, w_gate, w_up, w_down, cotangent,
):
    rows = MB * 64
    inputs = {
        "hidden": hidden_in.reshape(rows, D),
        "cot": cotangent.reshape(rows, D),
        "positions": positions,
        "norm_attn": norm_attn, "b_query": b_query, "norm_mlp": norm_mlp, "b_key": b_key, "value_bias": value_bias,
        "w_query": w_query, "w_key": w_key, "w_value": value_weight, "w_output": w_output,
        "w_gate": w_gate, "w_up": w_up, "w_down_own": w_down,
    }
    done = call(layer, inputs, LAYER_OUTS, {**FRONT_SCRATCH, **BACK_SCRATCH}, 0, "layer")
    done = finish(done)
    return (
        done["layer_out"].reshape(MB, 1, 64, D),
        done["grad_in"].reshape(MB, 1, 64, D),
        done["norm_attn"],
        done["o_query"],
        done["b_query"],
        done["o_key"],
        done["b_key"],
        done["o_value"],
        done["b_value"],
        done["o_output"],
        done["norm_mlp"],
        done["o_gate"],
        done["o_up"],
        done["o_down"],
    )


def solution(mesh):
    rows = P(("dp", "ctx"), None)
    vector = P(("dp", "ctx"))
    tokens = P(None, "dp", "ctx", None)
    in_specs = (
        tokens, P(None, "dp", "ctx"), vector, rows, vector, rows, vector, rows, vector, rows, vector,
        rows, rows, rows, tokens,
    )
    out_specs = (
        tokens, tokens, vector, rows, vector, rows, P(), rows, vector, rows, vector, rows, rows, rows,
    )
    return jax.shard_map(body, mesh=mesh, in_specs=in_specs, out_specs=out_specs, check_vma=False)
```
